512 devices in a mesh: tm: 64 (over x, y, z_lo), chan: 8 (over z_hi, core).
Axes of the slice: x: 4, y: 4, z: 16 (z_hi: 4, z_lo: 4; z = z_hi * 4 + z_lo), core: 2. Of those that a mesh axis runs over, the one named last changes fastest.
Arguments:
- samples: bfloat16 [2, 2, 512, 196608], P(None, None, None, ('tm', 'chan')), may hold values from -96 to 96
- scales: float32 [512, 768], P('chan', 'tm'), may hold values from 0.01 to 0.06
- flags: int32 [512, 768], P('chan', 'tm'), may hold values 0 or 1
- sweep: float32 [512], P('chan'), may hold values from 128 to 1024
- phase_bin: int32 [196608], P('tm'), may hold values from 0 to 1023, as said below
Outputs:
- profile: float32 [1024, 4, 512], P('tm', None, 'chan')
The draws below stay inside these ranges and needn't reach their ends.
Inputs may be any that keep to these rules, and one draw needn't show every extreme that they name: `flags`: A nonzero flag marks an excised block. phase_bin[t] = floor((1024 t + 1024 * o) / q) mod 1024, with whole numbers q in [2048, 8192) and o in [0, 2048) fixed by the draw, t counting samples from the start of the window.
All inputs are finite; a program needn't handle non-finite values.
Results may differ from the reference program's by a relative error of at most 0.0015.
Values may be sent and summed in bfloat16 or wider, within the bound.
No kernel may reach another device: no remote copies, remote signals or barrier semaphores. Data moves between devices by JAX's collectives and lax.ppermute only.
A program may use at most 64 MiB of HBM per device.

```python
import math
import jax
import jax.numpy as jnp
from jax import lax

NCHAN = 512
NFFT = 4096
OVER = 1024
BLK = 256
NBIN = 1024
TIME = 196608
NBLK = 768


def draw_phase_bin(key, part):
    key = jax.random.fold_in(key, 7)
    period_key, offset_key = jax.random.split(key)
    period = jax.random.randint(period_key, (), NFFT // 2, 2 * NFFT)
    offset = jax.random.randint(offset_key, (), 0, NFFT // 2)
    times = jnp.arange(TIME, dtype=jnp.int32)
    return (times * NBIN + offset * NBIN) // period % NBIN


def set_ends(values, stream_key, least, largest):
    longest = values.shape.index(max(values.shape))
    spots = []
    for shift in (0, 1):
        where = [jax.random.randint(jax.random.fold_in(stream_key, axis), (), 0, length) for axis, length in enumerate(values.shape)]
        where[longest] = (where[longest] + shift) % values.shape[longest]
        spots.append(tuple(where))
    return values.at[spots[0]].set(least).at[spots[1]].set(largest)


def steps_of(rng, dims, shards, smallest, high):
    level = 1.0
    for dim, blocks in shards:
        heights = jax.random.uniform(jax.random.fold_in(jax.random.fold_in(rng, 6), dim), (blocks,), jnp.float32, smallest / len(shards), high / len(shards))
        level = level * jnp.repeat(jnp.exp(heights), dims[dim] // blocks).reshape((-1,) + (1,) * (len(dims) - 1 - dim))
    return level


def gaussian(stream_key, extent, scale, limit, cuts=(), held_as=jnp.bfloat16):
    loudness = steps_of(stream_key, extent, cuts, -0.22, 0.18) if cuts else 1.0
    entries = jax.random.normal(stream_key, extent, jnp.float32) * scale * loudness
    return jnp.minimum(jnp.maximum(entries, -limit), limit).astype(held_as)


def setup_inputs(seed: int = 0) -> dict:
    key_list = jax.random.split(jax.random.key(seed), 6)
    return {
        "samples": gaussian(key_list[0], (2, 2, NCHAN, TIME), 16.0, 96.0, ((3, 512),)),
        "scales": jnp.clip(jnp.exp(math.log(0.06) - 1.7917595 * jax.random.uniform(key_list[1], (NCHAN, NBLK), jnp.float32) ** steps_of(key_list[1], (NCHAN, NBLK), ((0, 8), (1, 64)), -0.2, 0.2)), 0.01, 0.06),
        "flags": set_ends((jax.random.randint(key_list[2], (NCHAN, NBLK), 0, 8) < 1).astype(jnp.int32), jax.random.fold_in(key_list[2], 1), 0, 1),
        "sweep": jnp.clip(jnp.exp(math.log(1024.0) - 2.0794415 * jax.random.uniform(key_list[3], (NCHAN,), jnp.float32) ** steps_of(key_list[3], (NCHAN,), ((0, 8),), -0.2, 0.2)), 128.0, 1024.0),
        "phase_bin": draw_phase_bin(jax.random.fold_in(key_list[5], 71), 0),
    }


def reference(samples, scales, flags, sweep, phase_bin):
    total = samples.shape[-1]
    kept_len = NFFT - OVER
    frame_count = total // kept_len
    group = math.gcd(NCHAN, 32)
    weight = scales * (1 - flags).astype(jnp.float32)
    freq = jnp.arange(NFFT, dtype=jnp.int32)
    offset = jnp.where(freq < NFFT // 2, freq, freq - NFFT).astype(jnp.float32) / NFFT
    curve = offset * offset + offset
    starts = (jnp.arange(frame_count, dtype=jnp.int32) * kept_len)[:, None] + jnp.arange(NFFT, dtype=jnp.int32)[None, :]
    fold_scale = NBIN / total

    def one_group(index):
        first_chan = (index * group).astype(jnp.int32)
        raw = lax.dynamic_slice_in_dim(samples, first_chan, group, 2).astype(jnp.float32)
        gain = lax.dynamic_slice_in_dim(weight, first_chan, group, 0)
        gain = jnp.repeat(gain, BLK, axis=1)
        baseband = raw * gain[None, None]
        padded = jnp.pad(baseband, ((0, 0), (0, 0), (0, 0), (OVER, 0)))
        frames = padded[..., starts]
        spectrum = jnp.fft.fft(frames[:, 0] + 1j * frames[:, 1], axis=-1)
        rate = lax.dynamic_slice_in_dim(sweep, first_chan, group, 0)
        phase = jnp.pi * rate[:, None] * curve[None, :]
        chirp = jnp.cos(phase) + 1j * jnp.sin(phase)
        clean = jnp.fft.ifft(spectrum * chirp[None, :, None, :], axis=-1)[..., OVER:]
        clean = clean.reshape(2, group, total)
        horiz_re = jnp.real(clean[0])
        horiz_im = jnp.imag(clean[0])
        vert_re = jnp.real(clean[1])
        vert_im = jnp.imag(clean[1])
        power_h = horiz_re * horiz_re + horiz_im * horiz_im
        power_v = vert_re * vert_re + vert_im * vert_im
        cross_re = horiz_re * vert_re + horiz_im * vert_im
        cross_im = horiz_im * vert_re - horiz_re * vert_im
        stokes = jnp.stack([power_h + power_v, power_h - power_v, 2.0 * cross_re, 2.0 * cross_im], 0).astype(jnp.bfloat16)
        stokes_rows = stokes.astype(jnp.float32).reshape(4 * group, total).T
        summed = jax.ops.segment_sum(stokes_rows, phase_bin, num_segments=NBIN)
        return (summed * fold_scale).reshape(NBIN, 4, group)

    pieces = lax.map(one_group, jnp.arange(NCHAN // group, dtype=jnp.int32))
    return jnp.transpose(pieces, (1, 2, 0, 3)).reshape(NBIN, 4, NCHAN)
```

```python
import functools
import math

import jax
import jax.numpy as jnp
import numpy as np
from jax import lax
from jax.experimental import pallas as pl
from jax.experimental.pallas import tpu as pltpu
from jax.sharding import Mesh, PartitionSpec as P

NFFT = 4096
OVER = 1024
BLK = 256
NBIN = 1024
LANES = 128
ROWS = NFFT // LANES
RIM = OVER // LANES
KEPT = ROWS - RIM
RUNS = 4
MEMBERS = 8
PIECE = 384
SLAB = MEMBERS * PIECE
GROUP = 16
BLOCKS = SLAB // BLK
WINDOW = 144
ACC_ROWS = NBIN + WINDOW
HALF_ROOT = math.sqrt(0.5)


def lane_tables():
    angle = 2.0 * np.pi / LANES * (np.arange(LANES)[:, None] * np.arange(LANES)[None, :] % LANES)
    cos, sin = np.cos(angle), np.sin(angle)
    table = np.block([[cos, -sin], [sin, cos]]).astype(np.float32)
    high = table.astype(jnp.bfloat16)
    low = (table - high.astype(np.float32)).astype(jnp.bfloat16)
    return high, low


def twist_tables():
    angle = -2.0 * np.pi / NFFT * (np.arange(ROWS)[:, None] * np.arange(LANES)[None, :])
    return np.cos(angle).astype(np.float32), np.sin(angle).astype(np.float32)


def plus(a, b):
    return (a[0] + b[0], a[1] + b[1])


def minus(a, b):
    return (a[0] - b[0], a[1] - b[1])


def quarter(a, sign):
    return (a[1], -a[0]) if sign < 0 else (-a[1], a[0])


def dft4(x, sign):
    t0, t1 = plus(x[0], x[2]), minus(x[0], x[2])
    t2, t3 = plus(x[1], x[3]), quarter(minus(x[1], x[3]), sign)
    return [plus(t0, t2), plus(t1, t3), minus(t0, t2), minus(t1, t3)]


def dft8(x, sign):
    even = dft4(x[0::2], sign)
    odd = dft4(x[1::2], sign)
    re, im = odd[1]
    if sign < 0:
        odd[1] = ((re + im) * HALF_ROOT, (im - re) * HALF_ROOT)
    else:
        odd[1] = ((re - im) * HALF_ROOT, (im + re) * HALF_ROOT)
    odd[2] = quarter(odd[2], sign)
    re, im = odd[3]
    if sign < 0:
        odd[3] = ((im - re) * HALF_ROOT, (re + im) * -HALF_ROOT)
    else:
        odd[3] = ((re + im) * -HALF_ROOT, (re - im) * HALF_ROOT)
    return [plus(e, o) for e, o in zip(even, odd)] + [minus(e, o) for e, o in zip(even, odd)]


def turned(a, step, sign):
    step %= 32
    if step == 0:
        return a
    if step == 8:
        return quarter(a, sign)
    re, im = a
    if step == 4:
        if sign < 0:
            return ((re + im) * HALF_ROOT, (im - re) * HALF_ROOT)
        return ((re - im) * HALF_ROOT, (im + re) * HALF_ROOT)
    cos = math.cos(2.0 * math.pi * step / 32)
    sin = sign * math.sin(2.0 * math.pi * step / 32)
    return (re * cos - im * sin, re * sin + im * cos)


def split(values):
    high = values.astype(jnp.bfloat16)
    return high, (values - high.astype(jnp.float32)).astype(jnp.bfloat16)


def lane_dft(high, low, table_high, table_low):
    dot = functools.partial(jnp.dot, preferred_element_type=jnp.float32)
    return dot(high, table_high) + (dot(low, table_high) + dot(high, table_low))


def frame_profile(
    row_of, weight_of, base_of, marks_of, chirp_ref, twist_ref, table_ref, mid, y_ref, v_ref, stokes_ref, acc
):
    for pol in range(2):
        for b in range(4):
            rows = []
            for a in range(8):
                row = 4 * a + b
                gain = weight_of(row // 2)
                rows.append(tuple(row_of(row, pol, part).astype(jnp.float32) * gain for part in range(2)))
            for ka, value in enumerate(dft8(rows, -1)):
                value = turned(value, b * ka, -1)
                mid[pol, 0, b, ka] = value[0]
                mid[pol, 1, b, ka] = value[1]
        for ka in range(8):
            values = dft4([(mid[pol, 0, b, ka], mid[pol, 1, b, ka]) for b in range(4)], -1)
            for kb in range(4):
                k = ka + 8 * kb
                re, im = values[kb]
                if k:
                    cos, sin = twist_ref[0, k : k + 1], twist_ref[1, k : k + 1]
                    re, im = re * cos - im * sin, re * sin + im * cos
                for part, value in enumerate((re, im)):
                    high, low = split(value)
                    where = (pl.ds(GROUP * k, GROUP), pl.ds(LANES * part, LANES))
                    y_ref[0, *where] = high
                    y_ref[1, *where] = low
        for m in range(4):
            rows = pl.ds(8 * GROUP * m, 8 * GROUP)
            spectrum = lane_dft(y_ref[0, rows], y_ref[1, rows], table_ref[0], table_ref[1])
            re, im = spectrum[:, :LANES], spectrum[:, LANES:]
            cos, sin = chirp_ref[0, rows], chirp_ref[1, rows]
            swapped = jnp.concatenate([re * sin + im * cos, re * cos - im * sin], axis=1)
            back = lane_dft(*split(swapped), table_ref[0], table_ref[1])
            im, re = (back[:, part].reshape(8, GROUP, LANES) for part in (slice(0, LANES), slice(LANES, None)))
            cos = twist_ref[0, 8 * m : 8 * m + 8][:, None, :]
            sin = twist_ref[1, 8 * m : 8 * m + 8][:, None, :]
            v_ref[0, 8 * m : 8 * m + 8] = re * cos + im * sin
            v_ref[1, 8 * m : 8 * m + 8] = im * cos - re * sin
        for b in range(4):
            values = dft8([(v_ref[0, 4 * a + b], v_ref[1, 4 * a + b]) for a in range(8)], 1)
            for na, value in enumerate(values):
                value = turned(value, b * na, 1)
                mid[pol, 0, b, na] = value[0]
                mid[pol, 1, b, na] = value[1]
    for na in range(8):
        x, y = (
            dft4([(mid[pol, 0, b, na], mid[pol, 1, b, na]) for b in range(4)], 1) for pol in range(2)
        )
        for nb in range(1, 4):
            (xr, xi), (yr, yi) = x[nb], y[nb]
            power_x = xr * xr + xi * xi
            power_y = yr * yr + yi * yi
            cross_re = xr * yr + xi * yi
            cross_im = xi * yr - xr * yi
            row = na + 8 * (nb - 1)
            lanes = pl.ds(LANES * (row % 2), LANES)
            for s, value in enumerate((power_x + power_y, power_x - power_y, 2.0 * cross_re, 2.0 * cross_im)):
                stokes_ref[row // 2, pl.ds(GROUP * s, GROUP), lanes] = value.astype(jnp.bfloat16)
    bins = lax.broadcasted_iota(jnp.int32, (WINDOW, BLK), 0)
    for m in range(BLOCKS):
        onehot = jnp.where(bins == marks_of(m), 1.0, 0.0).astype(jnp.bfloat16)
        part = lax.dot_general(
            onehot, stokes_ref[m], (((1,), (1,)), ((), ())), preferred_element_type=jnp.float32
        )
        place = pl.ds(pl.multiple_of(base_of(m), 8), WINDOW)
        acc[place] += part


def own_row(buf_ref, slab, row, pol, part):
    return buf_ref[row // 3, slab, pol, part, :, pl.ds(LANES * (row % 3), LANES)]


def later_kernel(
    base_ref, buf_ref, weight_ref, marks_ref, chirp_ref, twist_ref, table_ref, acc_ref, mid, y_ref, v_ref, stokes_ref
):
    acc_ref[...] = jnp.zeros_like(acc_ref)

    def step(frame, carry):
        def row_of(row, pol, part):
            if row < RIM:
                return own_row(buf_ref, frame - 1, row + KEPT - RIM, pol, part)
            return own_row(buf_ref, frame, row - RIM, pol, part)

        frame_profile(
            row_of,
            lambda block: weight_ref[BLOCKS * frame + block],
            lambda m: base_ref[BLOCKS * frame + m],
            lambda m: marks_ref[BLOCKS * frame + m],
            chirp_ref,
            twist_ref,
            table_ref,
            mid,
            y_ref,
            v_ref,
            stokes_ref,
            acc_ref,
        )
        return carry

    lax.fori_loop(1, RUNS, step, 0)


def first_kernel(
    base_ref, buf_ref, tail_ref, weight_ref, marks_ref, chirp_ref, twist_ref, table_ref, given_ref, out_ref,
    acc, mid, y_ref, v_ref, stokes_ref,
):
    acc[...] = given_ref[...]

    def row_of(row, pol, part):
        if row < RIM:
            return own_row(tail_ref, 0, row + 1, pol, part)
        return own_row(buf_ref, 0, row - RIM, pol, part)

    frame_profile(
        row_of,
        lambda block: weight_ref[block],
        lambda m: base_ref[m],
        lambda m: marks_ref[m],
        chirp_ref,
        twist_ref,
        table_ref,
        mid,
        y_ref,
        v_ref,
        stokes_ref,
        acc,
    )
    acc[:WINDOW] += acc[NBIN:]
    for share in range(NBIN // 16):
        out_ref[share] = jnp.concatenate([acc[16 * share : 16 * share + 8], acc[16 * share + 8 : 16 * share + 16]], axis=1)


def scratch():
    return [
        pltpu.VMEM((2, 2, 4, 8, GROUP, LANES), jnp.float32),
        pltpu.VMEM((2, ROWS * GROUP, 2 * LANES), jnp.bfloat16),
        pltpu.VMEM((2, ROWS, GROUP, LANES), jnp.float32),
        pltpu.VMEM((BLOCKS, 4 * GROUP, BLK), jnp.bfloat16),
    ]


def whole():
    return pl.BlockSpec(memory_space=pltpu.VMEM)


def fold_frames(buf, tail_of, weight, base, marks, chirp):
    twist = jnp.asarray(np.stack(twist_tables()))
    table = jnp.asarray(np.stack(lane_tables()))
    tail = tail_of(buf)
    params = pltpu.CompilerParams(vmem_limit_bytes=28 * 1024 * 1024)
    flops = 2 * 2 * 2 * 3 * ROWS * GROUP * 256 * 256
    later = pl.pallas_call(
        later_kernel,
        out_shape=jax.ShapeDtypeStruct((ACC_ROWS, 4 * GROUP), jnp.float32),
        in_specs=[pl.BlockSpec(memory_space=pltpu.SMEM)] + [whole()] * 6,
        out_specs=whole(),
        scratch_shapes=scratch(),
        compiler_params=params,
        cost_estimate=pl.CostEstimate(flops=3 * flops, bytes_accessed=30_000_000, transcendentals=0),
        name="later_frames",
    )(base, buf, weight, marks, chirp, twist, table)
    block = (MEMBERS, 1) + buf.shape[2:]
    return pl.pallas_call(
        first_kernel,
        out_shape=jax.ShapeDtypeStruct((NBIN // 16, 8, LANES), jnp.float32),
        grid=(1,),
        in_specs=[pl.BlockSpec(memory_space=pltpu.SMEM), pl.BlockSpec(block, lambda i: (0,) * 6)] + [whole()] * 7,
        out_specs=whole(),
        scratch_shapes=[pltpu.VMEM((ACC_ROWS, 4 * GROUP), jnp.float32)] + scratch(),
        compiler_params=params,
        cost_estimate=pl.CostEstimate(flops=flops, bytes_accessed=10_000_000, transcendentals=0),
        name="first_frame",
    )(base, buf, tail, weight, marks, chirp, twist, table, later)


def gathered(block, axis):
    size = lax.axis_size(axis)
    parts = [block] + [
        lax.ppermute(block, axis, [(i, (i + turn) % size) for i in range(size)]) for turn in range(1, size)
    ]
    me = lax.axis_index(axis)
    pile = jnp.stack(parts)
    return jnp.concatenate(
        [lax.dynamic_slice_in_dim(pile, (me - i + size) % size, 1, 0) for i in range(size)]
    )


def from_before(block):
    size = lax.axis_size("xy")
    return lax.ppermute(block, "xy", [(i, i + 1) for i in range(size - 1)])


def chirp_table(sweep):
    k = jnp.arange(ROWS, dtype=jnp.int32)[:, None] + ROWS * jnp.arange(LANES, dtype=jnp.int32)[None, :]
    u = jnp.where(k < NFFT // 2, k, k - NFFT).astype(jnp.float32) / NFFT
    phase = (jnp.pi * sweep)[None, :, None] * (u * u + u)[:, None, :]
    table = jnp.stack([jnp.cos(phase), jnp.sin(phase)]) * (1.0 / NFFT)
    return table.reshape(2, ROWS * GROUP, LANES)


def on_device(samples, scales, flags, sweep, phase_bin):
    parts = samples.reshape(2, 2, MEMBERS * RUNS, GROUP, PIECE).transpose(2, 0, 1, 3, 4)
    buf = lax.all_to_all(parts, ("chan", "zl"), split_axis=0, concat_axis=0, tiled=True)
    buf = buf.reshape(MEMBERS, RUNS, 2, 2, GROUP, PIECE)

    me = lax.axis_index("zl")
    weight = scales * (1 - flags).astype(jnp.float32)
    message = jnp.concatenate([weight.reshape(-1), phase_bin.astype(jnp.float32)])
    letters = gathered(message, "zl")
    count = scales.shape[0] * BLOCKS
    weights = letters[:, :count].reshape(RUNS, scales.shape[0], BLOCKS)
    weights = lax.dynamic_slice_in_dim(weights, me * GROUP, GROUP, 1)
    weights = weights.transpose(0, 2, 1).reshape(RUNS * BLOCKS, GROUP)
    weights = jnp.concatenate([from_before(weights[-(OVER // BLK) :]), weights])
    weights = jnp.broadcast_to(weights[:, :, None], weights.shape + (LANES,))
    bins = letters[:, count:].astype(jnp.int32).reshape(RUNS * BLOCKS, 1, BLK)
    base = bins[:, 0, 0] // 8 * 8
    marks = (bins - base[:, None, None]) % NBIN
    chirp = chirp_table(lax.dynamic_slice_in_dim(sweep, me * GROUP, GROUP, 0))

    partial = fold_frames(buf, lambda b: from_before(b[5:, RUNS - 1 :]), weights, base, marks, chirp)
    shares = lax.all_to_all(partial, ("xy", "zl"), split_axis=0, concat_axis=0, tiled=True)
    total = shares.reshape(-1, RUNS, 8, 2, 4, GROUP).sum(0) * (NBIN / (SLAB * RUNS * lax.axis_size("xy")))
    return total.transpose(2, 1, 3, 0, 4).reshape(16, 4, RUNS * GROUP)


def solution(mesh):
    inner = Mesh(mesh.devices.reshape(-1, RUNS, MEMBERS), ("xy", "zl", "chan"))
    time = ("xy", "zl")
    placed = (
        P(None, None, None, ("xy", "zl", "chan")),
        P("chan", time),
        P("chan", time),
        P("chan"),
        P(time),
    )
    return jax.shard_map(
        on_device, mesh=inner, in_specs=placed, out_specs=P(time, None, "chan"), check_vma=False
    )
```

```python
import functools
import math

import jax
import jax.numpy as jnp
import numpy as np
from jax import lax
from jax.experimental import pallas as pl
from jax.experimental.pallas import tpu as pltpu
from jax.sharding import Mesh, PartitionSpec as P

NFFT = 4096
OVER = 1024
BLK = 256
NBIN = 1024
LANES = 128
ROWS = NFFT // LANES
RIM = OVER // LANES
KEPT = ROWS - RIM
RUNS = 4
MEMBERS = 8
PIECE = 384
SLAB = MEMBERS * PIECE
GROUP = 16
BLOCKS = SLAB // BLK
WINDOW = 144
ACC_ROWS = NBIN + WINDOW
HALF_ROOT = math.sqrt(0.5)


def lane_tables():
    angle = 2.0 * np.pi / LANES * (np.arange(LANES)[:, None] * np.arange(LANES)[None, :] % LANES)
    cos, sin = np.cos(angle), np.sin(angle)
    table = np.block([[cos, -sin], [sin, cos]]).astype(np.float32)
    high = table.astype(jnp.bfloat16)
    low = (table - high.astype(np.float32)).astype(jnp.bfloat16)
    return high, low


def twist_tables():
    angle = -2.0 * np.pi / NFFT * (np.arange(ROWS)[:, None] * np.arange(LANES)[None, :])
    return np.cos(angle).astype(np.float32), np.sin(angle).astype(np.float32)


def plus(a, b):
    return (a[0] + b[0], a[1] + b[1])


def minus(a, b):
    return (a[0] - b[0], a[1] - b[1])


def quarter(a, sign):
    return (a[1], -a[0]) if sign < 0 else (-a[1], a[0])


def dft4(x, sign):
    t0, t1 = plus(x[0], x[2]), minus(x[0], x[2])
    t2, t3 = plus(x[1], x[3]), quarter(minus(x[1], x[3]), sign)
    return [plus(t0, t2), plus(t1, t3), minus(t0, t2), minus(t1, t3)]


def dft8(x, sign):
    even = dft4(x[0::2], sign)
    odd = dft4(x[1::2], sign)
    re, im = odd[1]
    if sign < 0:
        odd[1] = ((re + im) * HALF_ROOT, (im - re) * HALF_ROOT)
    else:
        odd[1] = ((re - im) * HALF_ROOT, (im + re) * HALF_ROOT)
    odd[2] = quarter(odd[2], sign)
    re, im = odd[3]
    if sign < 0:
        odd[3] = ((im - re) * HALF_ROOT, (re + im) * -HALF_ROOT)
    else:
        odd[3] = ((re + im) * -HALF_ROOT, (re - im) * HALF_ROOT)
    return [plus(e, o) for e, o in zip(even, odd)] + [minus(e, o) for e, o in zip(even, odd)]


def turned(a, step, sign):
    step %= 32
    if step == 0:
        return a
    if step == 8:
        return quarter(a, sign)
    re, im = a
    if step == 4:
        if sign < 0:
            return ((re + im) * HALF_ROOT, (im - re) * HALF_ROOT)
        return ((re - im) * HALF_ROOT, (im + re) * HALF_ROOT)
    cos = math.cos(2.0 * math.pi * step / 32)
    sin = sign * math.sin(2.0 * math.pi * step / 32)
    return (re * cos - im * sin, re * sin + im * cos)


def split(values):
    high = values.astype(jnp.bfloat16)
    return high, (values - high.astype(jnp.float32)).astype(jnp.bfloat16)


def lane_dft(high, low, table_high, table_low):
    dot = functools.partial(jnp.dot, preferred_element_type=jnp.float32)
    return dot(high, table_high) + (dot(low, table_high) + dot(high, table_low))


def frame_profile(
    row_of, weight_of, base_of, marks_of, chirp_ref, twist_ref, table_ref, mid, y_refs, v_refs, stokes_ref, acc
):
    for pol in range(2):
        y_ref, v_ref = y_refs.at[pol], v_refs.at[pol]
        for b in range(4):
            rows = []
            for a in range(8):
                row = 4 * a + b
                gain = weight_of(row // 2)
                rows.append(tuple(row_of(row, pol, part).astype(jnp.float32) * gain for part in range(2)))
            for ka, value in enumerate(dft8(rows, -1)):
                value = turned(value, b * ka, -1)
                mid[pol, 0, b, ka] = value[0]
                mid[pol, 1, b, ka] = value[1]
        for ka in range(8):
            values = dft4([(mid[pol, 0, b, ka], mid[pol, 1, b, ka]) for b in range(4)], -1)
            for kb in range(4):
                k = ka + 8 * kb
                re, im = values[kb]
                if k:
                    cos, sin = twist_ref[0, k : k + 1], twist_ref[1, k : k + 1]
                    re, im = re * cos - im * sin, re * sin + im * cos
                for part, value in enumerate((re, im)):
                    high, low = split(value)
                    where = (pl.ds(GROUP * k, GROUP), pl.ds(LANES * part, LANES))
                    y_ref[0, *where] = high
                    y_ref[1, *where] = low
        for m in range(2):
            rows = pl.ds(16 * GROUP * m, 16 * GROUP)
            spectrum = lane_dft(y_ref[0, rows], y_ref[1, rows], table_ref[0], table_ref[1])
            re, im = spectrum[:, :LANES], spectrum[:, LANES:]
            cos, sin = chirp_ref[0, rows], chirp_ref[1, rows]
            swapped = jnp.concatenate([re * sin + im * cos, re * cos - im * sin], axis=1)
            back = lane_dft(*split(swapped), table_ref[0], table_ref[1])
            im, re = (back[:, part].reshape(16, GROUP, LANES) for part in (slice(0, LANES), slice(LANES, None)))
            cos = twist_ref[0, 16 * m : 16 * m + 16][:, None, :]
            sin = twist_ref[1, 16 * m : 16 * m + 16][:, None, :]
            v_ref[0, 16 * m : 16 * m + 16] = re * cos + im * sin
            v_ref[1, 16 * m : 16 * m + 16] = im * cos - re * sin
        for b in range(4):
            values = dft8([(v_ref[0, 4 * a + b], v_ref[1, 4 * a + b]) for a in range(8)], 1)
            for na, value in enumerate(values):
                value = turned(value, b * na, 1)
                mid[pol, 0, b, na] = value[0]
                mid[pol, 1, b, na] = value[1]
    for na in range(8):
        x, y = (
            dft4([(mid[pol, 0, b, na], mid[pol, 1, b, na]) for b in range(4)], 1) for pol in range(2)
        )
        for nb in range(1, 4):
            (xr, xi), (yr, yi) = x[nb], y[nb]
            power_x = xr * xr + xi * xi
            power_y = yr * yr + yi * yi
            cross_re = xr * yr + xi * yi
            cross_im = xi * yr - xr * yi
            row = na + 8 * (nb - 1)
            lanes = pl.ds(LANES * (row % 2), LANES)
            for s, value in enumerate((power_x + power_y, power_x - power_y, 2.0 * cross_re, 2.0 * cross_im)):
                stokes_ref[row // 2, pl.ds(GROUP * s, GROUP), lanes] = value.astype(jnp.bfloat16)
    bins = lax.broadcasted_iota(jnp.int32, (WINDOW, BLK), 0)
    for m in range(BLOCKS):
        onehot = jnp.where(bins == marks_of(m), 1.0, 0.0).astype(jnp.bfloat16)
        part = lax.dot_general(
            onehot, stokes_ref[m], (((1,), (1,)), ((), ())), preferred_element_type=jnp.float32
        )
        place = pl.ds(pl.multiple_of(base_of(m), 8), WINDOW)
        acc[place] += part


def own_row(buf_ref, slab, row, pol, part):
    return buf_ref[row // 3, slab, pol, part, :, pl.ds(LANES * (row % 3), LANES)]


def turn_of(me, slab):
    return (me - slab + RUNS) % RUNS


def base_from(base_refs, turn, m):
    value = base_refs[RUNS - 1][m]
    for other in range(RUNS - 1):
        value = jnp.where(turn == other, base_refs[other][m], value)
    return value


def lay_gains(gains, weights_of):
    for block in range(ROWS // 2):
        gains[block] = jnp.broadcast_to(weights_of(block), (GROUP, LANES))


def marks_from(marks_ref, index, m):
    return jnp.concatenate([marks_ref[index, 2 * m : 2 * m + 1], marks_ref[index, 2 * m + 1 : 2 * m + 2]], axis=1)


def later_kernel(me_ref, *refs):
    base_refs, refs = refs[:RUNS], refs[RUNS:]
    letter_refs, refs = refs[:RUNS], refs[RUNS:]
    buf_ref, chirp_ref, twist_ref, table_ref, acc_ref, sorted_ref, gains, marks, *scratches = refs
    me = me_ref[0]
    for turn in range(RUNS):
        sorted_ref[(me - turn + RUNS) % RUNS] = letter_refs[turn][...]
    marks[...] = sorted_ref[:, GROUP:].astype(jnp.int32)
    acc_ref[...] = jnp.zeros_like(acc_ref)

    def step(frame, carry):
        def row_of(row, pol, part):
            if row < RIM:
                return own_row(buf_ref, frame - 1, row + KEPT - RIM, pol, part)
            return own_row(buf_ref, frame, row - RIM, pol, part)

        before, own = sorted_ref[frame - 1, :GROUP], sorted_ref[frame, :GROUP]

        def weights_of(block):
            if block < RIM // 2:
                return before[:, block + BLOCKS - RIM // 2 : block + BLOCKS - RIM // 2 + 1]
            return own[:, block - RIM // 2 : block - RIM // 2 + 1]

        lay_gains(gains, weights_of)
        turn = turn_of(me, frame)
        frame_profile(
            row_of,
            lambda block: gains[block],
            lambda m: base_from(base_refs, turn, m),
            lambda m: marks_from(marks, frame, m),
            chirp_ref,
            twist_ref,
            table_ref,
            *scratches,
            acc_ref,
        )
        return carry

    lax.fori_loop(1, RUNS, step, 0)


def first_kernel(me_ref, *refs):
    base_refs, refs = refs[:RUNS], refs[RUNS:]
    rim_refs, refs = refs[:RUNS], refs[RUNS:]
    buf_ref, tail_ref, sorted_ref, chirp_ref, twist_ref, table_ref, given_ref, out_ref, acc, gains, marks, *scratches = refs
    acc[...] = given_ref[...]
    before = (rim_refs[0][...] + rim_refs[1][...]) + (rim_refs[2][...] + rim_refs[3][...])
    own = sorted_ref[0, :GROUP]
    marks[0] = sorted_ref[0, GROUP:].astype(jnp.int32)

    def weights_of(block):
        if block < RIM // 2:
            return before[:, block + BLOCKS - RIM // 2 : block + BLOCKS - RIM // 2 + 1]
        return own[:, block - RIM // 2 : block - RIM // 2 + 1]

    def row_of(row, pol, part):
        if row < RIM:
            return own_row(tail_ref, 0, row + 1, pol, part)
        return own_row(buf_ref, 0, row - RIM, pol, part)

    lay_gains(gains, weights_of)
    turn = turn_of(me_ref[0], 0)
    frame_profile(
        row_of,
        lambda block: gains[block],
        lambda m: base_from(base_refs, turn, m),
        lambda m: marks_from(marks, 0, m),
        chirp_ref,
        twist_ref,
        table_ref,
        *scratches,
        acc,
    )
    acc[:WINDOW] += acc[NBIN:]
    for share in range(NBIN // 16):
        out_ref[share] = jnp.concatenate([acc[16 * share : 16 * share + 8], acc[16 * share + 8 : 16 * share + 16]], axis=1)


def scratch():
    return [
        pltpu.VMEM((2, 2, 4, 8, GROUP, LANES), jnp.float32),
        pltpu.VMEM((2, 2, ROWS * GROUP, 2 * LANES), jnp.bfloat16),
        pltpu.VMEM((2, 2, ROWS, GROUP, LANES), jnp.float32),
        pltpu.VMEM((BLOCKS, 4 * GROUP, BLK), jnp.bfloat16),
    ]


def whole():
    return pl.BlockSpec(memory_space=pltpu.VMEM)


def smem():
    return pl.BlockSpec(memory_space=pltpu.SMEM)


def fold_frames(buf, tail_of, me, bases, letters, rims, chirp):
    twist = jnp.asarray(np.stack(twist_tables()))
    table = jnp.asarray(np.stack(lane_tables()))
    tail = tail_of(buf)
    params = pltpu.CompilerParams(vmem_limit_bytes=28 * 1024 * 1024)
    flops = 2 * 2 * 2 * 3 * ROWS * GROUP * 256 * 256
    letter_rows = GROUP + KEPT
    later, ordered = pl.pallas_call(
        later_kernel,
        out_shape=[
            jax.ShapeDtypeStruct((ACC_ROWS, 4 * GROUP), jnp.float32),
            jax.ShapeDtypeStruct((RUNS, letter_rows, LANES), jnp.float32),
        ],
        in_specs=[smem()] * (1 + RUNS) + [whole()] * (RUNS + 4),
        out_specs=[whole()] * 2,
        scratch_shapes=[
            pltpu.VMEM((ROWS // 2, GROUP, LANES), jnp.float32),
            pltpu.VMEM((RUNS, KEPT, LANES), jnp.int32),
        ]
        + scratch(),
        compiler_params=params,
        cost_estimate=pl.CostEstimate(flops=3 * flops, bytes_accessed=30_000_000, transcendentals=0),
        name="later_frames",
    )(me, *bases, *letters, buf, chirp, twist, table)
    block = (MEMBERS, 1) + buf.shape[2:]
    return pl.pallas_call(
        first_kernel,
        out_shape=jax.ShapeDtypeStruct((NBIN // 16, 8, LANES), jnp.float32),
        grid=(1,),
        in_specs=[smem()] * (1 + RUNS)
        + [whole()] * RUNS
        + [pl.BlockSpec(block, lambda i: (0,) * 6)]
        + [whole()] * 6,
        out_specs=whole(),
        scratch_shapes=[
            pltpu.VMEM((ACC_ROWS, 4 * GROUP), jnp.float32),
            pltpu.VMEM((ROWS // 2, GROUP, LANES), jnp.float32),
            pltpu.VMEM((1, KEPT, LANES), jnp.int32),
        ]
        + scratch(),
        compiler_params=params,
        cost_estimate=pl.CostEstimate(flops=flops, bytes_accessed=10_000_000, transcendentals=0),
        name="first_frame",
    )(me, *bases, *rims, buf, tail, ordered, chirp, twist, table, later)


def last_kernel(scale, shares_ref, out_ref):
    for slab in range(RUNS):
        total = jnp.sum(shares_ref[:, slab], axis=0) * scale
        for half in range(2):
            for s in range(4):
                lanes = slice(64 * half + GROUP * s, 64 * half + GROUP * (s + 1))
                out_ref[8 * half : 8 * half + 8, s, GROUP * slab : GROUP * (slab + 1)] = total[:, lanes]


def turned_to(block_for, axis, turn):
    size = lax.axis_size(axis)
    there = (lax.axis_index(axis) + turn) % size
    if turn == 0:
        return block_for(there)
    return lax.ppermute(block_for(there), axis, [(i, (i + turn) % size) for i in range(size)])


def from_before(block):
    size = lax.axis_size("xy")
    return lax.ppermute(block, "xy", [(i, i + 1) for i in range(size - 1)])


def chirp_table(sweep):
    k = jnp.arange(ROWS, dtype=jnp.int32)[:, None] + ROWS * jnp.arange(LANES, dtype=jnp.int32)[None, :]
    u = jnp.where(k < NFFT // 2, k, k - NFFT).astype(jnp.float32) / NFFT
    phase = (jnp.pi * sweep)[None, :, None] * (u * u + u)[:, None, :]
    table = jnp.stack([jnp.cos(phase), jnp.sin(phase)]) * (1.0 / NFFT)
    return table.reshape(2, ROWS * GROUP, LANES)


def on_device(samples, scales, flags, sweep, phase_bin):
    parts = samples.reshape(2, 2, MEMBERS * RUNS, GROUP, PIECE).transpose(2, 0, 1, 3, 4)
    buf = lax.all_to_all(parts, ("chan", "zl"), split_axis=0, concat_axis=0, tiled=True)
    buf = buf.reshape(MEMBERS, RUNS, 2, 2, GROUP, PIECE)

    me = lax.axis_index("zl")
    weight = scales * (1 - flags).astype(jnp.float32)
    weight = jnp.pad(weight, ((0, 0), (0, LANES - BLOCKS)))
    bins = phase_bin.reshape(KEPT, LANES)
    base = bins[::2, 0] // 8 * 8
    marks = (bins - jnp.repeat(base, 2)[:, None]) % NBIN

    def weights_for(place):
        return lax.dynamic_slice_in_dim(weight, place * GROUP, GROUP, 0)

    def letter_for(place):
        return jnp.concatenate([weights_for(place), marks.astype(jnp.float32)])

    letters = [turned_to(letter_for, "zl", turn) for turn in range(RUNS)]
    bases = [turned_to(lambda place: base, "zl", turn) for turn in range(RUNS)]
    size = lax.axis_size("xy")
    rims = [
        lax.ppermute(
            weight[GROUP * place : GROUP * (place + 1)],
            ("xy", "zl"),
            [(i * RUNS + RUNS - 1, (i + 1) * RUNS + place) for i in range(size - 1)],
        )
        for place in range(RUNS)
    ]
    chirp = chirp_table(lax.dynamic_slice_in_dim(sweep, me * GROUP, GROUP, 0))

    partial = fold_frames(
        buf, lambda b: from_before(b[5:, RUNS - 1 :]), me.reshape(1), bases, letters, rims, chirp
    )
    shares = lax.all_to_all(partial, ("xy", "zl"), split_axis=0, concat_axis=0, tiled=True)
    return pl.pallas_call(
        functools.partial(last_kernel, NBIN / (SLAB * RUNS * size)),
        out_shape=jax.ShapeDtypeStruct((16, 4, RUNS * GROUP), jnp.float32),
        name="last_sum",
    )(shares.reshape(-1, RUNS, 8, LANES))


def solution(mesh):
    inner = Mesh(mesh.devices.reshape(-1, RUNS, MEMBERS), ("xy", "zl", "chan"))
    time = ("xy", "zl")
    placed = (
        P(None, None, None, ("xy", "zl", "chan")),
        P("chan", time),
        P("chan", time),
        P("chan"),
        P(time),
    )
    return jax.shard_map(
        on_device, mesh=inner, in_specs=placed, out_specs=P(time, None, "chan"), check_vma=False
    )
```

```python
import functools
import math

import jax
import jax.numpy as jnp
import numpy as np
from jax import lax
from jax.experimental import pallas as pl
from jax.experimental.pallas import tpu as pltpu
from jax.sharding import Mesh, PartitionSpec as P

NFFT = 4096
OVER = 1024
BLK = 256
NBIN = 1024
LANES = 128
ROWS = NFFT // LANES
RIM = OVER // LANES
KEPT = ROWS - RIM
RUNS = 4
MEMBERS = 8
PIECE = 384
SLAB = MEMBERS * PIECE
GROUP = 16
BLOCKS = SLAB // BLK
WINDOW = 144
ACC_ROWS = NBIN + WINDOW
SPAN = 16
BASE_ROW = GROUP + KEPT
LETTER_ROWS = BASE_ROW + 8
HALF_ROOT = math.sqrt(0.5)


def lane_tables():
    angle = 2.0 * np.pi / LANES * (np.arange(LANES)[:, None] * np.arange(LANES)[None, :] % LANES)
    cos, sin = np.cos(angle), np.sin(angle)
    table = np.block([[cos, -sin], [sin, cos]]).astype(np.float32)
    high = table.astype(jnp.bfloat16)
    low = (table - high.astype(np.float32)).astype(jnp.bfloat16)
    return high, low


def twist_tables():
    angle = -2.0 * np.pi / NFFT * (np.arange(ROWS)[:, None] * np.arange(LANES)[None, :])
    return np.cos(angle).astype(np.float32), np.sin(angle).astype(np.float32)


def plus(a, b):
    return (a[0] + b[0], a[1] + b[1])


def minus(a, b):
    return (a[0] - b[0], a[1] - b[1])


def quarter(a, sign):
    return (a[1], -a[0]) if sign < 0 else (-a[1], a[0])


def dft4(x, sign):
    t0, t1 = plus(x[0], x[2]), minus(x[0], x[2])
    t2, t3 = plus(x[1], x[3]), quarter(minus(x[1], x[3]), sign)
    return [plus(t0, t2), plus(t1, t3), minus(t0, t2), minus(t1, t3)]


def dft8(x, sign):
    even = dft4(x[0::2], sign)
    odd = dft4(x[1::2], sign)
    re, im = odd[1]
    if sign < 0:
        odd[1] = ((re + im) * HALF_ROOT, (im - re) * HALF_ROOT)
    else:
        odd[1] = ((re - im) * HALF_ROOT, (im + re) * HALF_ROOT)
    odd[2] = quarter(odd[2], sign)
    re, im = odd[3]
    if sign < 0:
        odd[3] = ((im - re) * HALF_ROOT, (re + im) * -HALF_ROOT)
    else:
        odd[3] = ((re + im) * -HALF_ROOT, (re - im) * HALF_ROOT)
    return [plus(e, o) for e, o in zip(even, odd)] + [minus(e, o) for e, o in zip(even, odd)]


def turned(a, step, sign):
    step %= 32
    if step == 0:
        return a
    if step == 8:
        return quarter(a, sign)
    re, im = a
    if step == 4:
        if sign < 0:
            return ((re + im) * HALF_ROOT, (im - re) * HALF_ROOT)
        return ((re - im) * HALF_ROOT, (im + re) * HALF_ROOT)
    cos = math.cos(2.0 * math.pi * step / 32)
    sin = sign * math.sin(2.0 * math.pi * step / 32)
    return (re * cos - im * sin, re * sin + im * cos)


def split(values):
    high = values.astype(jnp.bfloat16)
    return high, (values - high.astype(jnp.float32)).astype(jnp.bfloat16)


def lane_dft(high, low, table_high, table_low):
    dot = functools.partial(jnp.dot, preferred_element_type=jnp.float32)
    return dot(high, table_high) + (dot(low, table_high) + dot(high, table_low))


def frame_profile(
    row_of, weight_of, base_of, marks_of, chirp_ref, twist_ref, table_ref, mid, y_refs, v_refs, stokes_ref, acc
):
    def rows_in(pol, b):
        rows = []
        for a in range(8):
            row = 4 * a + b
            gain = weight_of(row // 2)
            rows.append(tuple(row_of(row, pol, part).astype(jnp.float32) * gain for part in range(2)))
        for ka, value in enumerate(dft8(rows, -1)):
            value = turned(value, b * ka, -1)
            mid[pol, 0, b, ka] = value[0]
            mid[pol, 1, b, ka] = value[1]

    def rows_across(pol, ka):
        values = dft4([(mid[pol, 0, b, ka], mid[pol, 1, b, ka]) for b in range(4)], -1)
        for kb in range(4):
            k = ka + 8 * kb
            re, im = values[kb]
            if k:
                cos, sin = twist_ref[0, k : k + 1], twist_ref[1, k : k + 1]
                re, im = re * cos - im * sin, re * sin + im * cos
            for part, value in enumerate((re, im)):
                high, low = split(value)
                where = (pl.ds(GROUP * k, GROUP), pl.ds(LANES * part, LANES))
                y_refs[pol, 0, *where] = high
                y_refs[pol, 1, *where] = low

    def lanes_there_and_back(pol, m):
        rows = pl.ds(SPAN * GROUP * m, SPAN * GROUP)
        spectrum = lane_dft(y_refs[pol, 0, rows], y_refs[pol, 1, rows], table_ref[0], table_ref[1])
        re, im = spectrum[:, :LANES], spectrum[:, LANES:]
        cos, sin = chirp_ref[0, rows], chirp_ref[1, rows]
        swapped = jnp.concatenate([re * sin + im * cos, re * cos - im * sin], axis=1)
        back = lane_dft(*split(swapped), table_ref[0], table_ref[1])
        im, re = (back[:, part].reshape(SPAN, GROUP, LANES) for part in (slice(0, LANES), slice(LANES, None)))
        cos = twist_ref[0, SPAN * m : SPAN * (m + 1)][:, None, :]
        sin = twist_ref[1, SPAN * m : SPAN * (m + 1)][:, None, :]
        v_refs[pol, 0, SPAN * m : SPAN * (m + 1)] = re * cos + im * sin
        v_refs[pol, 1, SPAN * m : SPAN * (m + 1)] = im * cos - re * sin

    def rows_back(pol, b):
        values = dft8([(v_refs[pol, 0, 4 * a + b], v_refs[pol, 1, 4 * a + b]) for a in range(8)], 1)
        for na, value in enumerate(values):
            value = turned(value, b * na, 1)
            mid[pol, 0, b, na] = value[0]
            mid[pol, 1, b, na] = value[1]

    def rows_out(na):
        x, y = (
            dft4([(mid[pol, 0, b, na], mid[pol, 1, b, na]) for b in range(4)], 1) for pol in range(2)
        )
        for nb in range(1, 4):
            (xr, xi), (yr, yi) = x[nb], y[nb]
            power_x = xr * xr + xi * xi
            power_y = yr * yr + yi * yi
            cross_re = xr * yr + xi * yi
            cross_im = xi * yr - xr * yi
            row = na + 8 * (nb - 1)
            lanes = pl.ds(LANES * (row % 2), LANES)
            for s, value in enumerate((power_x + power_y, power_x - power_y, 2.0 * cross_re, 2.0 * cross_im)):
                stokes_ref[row // 2, pl.ds(GROUP * s, GROUP), lanes] = value.astype(jnp.bfloat16)

    bins = lax.broadcasted_iota(jnp.int32, (WINDOW, BLK), 0)

    def fold(m):
        onehot = jnp.where(bins == marks_of(m), 1.0, 0.0).astype(jnp.bfloat16)
        part = lax.dot_general(
            onehot, stokes_ref[m], (((1,), (1,)), ((), ())), preferred_element_type=jnp.float32
        )
        place = pl.ds(pl.multiple_of(base_of(m), 8), WINDOW)
        acc[place] += part

    spans = ROWS // SPAN
    for b in range(4):
        rows_in(0, b)
    for ka in range(8):
        rows_across(0, ka)
    for m in range(spans):
        lanes_there_and_back(0, m)
        for b in range(4 * m // spans, 4 * (m + 1) // spans):
            rows_in(1, b)
    for ka in range(8):
        rows_across(1, ka)
    for m in range(spans):
        lanes_there_and_back(1, m)
        for b in range(4 * m // spans, 4 * (m + 1) // spans):
            rows_back(0, b)
    for b in range(4):
        rows_back(1, b)
    for na in range(8):
        rows_out(na)
        if na % 2:
            for m in range(na // 2, BLOCKS, 4):
                fold(m)


def own_row(buf_ref, slab, row, pol, part):
    return buf_ref[row // 3, slab, pol, part, :, pl.ds(LANES * (row % 3), LANES)]


def lay_gains(gains, weights_of):
    for block in range(ROWS // 2):
        gains[block] = jnp.broadcast_to(weights_of(block), (GROUP, LANES))


def marks_from(marks_ref, index, m):
    return jnp.concatenate([marks_ref[index, 2 * m : 2 * m + 1], marks_ref[index, 2 * m + 1 : 2 * m + 2]], axis=1)


def later_kernel(me_ref, *refs):
    letter_refs, refs = refs[:RUNS], refs[RUNS:]
    buf_ref, chirp_ref, twist_ref, table_ref, acc_ref, sorted_ref, gains, marks, *scratches = refs
    me = me_ref[0]
    for turn in range(RUNS):
        sorted_ref[(me - turn + RUNS) % RUNS] = letter_refs[turn][...]
    marks[...] = sorted_ref[:, GROUP : GROUP + KEPT].astype(jnp.int32)
    acc_ref[...] = jnp.zeros_like(acc_ref)

    def step(frame, carry):
        def row_of(row, pol, part):
            if row < RIM:
                return own_row(buf_ref, frame - 1, row + KEPT - RIM, pol, part)
            return own_row(buf_ref, frame, row - RIM, pol, part)

        before, own = sorted_ref[frame - 1, :GROUP], sorted_ref[frame, :GROUP]

        def weights_of(block):
            if block < RIM // 2:
                return before[:, block + BLOCKS - RIM // 2 : block + BLOCKS - RIM // 2 + 1]
            return own[:, block - RIM // 2 : block - RIM // 2 + 1]

        lay_gains(gains, weights_of)
        bases = sorted_ref[frame, BASE_ROW : BASE_ROW + 1].astype(jnp.int32)
        frame_profile(
            row_of,
            lambda block: gains[block],
            lambda m: bases[0, m],
            lambda m: marks_from(marks, frame, m),
            chirp_ref,
            twist_ref,
            table_ref,
            *scratches,
            acc_ref,
        )
        return carry

    lax.fori_loop(1, RUNS, step, 0)


def first_kernel(
    buf_ref, tail_ref, sorted_ref, chirp_ref, twist_ref, table_ref, given_ref, out_ref, acc, gains, marks, *scratches
):
    acc[...] = given_ref[...]
    high, middle, low = (tail_ref[0, 0, part // 2, part % 2, :, :LANES].astype(jnp.float32) for part in range(3))
    before = (high + middle) + low
    own = sorted_ref[0, :GROUP]
    marks[0] = sorted_ref[0, GROUP : GROUP + KEPT].astype(jnp.int32)

    def weights_of(block):
        if block < RIM // 2:
            return before[:, block + BLOCKS - RIM // 2 : block + BLOCKS - RIM // 2 + 1]
        return own[:, block - RIM // 2 : block - RIM // 2 + 1]

    def row_of(row, pol, part):
        if row < RIM:
            return own_row(tail_ref, 0, row + 1, pol, part)
        return own_row(buf_ref, 0, row - RIM, pol, part)

    lay_gains(gains, weights_of)
    bases = sorted_ref[0, BASE_ROW : BASE_ROW + 1].astype(jnp.int32)
    frame_profile(
        row_of,
        lambda block: gains[block],
        lambda m: bases[0, m],
        lambda m: marks_from(marks, 0, m),
        chirp_ref,
        twist_ref,
        table_ref,
        *scratches,
        acc,
    )
    acc[:WINDOW] += acc[NBIN:]
    for share in range(NBIN // 16):
        out_ref[share] = jnp.concatenate([acc[16 * share : 16 * share + 8], acc[16 * share + 8 : 16 * share + 16]], axis=1)


def tail_kernel(me_ref, *refs):
    letter_refs, piece_refs, out_ref, sorted_ref = refs[:RUNS], refs[RUNS:-2], refs[-2], refs[-1]
    me = me_ref[0]
    for turn in range(RUNS):
        sorted_ref[(me - turn + RUNS) % RUNS] = letter_refs[turn][:GROUP]
    rest = sorted_ref[RUNS - 1]
    for index, piece in enumerate(piece_refs):
        out_ref[index] = piece[0]
    for part in range(3):
        rounded = rest.astype(jnp.bfloat16)
        out_ref[0, 0, part // 2, part % 2, :, :LANES] = rounded
        rest = rest - rounded.astype(jnp.float32)


def spread_kernel(samples_ref, out_ref, sems):
    copies = [
        pltpu.make_async_copy(samples_ref.at[pol, part], out_ref.at[:, pol, part], sems.at[pol, part])
        for pol in range(2)
        for part in range(2)
    ]
    for copy in copies:
        copy.start()
    for copy in copies:
        copy.wait()


def scratch():
    return [
        pltpu.VMEM((2, 2, 4, 8, GROUP, LANES), jnp.float32),
        pltpu.VMEM((2, 2, ROWS * GROUP, 2 * LANES), jnp.bfloat16),
        pltpu.VMEM((2, 2, ROWS, GROUP, LANES), jnp.float32),
        pltpu.VMEM((BLOCKS, 4 * GROUP, BLK), jnp.bfloat16),
    ]


def whole():
    return pl.BlockSpec(memory_space=pltpu.VMEM)


def smem():
    return pl.BlockSpec(memory_space=pltpu.SMEM)


def tail_message(me, letters, buf):
    block = (1, 1) + buf.shape[2:]
    first = MEMBERS - 3
    return pl.pallas_call(
        tail_kernel,
        out_shape=jax.ShapeDtypeStruct((3, 1) + buf.shape[2:], buf.dtype),
        grid=(1,),
        in_specs=[smem()]
        + [whole()] * RUNS
        + [pl.BlockSpec(block, lambda i, at=first + at: (at, RUNS - 1, 0, 0, 0, 0)) for at in range(3)],
        out_specs=whole(),
        scratch_shapes=[pltpu.VMEM((RUNS, GROUP, LANES), jnp.float32)],
        name="tail_message",
    )(me, *letters, buf, buf, buf)


def fold_frames(buf, tail_of, me, letters, chirp):
    twist = jnp.asarray(np.stack(twist_tables()))
    table = jnp.asarray(np.stack(lane_tables()))
    tail = tail_of(tail_message(me, letters, buf))
    params = pltpu.CompilerParams(vmem_limit_bytes=28 * 1024 * 1024)
    flops = 2 * 2 * 2 * 3 * ROWS * GROUP * 256 * 256
    later, ordered = pl.pallas_call(
        later_kernel,
        out_shape=[
            jax.ShapeDtypeStruct((ACC_ROWS, 4 * GROUP), jnp.float32),
            jax.ShapeDtypeStruct((RUNS, LETTER_ROWS, LANES), jnp.float32),
        ],
        in_specs=[smem()] + [whole()] * (RUNS + 4),
        out_specs=[whole()] * 2,
        scratch_shapes=[
            pltpu.VMEM((ROWS // 2, GROUP, LANES), jnp.float32),
            pltpu.VMEM((RUNS, KEPT, LANES), jnp.int32),
        ]
        + scratch(),
        compiler_params=params,
        cost_estimate=pl.CostEstimate(flops=3 * flops, bytes_accessed=30_000_000, transcendentals=0),
        name="later_frames",
    )(me, *letters, buf, chirp, twist, table)
    block = (MEMBERS, 1) + buf.shape[2:]
    return pl.pallas_call(
        first_kernel,
        out_shape=jax.ShapeDtypeStruct((NBIN // 16, 8, LANES), jnp.float32),
        grid=(1,),
        in_specs=[pl.BlockSpec(block, lambda i: (0,) * 6)] + [whole()] * 6,
        out_specs=whole(),
        scratch_shapes=[
            pltpu.VMEM((ACC_ROWS, 4 * GROUP), jnp.float32),
            pltpu.VMEM((ROWS // 2, GROUP, LANES), jnp.float32),
            pltpu.VMEM((1, KEPT, LANES), jnp.int32),
        ]
        + scratch(),
        compiler_params=params,
        cost_estimate=pl.CostEstimate(flops=flops, bytes_accessed=10_000_000, transcendentals=0),
        name="first_frame",
    )(buf, tail, ordered, chirp, twist, table, later)


def last_kernel(scale, shares_ref, out_ref):
    total = [jnp.sum(shares_ref[:, slab], axis=0) * scale for slab in range(RUNS)]
    for half in range(2):
        for s in range(4):
            lanes = slice(64 * half + GROUP * s, 64 * half + GROUP * (s + 1))
            out_ref[pl.ds(32 * half + s, 8, stride=4)] = jnp.concatenate([part[:, lanes] for part in total], axis=1)


def turned_to(block_for, axis, turn):
    size = lax.axis_size(axis)
    there = (lax.axis_index(axis) + turn) % size
    if turn == 0:
        return block_for(there)
    return lax.ppermute(block_for(there), axis, [(i, (i + turn) % size) for i in range(size)])


def from_before(block):
    size = lax.axis_size("xy")
    return lax.ppermute(block, "xy", [(i, i + 1) for i in range(size - 1)])


def chirp_table(sweep):
    k = jnp.arange(ROWS, dtype=jnp.int32)[:, None] + ROWS * jnp.arange(LANES, dtype=jnp.int32)[None, :]
    u = jnp.where(k < NFFT // 2, k, k - NFFT).astype(jnp.float32) / NFFT
    phase = (jnp.pi * sweep)[None, :, None] * (u * u + u)[:, None, :]
    table = jnp.stack([jnp.cos(phase), jnp.sin(phase)]) * (1.0 / NFFT)
    return table.reshape(2, ROWS * GROUP, LANES)


def on_device(samples, scales, flags, sweep, phase_bin):
    parts = pl.pallas_call(
        spread_kernel,
        out_shape=jax.ShapeDtypeStruct((MEMBERS * RUNS, 2, 2, GROUP, PIECE), samples.dtype),
        in_specs=[pl.BlockSpec(memory_space=pl.ANY)],
        out_specs=pl.BlockSpec(memory_space=pl.ANY),
        scratch_shapes=[pltpu.SemaphoreType.DMA((2, 2))],
        name="spread",
    )(samples.reshape(2, 2, MEMBERS * RUNS, GROUP, PIECE))
    buf = lax.all_to_all(parts, ("chan", "zl"), split_axis=0, concat_axis=0, tiled=True)
    buf = buf.reshape(MEMBERS, RUNS, 2, 2, GROUP, PIECE)

    me = lax.axis_index("zl")
    weight = scales * (1 - flags).astype(jnp.float32)
    weight = jnp.pad(weight, ((0, 0), (0, LANES - BLOCKS)))
    bins = phase_bin.reshape(KEPT, LANES)
    base = bins[::2, 0] // 8 * 8
    marks = (bins - jnp.repeat(base, 2)[:, None]) % NBIN

    def weights_for(place):
        return lax.dynamic_slice_in_dim(weight, place * GROUP, GROUP, 0)

    base_rows = jnp.pad(base[None, :], ((0, LETTER_ROWS - BASE_ROW - 1), (0, LANES - BLOCKS)))
    below = jnp.concatenate([marks, base_rows]).astype(jnp.float32)
    letters = [
        turned_to(lambda place: jnp.concatenate([weights_for(place), below]), "zl", turn) for turn in range(RUNS)
    ]
    chirp = chirp_table(lax.dynamic_slice_in_dim(sweep, me * GROUP, GROUP, 0))

    partial = fold_frames(buf, from_before, me.reshape(1), letters, chirp)
    shares = lax.all_to_all(partial, ("xy", "zl"), split_axis=0, concat_axis=0, tiled=True)
    size = lax.axis_size("xy")
    return pl.pallas_call(
        functools.partial(last_kernel, NBIN / (SLAB * RUNS * size)),
        out_shape=jax.ShapeDtypeStruct((16 * 4, RUNS * GROUP), jnp.float32),
        name="last_sum",
    )(shares.reshape(size, RUNS, 8, LANES)).reshape(16, 4, RUNS * GROUP)


def solution(mesh):
    inner = Mesh(mesh.devices.reshape(-1, RUNS, MEMBERS), ("xy", "zl", "chan"))
    time = ("xy", "zl")
    placed = (
        P(None, None, None, ("xy", "zl", "chan")),
        P("chan", time),
        P("chan", time),
        P("chan"),
        P(time),
    )
    return jax.shard_map(
        on_device, mesh=inner, in_specs=placed, out_specs=P(time, None, "chan"), check_vma=False
    )
```

```python
import functools
import math

import jax
import jax.numpy as jnp
import numpy as np
from jax import lax
from jax.experimental import pallas as pl
from jax.experimental.pallas import tpu as pltpu
from jax.sharding import Mesh, PartitionSpec as P

NFFT = 4096
OVER = 1024
BLK = 256
NBIN = 1024
LANES = 128
ROWS = NFFT // LANES
RIM = OVER // LANES
KEPT = ROWS - RIM
RUNS = 4
MEMBERS = 8
PIECE = 384
SLAB = MEMBERS * PIECE
GROUP = 16
BLOCKS = SLAB // BLK
WINDOW = 144
ACC_ROWS = NBIN + WINDOW
SPAN = 16
BASE_ROW = GROUP + KEPT
LETTER_ROWS = BASE_ROW + 8
HALF_ROOT = math.sqrt(0.5)


def lane_tables():
    angle = 2.0 * np.pi / LANES * (np.arange(LANES)[:, None] * np.arange(LANES)[None, :] % LANES)
    cos, sin = np.cos(angle), np.sin(angle)
    table = np.block([[cos, -sin], [sin, cos]]).astype(np.float32)
    high = table.astype(jnp.bfloat16)
    low = (table - high.astype(np.float32)).astype(jnp.bfloat16)
    return high, low


def twist_tables():
    angle = -2.0 * np.pi / NFFT * (np.arange(ROWS)[:, None] * np.arange(LANES)[None, :])
    return np.cos(angle).astype(np.float32), np.sin(angle).astype(np.float32)


def plus(a, b):
    return (a[0] + b[0], a[1] + b[1])


def minus(a, b):
    return (a[0] - b[0], a[1] - b[1])


def quarter(a, sign):
    return (a[1], -a[0]) if sign < 0 else (-a[1], a[0])


def dft4(x, sign):
    t0, t1 = plus(x[0], x[2]), minus(x[0], x[2])
    t2, t3 = plus(x[1], x[3]), quarter(minus(x[1], x[3]), sign)
    return [plus(t0, t2), plus(t1, t3), minus(t0, t2), minus(t1, t3)]


def dft8(x, sign):
    even = dft4(x[0::2], sign)
    odd = dft4(x[1::2], sign)
    re, im = odd[1]
    if sign < 0:
        odd[1] = ((re + im) * HALF_ROOT, (im - re) * HALF_ROOT)
    else:
        odd[1] = ((re - im) * HALF_ROOT, (im + re) * HALF_ROOT)
    odd[2] = quarter(odd[2], sign)
    re, im = odd[3]
    if sign < 0:
        odd[3] = ((im - re) * HALF_ROOT, (re + im) * -HALF_ROOT)
    else:
        odd[3] = ((re + im) * -HALF_ROOT, (re - im) * HALF_ROOT)
    return [plus(e, o) for e, o in zip(even, odd)] + [minus(e, o) for e, o in zip(even, odd)]


def turned(a, step, sign):
    step %= 32
    if step == 0:
        return a
    if step == 8:
        return quarter(a, sign)
    re, im = a
    if step == 4:
        if sign < 0:
            return ((re + im) * HALF_ROOT, (im - re) * HALF_ROOT)
        return ((re - im) * HALF_ROOT, (im + re) * HALF_ROOT)
    cos = math.cos(2.0 * math.pi * step / 32)
    sin = sign * math.sin(2.0 * math.pi * step / 32)
    return (re * cos - im * sin, re * sin + im * cos)


def split(values):
    high = values.astype(jnp.bfloat16)
    return high, (values - high.astype(jnp.float32)).astype(jnp.bfloat16)


def lane_dft(high, low, table_high, table_low):
    dot = functools.partial(jnp.dot, preferred_element_type=jnp.float32)
    return dot(high, table_high) + (dot(low, table_high) + dot(high, table_low))


def frame_profile(
    row_of, weight_of, base_of, marks_of, chirp_ref, twist_ref, table_ref, mid, y_refs, v_refs, stokes_ref, acc
):
    def rows_in(pol, b):
        rows = []
        for a in range(8):
            row = 4 * a + b
            gain = weight_of(row // 2)
            rows.append(tuple(row_of(row, pol, part).astype(jnp.float32) * gain for part in range(2)))
        for ka, value in enumerate(dft8(rows, -1)):
            value = turned(value, b * ka, -1)
            mid[pol, 0, b, ka] = value[0]
            mid[pol, 1, b, ka] = value[1]

    def rows_across(pol, ka):
        values = dft4([(mid[pol, 0, b, ka], mid[pol, 1, b, ka]) for b in range(4)], -1)
        for kb in range(4):
            k = ka + 8 * kb
            re, im = values[kb]
            if k:
                cos, sin = twist_ref[0, k : k + 1], twist_ref[1, k : k + 1]
                re, im = re * cos - im * sin, re * sin + im * cos
            for part, value in enumerate((re, im)):
                high, low = split(value)
                where = (pl.ds(GROUP * k, GROUP), pl.ds(LANES * part, LANES))
                y_refs[pol, 0, *where] = high
                y_refs[pol, 1, *where] = low

    def lanes_there_and_back(pol, m):
        rows = pl.ds(SPAN * GROUP * m, SPAN * GROUP)
        spectrum = lane_dft(y_refs[pol, 0, rows], y_refs[pol, 1, rows], table_ref[0], table_ref[1])
        re, im = spectrum[:, :LANES], spectrum[:, LANES:]
        cos, sin = chirp_ref[0, rows], chirp_ref[1, rows]
        swapped = jnp.concatenate([re * sin + im * cos, re * cos - im * sin], axis=1)
        back = lane_dft(*split(swapped), table_ref[0], table_ref[1])
        im, re = (back[:, part].reshape(SPAN, GROUP, LANES) for part in (slice(0, LANES), slice(LANES, None)))
        cos = twist_ref[0, SPAN * m : SPAN * (m + 1)][:, None, :]
        sin = twist_ref[1, SPAN * m : SPAN * (m + 1)][:, None, :]
        v_refs[pol, 0, SPAN * m : SPAN * (m + 1)] = re * cos + im * sin
        v_refs[pol, 1, SPAN * m : SPAN * (m + 1)] = im * cos - re * sin

    def rows_back(pol, b):
        values = dft8([(v_refs[pol, 0, 4 * a + b], v_refs[pol, 1, 4 * a + b]) for a in range(8)], 1)
        for na, value in enumerate(values):
            value = turned(value, b * na, 1)
            mid[pol, 0, b, na] = value[0]
            mid[pol, 1, b, na] = value[1]

    def rows_out(na):
        x, y = (
            dft4([(mid[pol, 0, b, na], mid[pol, 1, b, na]) for b in range(4)], 1) for pol in range(2)
        )
        for nb in range(1, 4):
            (xr, xi), (yr, yi) = x[nb], y[nb]
            power_x = xr * xr + xi * xi
            power_y = yr * yr + yi * yi
            cross_re = xr * yr + xi * yi
            cross_im = xi * yr - xr * yi
            row = na + 8 * (nb - 1)
            lanes = pl.ds(LANES * (row % 2), LANES)
            for s, value in enumerate((power_x + power_y, power_x - power_y, 2.0 * cross_re, 2.0 * cross_im)):
                stokes_ref[row // 2, pl.ds(GROUP * s, GROUP), lanes] = value.astype(jnp.bfloat16)

    bins = lax.broadcasted_iota(jnp.int32, (WINDOW, BLK), 0)

    def fold(m):
        onehot = jnp.where(bins == marks_of(m), 1.0, 0.0).astype(jnp.bfloat16)
        part = lax.dot_general(
            onehot, stokes_ref[m], (((1,), (1,)), ((), ())), preferred_element_type=jnp.float32
        )
        place = pl.ds(pl.multiple_of(base_of(m), 8), WINDOW)
        acc[place] += part

    spans = ROWS // SPAN
    for b in range(4):
        rows_in(0, b)
    for ka in range(8):
        rows_across(0, ka)
    for m in range(spans):
        lanes_there_and_back(0, m)
        for b in range(4 * m // spans, 4 * (m + 1) // spans):
            rows_in(1, b)
    for ka in range(8):
        rows_across(1, ka)
    for m in range(spans):
        lanes_there_and_back(1, m)
        for b in range(4 * m // spans, 4 * (m + 1) // spans):
            rows_back(0, b)
    for b in range(4):
        rows_back(1, b)
    for na in range(8):
        rows_out(na)
        if na % 2:
            for m in range(na // 2, BLOCKS, 4):
                fold(m)


def own_row(buf_ref, slab, row, pol, part):
    return buf_ref[row // 3, slab, pol, part, :, pl.ds(LANES * (row % 3), LANES)]


def lay_gains(gains, weights_of):
    for block in range(ROWS // 2):
        gains[block] = jnp.broadcast_to(weights_of(block), (GROUP, LANES))


def marks_from(marks_ref, index, m):
    return jnp.concatenate([marks_ref[index, 2 * m : 2 * m + 1], marks_ref[index, 2 * m + 1 : 2 * m + 2]], axis=1)


def later_kernel(me_ref, *refs):
    letter_refs, refs = refs[:RUNS], refs[RUNS:]
    buf_ref, chirp_ref, twist_ref, table_ref, acc_ref, sorted_ref, gains, marks, *scratches = refs
    me = me_ref[0]
    for turn in range(RUNS):
        sorted_ref[(me - turn + RUNS) % RUNS] = letter_refs[turn][...]
    marks[...] = sorted_ref[:, GROUP : GROUP + KEPT].astype(jnp.int32)
    acc_ref[...] = jnp.zeros_like(acc_ref)

    def step(frame, carry):
        def row_of(row, pol, part):
            if row < RIM:
                return own_row(buf_ref, frame - 1, row + KEPT - RIM, pol, part)
            return own_row(buf_ref, frame, row - RIM, pol, part)

        before, own = sorted_ref[frame - 1, :GROUP], sorted_ref[frame, :GROUP]

        def weights_of(block):
            if block < RIM // 2:
                return before[:, block + BLOCKS - RIM // 2 : block + BLOCKS - RIM // 2 + 1]
            return own[:, block - RIM // 2 : block - RIM // 2 + 1]

        lay_gains(gains, weights_of)
        bases = sorted_ref[frame, BASE_ROW : BASE_ROW + 1].astype(jnp.int32)
        frame_profile(
            row_of,
            lambda block: gains[block],
            lambda m: bases[0, m],
            lambda m: marks_from(marks, frame, m),
            chirp_ref,
            twist_ref,
            table_ref,
            *scratches,
            acc_ref,
        )
        return carry

    lax.fori_loop(1, RUNS, step, 0)


def first_kernel(
    buf_ref, tail_ref, sorted_ref, chirp_ref, twist_ref, table_ref, given_ref, out_ref, acc, gains, marks, *scratches
):
    acc[...] = given_ref[...]
    high, middle, low = (tail_ref[0, 0, part // 2, part % 2, :, :LANES].astype(jnp.float32) for part in range(3))
    before = (high + middle) + low
    own = sorted_ref[0, :GROUP]
    marks[0] = sorted_ref[0, GROUP : GROUP + KEPT].astype(jnp.int32)

    def weights_of(block):
        if block < RIM // 2:
            return before[:, block + BLOCKS - RIM // 2 : block + BLOCKS - RIM // 2 + 1]
        return own[:, block - RIM // 2 : block - RIM // 2 + 1]

    def row_of(row, pol, part):
        if row < RIM:
            return own_row(tail_ref, 0, row + 1, pol, part)
        return own_row(buf_ref, 0, row - RIM, pol, part)

    lay_gains(gains, weights_of)
    bases = sorted_ref[0, BASE_ROW : BASE_ROW + 1].astype(jnp.int32)
    frame_profile(
        row_of,
        lambda block: gains[block],
        lambda m: bases[0, m],
        lambda m: marks_from(marks, 0, m),
        chirp_ref,
        twist_ref,
        table_ref,
        *scratches,
        acc,
    )
    acc[:WINDOW] += acc[NBIN:]
    for share in range(NBIN // 16):
        out_ref[share] = jnp.concatenate([acc[16 * share : 16 * share + 8], acc[16 * share + 8 : 16 * share + 16]], axis=1)


def tail_kernel(me_ref, *refs):
    letter_refs, piece_refs, out_ref, sorted_ref = refs[:RUNS], refs[RUNS:-2], refs[-2], refs[-1]
    me = me_ref[0]
    for turn in range(RUNS):
        sorted_ref[(me - turn + RUNS) % RUNS] = letter_refs[turn][:GROUP]
    rest = sorted_ref[RUNS - 1]
    for index, piece in enumerate(piece_refs):
        out_ref[index] = piece[0]
    for part in range(3):
        rounded = rest.astype(jnp.bfloat16)
        out_ref[0, 0, part // 2, part % 2, :, :LANES] = rounded
        rest = rest - rounded.astype(jnp.float32)


def spread_kernel(samples_ref, out_ref, sems):
    copies = [
        pltpu.make_async_copy(samples_ref.at[pol, part], out_ref.at[:, pol, part], sems.at[pol, part])
        for pol in range(2)
        for part in range(2)
    ]
    for copy in copies:
        copy.start()
    for copy in copies:
        copy.wait()


def scratch():
    return [
        pltpu.VMEM((2, 2, 4, 8, GROUP, LANES), jnp.float32),
        pltpu.VMEM((2, 2, ROWS * GROUP, 2 * LANES), jnp.bfloat16),
        pltpu.VMEM((2, 2, ROWS, GROUP, LANES), jnp.float32),
        pltpu.VMEM((BLOCKS, 4 * GROUP, BLK), jnp.bfloat16),
    ]


def whole():
    return pl.BlockSpec(memory_space=pltpu.VMEM)


def small_kernel():
    return pltpu.CompilerParams(vmem_limit_bytes=4 * 1024 * 1024)


def smem():
    return pl.BlockSpec(memory_space=pltpu.SMEM)


def tail_message(me, letters, buf):
    block = (1, 1) + buf.shape[2:]
    first = MEMBERS - 3
    return pl.pallas_call(
        tail_kernel,
        out_shape=jax.ShapeDtypeStruct((3, 1) + buf.shape[2:], buf.dtype),
        grid=(1,),
        in_specs=[smem()]
        + [whole()] * RUNS
        + [pl.BlockSpec(block, lambda i, at=first + at: (at, RUNS - 1, 0, 0, 0, 0)) for at in range(3)],
        out_specs=whole(),
        scratch_shapes=[pltpu.VMEM((RUNS, GROUP, LANES), jnp.float32)],
        compiler_params=small_kernel(),
        name="tail_message",
    )(me, *letters, buf, buf, buf)


def fold_frames(buf, tail_of, me, letters, chirp):
    twist = jnp.asarray(np.stack(twist_tables()))
    table = jnp.asarray(np.stack(lane_tables()))
    tail = tail_of(tail_message(me, letters, buf))
    params = pltpu.CompilerParams(vmem_limit_bytes=28 * 1024 * 1024)
    flops = 2 * 2 * 2 * 3 * ROWS * GROUP * 256 * 256
    later, ordered = pl.pallas_call(
        later_kernel,
        out_shape=[
            jax.ShapeDtypeStruct((ACC_ROWS, 4 * GROUP), jnp.float32),
            jax.ShapeDtypeStruct((RUNS, LETTER_ROWS, LANES), jnp.float32),
        ],
        in_specs=[smem()] + [whole()] * (RUNS + 4),
        out_specs=[whole()] * 2,
        scratch_shapes=[
            pltpu.VMEM((ROWS // 2, GROUP, LANES), jnp.float32),
            pltpu.VMEM((RUNS, KEPT, LANES), jnp.int32),
        ]
        + scratch(),
        compiler_params=params,
        cost_estimate=pl.CostEstimate(flops=3 * flops, bytes_accessed=30_000_000, transcendentals=0),
        name="later_frames",
    )(me, *letters, buf, chirp, twist, table)
    block = (MEMBERS, 1) + buf.shape[2:]
    return pl.pallas_call(
        first_kernel,
        out_shape=jax.ShapeDtypeStruct((NBIN // 16, 8, LANES), jnp.float32),
        grid=(1,),
        in_specs=[pl.BlockSpec(block, lambda i: (0,) * 6)] + [whole()] * 6,
        out_specs=whole(),
        scratch_shapes=[
            pltpu.VMEM((ACC_ROWS, 4 * GROUP), jnp.float32),
            pltpu.VMEM((ROWS // 2, GROUP, LANES), jnp.float32),
            pltpu.VMEM((1, KEPT, LANES), jnp.int32),
        ]
        + scratch(),
        compiler_params=params,
        cost_estimate=pl.CostEstimate(flops=flops, bytes_accessed=10_000_000, transcendentals=0),
        name="first_frame",
    )(buf, tail, ordered, chirp, twist, table, later)


def last_kernel(scale, shares_ref, out_ref):
    total = [jnp.sum(shares_ref[:, slab], axis=0) * scale for slab in range(RUNS)]
    for half in range(2):
        for s in range(4):
            lanes = slice(64 * half + GROUP * s, 64 * half + GROUP * (s + 1))
            out_ref[pl.ds(32 * half + s, 8, stride=4)] = jnp.concatenate([part[:, lanes] for part in total], axis=1)


def turned_to(block_for, axis, turn):
    size = lax.axis_size(axis)
    there = (lax.axis_index(axis) + turn) % size
    if turn == 0:
        return block_for(there)
    return lax.ppermute(block_for(there), axis, [(i, (i + turn) % size) for i in range(size)])


def from_before(block):
    size = lax.axis_size("xy")
    return lax.ppermute(block, "xy", [(i, i + 1) for i in range(size - 1)])


def chirp_table(sweep):
    k = jnp.arange(ROWS, dtype=jnp.int32)[:, None] + ROWS * jnp.arange(LANES, dtype=jnp.int32)[None, :]
    u = jnp.where(k < NFFT // 2, k, k - NFFT).astype(jnp.float32) / NFFT
    phase = (jnp.pi * sweep)[None, :, None] * (u * u + u)[:, None, :]
    table = jnp.stack([jnp.cos(phase), jnp.sin(phase)]) * (1.0 / NFFT)
    return table.reshape(2, ROWS * GROUP, LANES)


def on_device(samples, scales, flags, sweep, phase_bin):
    parts = pl.pallas_call(
        spread_kernel,
        out_shape=jax.ShapeDtypeStruct((MEMBERS * RUNS, 2, 2, GROUP, PIECE), samples.dtype),
        in_specs=[pl.BlockSpec(memory_space=pl.ANY)],
        out_specs=whole(),
        scratch_shapes=[pltpu.SemaphoreType.DMA((2, 2))],
        compiler_params=small_kernel(),
        name="spread",
    )(samples.reshape(2, 2, MEMBERS * RUNS, GROUP, PIECE))
    buf = lax.all_to_all(parts, ("chan", "zl"), split_axis=0, concat_axis=0, tiled=True)
    buf = buf.reshape(MEMBERS, RUNS, 2, 2, GROUP, PIECE)

    me = lax.axis_index("zl")
    weight = scales * (1 - flags).astype(jnp.float32)
    weight = jnp.pad(weight, ((0, 0), (0, LANES - BLOCKS)))
    bins = phase_bin.reshape(KEPT, LANES)
    base = bins[::2, 0] // 8 * 8
    marks = (bins - jnp.repeat(base, 2)[:, None]) % NBIN

    def weights_for(place):
        return lax.dynamic_slice_in_dim(weight, place * GROUP, GROUP, 0)

    base_rows = jnp.pad(base[None, :], ((0, LETTER_ROWS - BASE_ROW - 1), (0, LANES - BLOCKS)))
    below = jnp.concatenate([marks, base_rows]).astype(jnp.float32)
    letters = [
        turned_to(lambda place: jnp.concatenate([weights_for(place), below]), "zl", turn) for turn in range(RUNS)
    ]
    chirp = chirp_table(lax.dynamic_slice_in_dim(sweep, me * GROUP, GROUP, 0))

    partial = fold_frames(buf, from_before, me.reshape(1), letters, chirp)
    shares = lax.all_to_all(partial, ("xy", "zl"), split_axis=0, concat_axis=0, tiled=True)
    size = lax.axis_size("xy")
    return pl.pallas_call(
        functools.partial(last_kernel, NBIN / (SLAB * RUNS * size)),
        out_shape=jax.ShapeDtypeStruct((16 * 4, RUNS * GROUP), jnp.float32),
        compiler_params=small_kernel(),
        name="last_sum",
    )(shares.reshape(size, RUNS, 8, LANES)).reshape(16, 4, RUNS * GROUP)


def solution(mesh):
    inner = Mesh(mesh.devices.reshape(-1, RUNS, MEMBERS), ("xy", "zl", "chan"))
    time = ("xy", "zl")
    placed = (
        P(None, None, None, ("xy", "zl", "chan")),
        P("chan", time),
        P("chan", time),
        P("chan"),
        P(time),
    )
    return jax.shard_map(
        on_device, mesh=inner, in_specs=placed, out_specs=P(time, None, "chan"), check_vma=False
    )
```

```python
import functools
import math

import jax
import jax.numpy as jnp
import numpy as np
from jax import lax
from jax.experimental import pallas as pl
from jax.experimental.pallas import tpu as pltpu
from jax.sharding import Mesh, PartitionSpec as P

NFFT = 4096
OVER = 1024
BLK = 256
NBIN = 1024
LANES = 128
ROWS = NFFT // LANES
RIM = OVER // LANES
KEPT = ROWS - RIM
RUNS = 4
MEMBERS = 8
PIECE = 384
SLAB = MEMBERS * PIECE
GROUP = 16
BLOCKS = SLAB // BLK
WINDOW = 144
ACC_ROWS = NBIN + WINDOW
DOT_ROWS = 256
BASE_ROW = GROUP + KEPT
LETTER_ROWS = BASE_ROW + 8
HALF_ROOT = math.sqrt(0.5)


def lane_tables():
    angle = 2.0 * np.pi / LANES * (np.arange(LANES)[:, None] * np.arange(LANES)[None, :] % LANES)
    cos, sin = np.cos(angle), np.sin(angle)
    table = np.block([[cos, -sin], [sin, cos]]).astype(np.float32)
    high = table.astype(jnp.bfloat16)
    low = (table - high.astype(np.float32)).astype(jnp.bfloat16)
    return high, low


def twist_tables():
    angle = -2.0 * np.pi / NFFT * (np.arange(ROWS)[:, None] * np.arange(LANES)[None, :])
    return np.cos(angle).astype(np.float32), np.sin(angle).astype(np.float32)


def plus(a, b):
    return (a[0] + b[0], a[1] + b[1])


def minus(a, b):
    return (a[0] - b[0], a[1] - b[1])


def quarter(a, sign):
    return (a[1], -a[0]) if sign < 0 else (-a[1], a[0])


def dft4(x, sign):
    t0, t1 = plus(x[0], x[2]), minus(x[0], x[2])
    t2, t3 = plus(x[1], x[3]), quarter(minus(x[1], x[3]), sign)
    return [plus(t0, t2), plus(t1, t3), minus(t0, t2), minus(t1, t3)]


def dft8(x, sign):
    even = dft4(x[0::2], sign)
    odd = dft4(x[1::2], sign)
    re, im = odd[1]
    if sign < 0:
        odd[1] = ((re + im) * HALF_ROOT, (im - re) * HALF_ROOT)
    else:
        odd[1] = ((re - im) * HALF_ROOT, (im + re) * HALF_ROOT)
    odd[2] = quarter(odd[2], sign)
    re, im = odd[3]
    if sign < 0:
        odd[3] = ((im - re) * HALF_ROOT, (re + im) * -HALF_ROOT)
    else:
        odd[3] = ((re + im) * -HALF_ROOT, (re - im) * HALF_ROOT)
    return [plus(e, o) for e, o in zip(even, odd)] + [minus(e, o) for e, o in zip(even, odd)]


def turned(a, step, sign):
    step %= 32
    if step == 0:
        return a
    if step == 8:
        return quarter(a, sign)
    re, im = a
    if step == 4:
        if sign < 0:
            return ((re + im) * HALF_ROOT, (im - re) * HALF_ROOT)
        return ((re - im) * HALF_ROOT, (im + re) * HALF_ROOT)
    cos = math.cos(2.0 * math.pi * step / 32)
    sin = sign * math.sin(2.0 * math.pi * step / 32)
    return (re * cos - im * sin, re * sin + im * cos)


def split(values):
    high = values.astype(jnp.bfloat16)
    return high, (values - high.astype(jnp.float32)).astype(jnp.bfloat16)


def lane_dft(high, low, table_high, table_low):
    dot = functools.partial(jnp.dot, preferred_element_type=jnp.float32)
    return dot(high, table_high) + (dot(low, table_high) + dot(high, table_low))


def frame_profile(
    row_of, weight_of, base_of, marks_of, chirp_ref, twist_ref, table_ref, mid, y_refs, s_refs, stokes_ref, acc
):
    def rows_in(pol, b):
        rows = []
        for a in range(8):
            row = 4 * a + b
            gain = weight_of(row // 2)
            rows.append(tuple(row_of(row, pol, part).astype(jnp.float32) * gain for part in range(2)))
        for ka, value in enumerate(dft8(rows, -1)):
            value = turned(value, b * ka, -1)
            mid[pol, 0, b, ka] = value[0]
            mid[pol, 1, b, ka] = value[1]

    def rows_across(pol, ka):
        values = dft4([(mid[pol, 0, b, ka], mid[pol, 1, b, ka]) for b in range(4)], -1)
        for kb in range(4):
            k = ka + 8 * kb
            re, im = values[kb]
            if k:
                cos, sin = twist_ref[0, k : k + 1], twist_ref[1, k : k + 1]
                re, im = re * cos - im * sin, re * sin + im * cos
            for part, value in enumerate((re, im)):
                high, low = split(value)
                where = (pl.ds(GROUP * k, GROUP), pl.ds(LANES * part, LANES))
                y_refs[pol, 0, *where] = high
                y_refs[pol, 1, *where] = low

    def lanes(pol, m):
        rows = pl.ds(DOT_ROWS * m, DOT_ROWS)
        s_refs[pol, rows] = lane_dft(y_refs[pol, 0, rows], y_refs[pol, 1, rows], table_ref[0], table_ref[1])

    def filtered(pol, k):
        rows = pl.ds(GROUP * k, GROUP)
        re, im = s_refs[pol, rows, :LANES], s_refs[pol, rows, LANES:]
        cos, sin = chirp_ref[0, rows], chirp_ref[1, rows]
        for part, value in enumerate((re * sin + im * cos, re * cos - im * sin)):
            high, low = split(value)
            where = (rows, pl.ds(LANES * part, LANES))
            y_refs[pol, 0, *where] = high
            y_refs[pol, 1, *where] = low

    def untwisted(pol, k):
        rows = pl.ds(GROUP * k, GROUP)
        im, re = s_refs[pol, rows, :LANES], s_refs[pol, rows, LANES:]
        if k == 0:
            return re, im
        cos, sin = twist_ref[0, k : k + 1], twist_ref[1, k : k + 1]
        return re * cos + im * sin, im * cos - re * sin

    def rows_back(pol, b):
        values = dft8([untwisted(pol, 4 * a + b) for a in range(8)], 1)
        for na, value in enumerate(values):
            value = turned(value, b * na, 1)
            mid[pol, 0, b, na] = value[0]
            mid[pol, 1, b, na] = value[1]

    def rows_out(na):
        x, y = (
            dft4([(mid[pol, 0, b, na], mid[pol, 1, b, na]) for b in range(4)], 1) for pol in range(2)
        )
        for nb in range(1, 4):
            (xr, xi), (yr, yi) = x[nb], y[nb]
            power_x = xr * xr + xi * xi
            power_y = yr * yr + yi * yi
            cross_re = xr * yr + xi * yi
            cross_im = xi * yr - xr * yi
            row = na + 8 * (nb - 1)
            lanes = pl.ds(LANES * (row % 2), LANES)
            for s, value in enumerate((power_x + power_y, power_x - power_y, 2.0 * cross_re, 2.0 * cross_im)):
                stokes_ref[row // 2, pl.ds(GROUP * s, GROUP), lanes] = value.astype(jnp.bfloat16)

    bins = lax.broadcasted_iota(jnp.int32, (WINDOW, BLK), 0).astype(jnp.bfloat16)

    def fold(m):
        onehot = jnp.where(bins == marks_of(m).astype(jnp.bfloat16), jnp.bfloat16(1), jnp.bfloat16(0))
        part = lax.dot_general(
            onehot, stokes_ref[m], (((1,), (1,)), ((), ())), preferred_element_type=jnp.float32
        )
        place = pl.ds(pl.multiple_of(base_of(m), 8), WINDOW)
        acc[place] += part

    spans = ROWS * GROUP // DOT_ROWS
    for b in range(4):
        rows_in(0, b)
    for ka in range(8):
        rows_across(0, ka)
    for m in range(spans):
        lanes(0, m)
    for b in range(4):
        rows_in(1, b)
    for ka in range(8):
        rows_across(1, ka)
    for k in range(ROWS):
        filtered(0, k)
    for m in range(spans):
        lanes(1, m)
    for m in range(spans):
        lanes(0, m)
    for k in range(ROWS):
        filtered(1, k)
    for b in range(4):
        rows_back(0, b)
    for m in range(spans):
        lanes(1, m)
    for b in range(4):
        rows_back(1, b)
    for na in range(8):
        rows_out(na)
        if na % 2:
            for m in range(na // 2, BLOCKS, 4):
                fold(m)


def own_row(buf_ref, slab, row, pol, part):
    return buf_ref[row // 3, slab, pol, part, :, pl.ds(LANES * (row % 3), LANES)]


def lay_gains(gains, weights_of):
    for block in range(ROWS // 2):
        gains[block] = jnp.broadcast_to(weights_of(block), (GROUP, LANES))


def marks_from(marks_ref, index, m):
    return jnp.concatenate([marks_ref[index, 2 * m : 2 * m + 1], marks_ref[index, 2 * m + 1 : 2 * m + 2]], axis=1)


def later_kernel(me_ref, *refs):
    letter_refs, refs = refs[:RUNS], refs[RUNS:]
    buf_ref, chirp_ref, twist_ref, table_ref, acc_ref, sorted_ref, gains, marks, *scratches = refs
    me = me_ref[0]
    for turn in range(RUNS):
        sorted_ref[(me - turn + RUNS) % RUNS] = letter_refs[turn][...]
    marks[...] = sorted_ref[:, GROUP : GROUP + KEPT].astype(jnp.int32)
    acc_ref[...] = jnp.zeros_like(acc_ref)

    def step(frame, carry):
        def row_of(row, pol, part):
            if row < RIM:
                return own_row(buf_ref, frame - 1, row + KEPT - RIM, pol, part)
            return own_row(buf_ref, frame, row - RIM, pol, part)

        before, own = sorted_ref[frame - 1, :GROUP], sorted_ref[frame, :GROUP]

        def weights_of(block):
            if block < RIM // 2:
                return before[:, block + BLOCKS - RIM // 2 : block + BLOCKS - RIM // 2 + 1]
            return own[:, block - RIM // 2 : block - RIM // 2 + 1]

        lay_gains(gains, weights_of)
        bases = sorted_ref[frame, BASE_ROW : BASE_ROW + 1].astype(jnp.int32)
        frame_profile(
            row_of,
            lambda block: gains[block],
            lambda m: bases[0, m],
            lambda m: marks_from(marks, frame, m),
            chirp_ref,
            twist_ref,
            table_ref,
            *scratches,
            acc_ref,
        )
        return carry

    lax.fori_loop(1, RUNS, step, 0)


def first_kernel(
    buf_ref, tail_ref, sorted_ref, chirp_ref, twist_ref, table_ref, given_ref, out_ref, acc, gains, marks, *scratches
):
    acc[...] = given_ref[...]
    high, middle, low = (tail_ref[0, 0, part // 2, part % 2, :, :LANES].astype(jnp.float32) for part in range(3))
    before = (high + middle) + low
    own = sorted_ref[0, :GROUP]
    marks[0] = sorted_ref[0, GROUP : GROUP + KEPT].astype(jnp.int32)

    def weights_of(block):
        if block < RIM // 2:
            return before[:, block + BLOCKS - RIM // 2 : block + BLOCKS - RIM // 2 + 1]
        return own[:, block - RIM // 2 : block - RIM // 2 + 1]

    def row_of(row, pol, part):
        if row < RIM:
            return own_row(tail_ref, 0, row + 1, pol, part)
        return own_row(buf_ref, 0, row - RIM, pol, part)

    lay_gains(gains, weights_of)
    bases = sorted_ref[0, BASE_ROW : BASE_ROW + 1].astype(jnp.int32)
    frame_profile(
        row_of,
        lambda block: gains[block],
        lambda m: bases[0, m],
        lambda m: marks_from(marks, 0, m),
        chirp_ref,
        twist_ref,
        table_ref,
        *scratches,
        acc,
    )
    acc[:WINDOW] += acc[NBIN:]
    for share in range(NBIN // 16):
        place = share % RUNS * (NBIN // 16 // RUNS) + share // RUNS
        out_ref[place] = jnp.concatenate([acc[16 * share : 16 * share + 8], acc[16 * share + 8 : 16 * share + 16]], axis=1)


def tail_kernel(me_ref, *refs):
    letter_refs, piece_refs, out_ref, sorted_ref = refs[:RUNS], refs[RUNS:-2], refs[-2], refs[-1]
    me = me_ref[0]
    for turn in range(RUNS):
        sorted_ref[(me - turn + RUNS) % RUNS] = letter_refs[turn][:GROUP]
    rest = sorted_ref[RUNS - 1]
    for index, piece in enumerate(piece_refs):
        out_ref[index] = piece[0]
    for part in range(3):
        rounded = rest.astype(jnp.bfloat16)
        out_ref[0, 0, part // 2, part % 2, :, :LANES] = rounded
        rest = rest - rounded.astype(jnp.float32)


def spread_kernel(samples_ref, out_ref, sems):
    copies = [
        pltpu.make_async_copy(samples_ref.at[pol, part], out_ref.at[:, pol, part], sems.at[pol, part])
        for pol in range(2)
        for part in range(2)
    ]
    for copy in copies:
        copy.start()
    for copy in copies:
        copy.wait()


def scratch():
    return [
        pltpu.VMEM((2, 2, 4, 8, GROUP, LANES), jnp.float32),
        pltpu.VMEM((2, 2, ROWS * GROUP, 2 * LANES), jnp.bfloat16),
        pltpu.VMEM((2, ROWS * GROUP, 2 * LANES), jnp.float32),
        pltpu.VMEM((BLOCKS, 4 * GROUP, BLK), jnp.bfloat16),
    ]


def whole():
    return pl.BlockSpec(memory_space=pltpu.VMEM)


def small_kernel():
    return pltpu.CompilerParams(vmem_limit_bytes=4 * 1024 * 1024)


def smem():
    return pl.BlockSpec(memory_space=pltpu.SMEM)


def tail_message(me, letters, buf):
    block = (1, 1) + buf.shape[2:]
    first = MEMBERS - 3
    return pl.pallas_call(
        tail_kernel,
        out_shape=jax.ShapeDtypeStruct((3, 1) + buf.shape[2:], buf.dtype),
        grid=(1,),
        in_specs=[smem()]
        + [whole()] * RUNS
        + [pl.BlockSpec(block, lambda i, at=first + at: (at, RUNS - 1, 0, 0, 0, 0)) for at in range(3)],
        out_specs=whole(),
        scratch_shapes=[pltpu.VMEM((RUNS, GROUP, LANES), jnp.float32)],
        compiler_params=small_kernel(),
        name="tail_message",
    )(me, *letters, buf, buf, buf)


def fold_frames(buf, tail_of, me, letters, chirp):
    twist = jnp.asarray(np.stack(twist_tables()))
    table = jnp.asarray(np.stack(lane_tables()))
    tail = tail_of(tail_message(me, letters, buf))
    params = pltpu.CompilerParams(vmem_limit_bytes=28 * 1024 * 1024)
    flops = 2 * 2 * 2 * 3 * ROWS * GROUP * 256 * 256
    later, ordered = pl.pallas_call(
        later_kernel,
        out_shape=[
            jax.ShapeDtypeStruct((ACC_ROWS, 4 * GROUP), jnp.float32),
            jax.ShapeDtypeStruct((RUNS, LETTER_ROWS, LANES), jnp.float32),
        ],
        in_specs=[smem()] + [whole()] * (RUNS + 4),
        out_specs=[whole()] * 2,
        scratch_shapes=[
            pltpu.VMEM((ROWS // 2, GROUP, LANES), jnp.float32),
            pltpu.VMEM((RUNS, KEPT, LANES), jnp.int32),
        ]
        + scratch(),
        compiler_params=params,
        cost_estimate=pl.CostEstimate(flops=3 * flops, bytes_accessed=30_000_000, transcendentals=0),
        name="later_frames",
    )(me, *letters, buf, chirp, twist, table)
    block = (MEMBERS, 1) + buf.shape[2:]
    return pl.pallas_call(
        first_kernel,
        out_shape=jax.ShapeDtypeStruct((NBIN // 16, 8, LANES), jnp.float32),
        grid=(1,),
        in_specs=[pl.BlockSpec(block, lambda i: (0,) * 6)] + [whole()] * 6,
        out_specs=whole(),
        scratch_shapes=[
            pltpu.VMEM((ACC_ROWS, 4 * GROUP), jnp.float32),
            pltpu.VMEM((ROWS // 2, GROUP, LANES), jnp.float32),
            pltpu.VMEM((1, KEPT, LANES), jnp.int32),
        ]
        + scratch(),
        compiler_params=params,
        cost_estimate=pl.CostEstimate(flops=flops, bytes_accessed=10_000_000, transcendentals=0),
        name="first_frame",
    )(buf, tail, ordered, chirp, twist, table, later)


def last_kernel(scale, shares_ref, out_ref):
    total = [jnp.sum(shares_ref[slab], axis=0) * scale for slab in range(RUNS)]
    for half in range(2):
        for s in range(4):
            lanes = slice(64 * half + GROUP * s, 64 * half + GROUP * (s + 1))
            out_ref[pl.ds(32 * half + s, 8, stride=4)] = jnp.concatenate([part[:, lanes] for part in total], axis=1)


def turned_to(block_for, axis, turn):
    size = lax.axis_size(axis)
    there = (lax.axis_index(axis) + turn) % size
    if turn == 0:
        return block_for(there)
    return lax.ppermute(block_for(there), axis, [(i, (i + turn) % size) for i in range(size)])


def from_before(block):
    size = lax.axis_size("xy")
    return lax.ppermute(block, "xy", [(i, i + 1) for i in range(size - 1)])


def chirp_table(sweep):
    k = jnp.arange(ROWS, dtype=jnp.int32)[:, None] + ROWS * jnp.arange(LANES, dtype=jnp.int32)[None, :]
    u = jnp.where(k < NFFT // 2, k, k - NFFT).astype(jnp.float32) / NFFT
    phase = (jnp.pi * sweep)[None, :, None] * (u * u + u)[:, None, :]
    table = jnp.stack([jnp.cos(phase), jnp.sin(phase)]) * (1.0 / NFFT)
    return table.reshape(2, ROWS * GROUP, LANES)


def on_device(samples, scales, flags, sweep, phase_bin):
    parts = pl.pallas_call(
        spread_kernel,
        out_shape=jax.ShapeDtypeStruct((MEMBERS * RUNS, 2, 2, GROUP, PIECE), samples.dtype),
        in_specs=[pl.BlockSpec(memory_space=pltpu.HBM)],
        out_specs=whole(),
        scratch_shapes=[pltpu.SemaphoreType.DMA((2, 2))],
        compiler_params=small_kernel(),
        name="spread",
    )(samples.reshape(2, 2, MEMBERS * RUNS, GROUP, PIECE))
    buf = lax.all_to_all(parts, ("chan", "zl"), split_axis=0, concat_axis=0, tiled=True)
    buf = buf.reshape(MEMBERS, RUNS, 2, 2, GROUP, PIECE)

    me = lax.axis_index("zl")
    weight = scales * (1 - flags).astype(jnp.float32)
    weight = jnp.pad(weight, ((0, 0), (0, LANES - BLOCKS)))
    bins = phase_bin.reshape(KEPT, LANES)
    base = bins[::2, 0] // 8 * 8
    marks = (bins - jnp.repeat(base, 2)[:, None]) % NBIN

    def weights_for(place):
        return lax.dynamic_slice_in_dim(weight, place * GROUP, GROUP, 0)

    base_rows = jnp.pad(base[None, :], ((0, LETTER_ROWS - BASE_ROW - 1), (0, LANES - BLOCKS)))
    below = jnp.concatenate([marks, base_rows]).astype(jnp.float32)
    letters = [
        turned_to(lambda place: jnp.concatenate([weights_for(place), below]), "zl", turn) for turn in range(RUNS)
    ]
    chirp = chirp_table(lax.dynamic_slice_in_dim(sweep, me * GROUP, GROUP, 0))

    partial = fold_frames(buf, from_before, me.reshape(1), letters, chirp)
    shares = lax.all_to_all(partial, ("zl", "xy"), split_axis=0, concat_axis=0, tiled=True)
    size = lax.axis_size("xy")
    return pl.pallas_call(
        functools.partial(last_kernel, NBIN / (SLAB * RUNS * size)),
        out_shape=jax.ShapeDtypeStruct((16 * 4, RUNS * GROUP), jnp.float32),
        compiler_params=small_kernel(),
        name="last_sum",
    )(shares.reshape(RUNS, size, 8, LANES)).reshape(16, 4, RUNS * GROUP)


def solution(mesh):
    inner = Mesh(mesh.devices.reshape(-1, RUNS, MEMBERS), ("xy", "zl", "chan"))
    time = ("xy", "zl")
    placed = (
        P(None, None, None, ("xy", "zl", "chan")),
        P("chan", time),
        P("chan", time),
        P("chan"),
        P(time),
    )
    return jax.shard_map(
        on_device, mesh=inner, in_specs=placed, out_specs=P(time, None, "chan"), check_vma=False
    )
```

```python
import functools
import math

import jax
import jax.numpy as jnp
import numpy as np
from jax import lax
from jax.experimental import pallas as pl
from jax.experimental.pallas import tpu as pltpu
from jax.sharding import Mesh, PartitionSpec as P

NFFT = 4096
OVER = 1024
BLK = 256
NBIN = 1024
LANES = 128
ROWS = NFFT // LANES
RIM = OVER // LANES
KEPT = ROWS - RIM
RUNS = 4
MEMBERS = 8
PIECE = 384
SLAB = MEMBERS * PIECE
GROUP = 16
BLOCKS = SLAB // BLK
WINDOW = 144
ACC_ROWS = NBIN + WINDOW
DOT_ROWS = 256
BASE_ROW = GROUP + KEPT
LETTER_ROWS = BASE_ROW + 8
HALF_ROOT = math.sqrt(0.5)


def lane_tables():
    angle = 2.0 * np.pi / LANES * (np.arange(LANES)[:, None] * np.arange(LANES)[None, :] % LANES)
    cos, sin = np.cos(angle), np.sin(angle)
    table = np.block([[cos, -sin], [sin, cos]]).astype(np.float32)
    high = table.astype(jnp.bfloat16)
    low = (table - high.astype(np.float32)).astype(jnp.bfloat16)
    return high, low


def twist_tables():
    angle = -2.0 * np.pi / NFFT * (np.arange(ROWS)[:, None] * np.arange(LANES)[None, :])
    return np.cos(angle).astype(np.float32), np.sin(angle).astype(np.float32)


def plus(a, b):
    return (a[0] + b[0], a[1] + b[1])


def minus(a, b):
    return (a[0] - b[0], a[1] - b[1])


def quarter(a, sign):
    return (a[1], -a[0]) if sign < 0 else (-a[1], a[0])


def dft4(x, sign):
    t0, t1 = plus(x[0], x[2]), minus(x[0], x[2])
    t2, t3 = plus(x[1], x[3]), quarter(minus(x[1], x[3]), sign)
    return [plus(t0, t2), plus(t1, t3), minus(t0, t2), minus(t1, t3)]


def dft8(x, sign):
    even = dft4(x[0::2], sign)
    odd = dft4(x[1::2], sign)
    re, im = odd[1]
    if sign < 0:
        odd[1] = ((re + im) * HALF_ROOT, (im - re) * HALF_ROOT)
    else:
        odd[1] = ((re - im) * HALF_ROOT, (im + re) * HALF_ROOT)
    odd[2] = quarter(odd[2], sign)
    re, im = odd[3]
    if sign < 0:
        odd[3] = ((im - re) * HALF_ROOT, (re + im) * -HALF_ROOT)
    else:
        odd[3] = ((re + im) * -HALF_ROOT, (re - im) * HALF_ROOT)
    return [plus(e, o) for e, o in zip(even, odd)] + [minus(e, o) for e, o in zip(even, odd)]


def turned(a, step, sign):
    step %= 32
    if step == 0:
        return a
    if step == 8:
        return quarter(a, sign)
    re, im = a
    if step == 4:
        if sign < 0:
            return ((re + im) * HALF_ROOT, (im - re) * HALF_ROOT)
        return ((re - im) * HALF_ROOT, (im + re) * HALF_ROOT)
    cos = math.cos(2.0 * math.pi * step / 32)
    sin = sign * math.sin(2.0 * math.pi * step / 32)
    return (re * cos - im * sin, re * sin + im * cos)


def split(values):
    high = values.astype(jnp.bfloat16)
    return high, (values - high.astype(jnp.float32)).astype(jnp.bfloat16)


def lane_dft(high, low, table_high, table_low):
    dot = functools.partial(jnp.dot, preferred_element_type=jnp.float32)
    return dot(high, table_high) + (dot(low, table_high) + dot(high, table_low))


def frame_profile(
    row_of, weight_of, base_of, marks_of, chirp_ref, twist_ref, table_ref, mid, y_refs, s_refs, stokes_ref, acc
):
    def rows_in(pol, b):
        rows = []
        for a in range(8):
            row = 4 * a + b
            gain = weight_of(row // 2)
            rows.append(tuple(row_of(row, pol, part).astype(jnp.float32) * gain for part in range(2)))
        for ka, value in enumerate(dft8(rows, -1)):
            value = turned(value, b * ka, -1)
            mid[pol, 0, b, ka] = value[0]
            mid[pol, 1, b, ka] = value[1]

    def rows_across(pol, ka):
        values = dft4([(mid[pol, 0, b, ka], mid[pol, 1, b, ka]) for b in range(4)], -1)
        for kb in range(4):
            k = ka + 8 * kb
            re, im = values[kb]
            if k:
                cos, sin = twist_ref[0, k : k + 1], twist_ref[1, k : k + 1]
                re, im = re * cos - im * sin, re * sin + im * cos
            for part, value in enumerate((re, im)):
                high, low = split(value)
                where = (pl.ds(GROUP * k, GROUP), pl.ds(LANES * part, LANES))
                y_refs[pol, 0, *where] = high
                y_refs[pol, 1, *where] = low

    def lanes(pol, m):
        rows = pl.ds(DOT_ROWS * m, DOT_ROWS)
        s_refs[pol, rows] = lane_dft(y_refs[pol, 0, rows], y_refs[pol, 1, rows], table_ref[0], table_ref[1])

    def filtered(pol, k):
        rows = pl.ds(GROUP * k, GROUP)
        re, im = s_refs[pol, rows, :LANES], s_refs[pol, rows, LANES:]
        cos, sin = chirp_ref[0, rows], chirp_ref[1, rows]
        for part, value in enumerate((re * sin + im * cos, re * cos - im * sin)):
            high, low = split(value)
            where = (rows, pl.ds(LANES * part, LANES))
            y_refs[pol, 0, *where] = high
            y_refs[pol, 1, *where] = low

    def untwisted(pol, k):
        rows = pl.ds(GROUP * k, GROUP)
        im, re = s_refs[pol, rows, :LANES], s_refs[pol, rows, LANES:]
        if k == 0:
            return re, im
        cos, sin = twist_ref[0, k : k + 1], twist_ref[1, k : k + 1]
        return re * cos + im * sin, im * cos - re * sin

    def rows_back(pol, b):
        values = dft8([untwisted(pol, 4 * a + b) for a in range(8)], 1)
        for na, value in enumerate(values):
            value = turned(value, b * na, 1)
            mid[pol, 0, b, na] = value[0]
            mid[pol, 1, b, na] = value[1]

    def rows_out(na):
        x, y = (
            dft4([(mid[pol, 0, b, na], mid[pol, 1, b, na]) for b in range(4)], 1) for pol in range(2)
        )
        for nb in range(1, 4):
            (xr, xi), (yr, yi) = x[nb], y[nb]
            power_x = xr * xr + xi * xi
            power_y = yr * yr + yi * yi
            cross_re = xr * yr + xi * yi
            cross_im = xi * yr - xr * yi
            row = na + 8 * (nb - 1)
            lanes = pl.ds(LANES * (row % 2), LANES)
            for s, value in enumerate((power_x + power_y, power_x - power_y, 2.0 * cross_re, 2.0 * cross_im)):
                stokes_ref[row // 2, pl.ds(GROUP * s, GROUP), lanes] = value.astype(jnp.bfloat16)

    bins = lax.broadcasted_iota(jnp.int32, (WINDOW, BLK), 0).astype(jnp.bfloat16)

    def fold(m):
        onehot = jnp.where(bins == marks_of(m).astype(jnp.bfloat16), jnp.bfloat16(1), jnp.bfloat16(0))
        part = lax.dot_general(
            onehot, stokes_ref[m], (((1,), (1,)), ((), ())), preferred_element_type=jnp.float32
        )
        place = pl.ds(pl.multiple_of(base_of(m), 8), WINDOW)
        acc[place] += part

    spans = ROWS * GROUP // DOT_ROWS
    for b in range(4):
        rows_in(0, b)
    for ka in range(8):
        rows_across(0, ka)
    for m in range(spans):
        lanes(0, m)
    for b in range(4):
        rows_in(1, b)
    for ka in range(8):
        rows_across(1, ka)
    for k in range(ROWS):
        filtered(0, k)
    for m in range(spans):
        lanes(1, m)
    for m in range(spans):
        lanes(0, m)
    for k in range(ROWS):
        filtered(1, k)
    for b in range(4):
        rows_back(0, b)
    for m in range(spans):
        lanes(1, m)
    for b in range(4):
        rows_back(1, b)
    for na in range(8):
        rows_out(na)
        if na % 2:
            for m in range(na // 2, BLOCKS, 4):
                fold(m)


def own_row(buf_ref, slab, row, pol, part):
    return buf_ref[row // 3, slab, pol, part, :, pl.ds(LANES * (row % 3), LANES)]


def lay_gains(gains, weights_of):
    for block in range(ROWS // 2):
        gains[block] = jnp.broadcast_to(weights_of(block), (GROUP, LANES))


def marks_from(marks_ref, index, m):
    return jnp.concatenate([marks_ref[index, 2 * m : 2 * m + 1], marks_ref[index, 2 * m + 1 : 2 * m + 2]], axis=1)


def later_kernel(me_ref, *refs):
    letter_refs, refs = refs[:RUNS], refs[RUNS:]
    buf_ref, chirp_ref, twist_ref, table_ref, acc_ref, sorted_ref, gains, marks, *scratches = refs
    me = me_ref[0]
    for turn in range(RUNS):
        sorted_ref[(me - turn + RUNS) % RUNS] = letter_refs[turn][...]
    marks[...] = sorted_ref[:, GROUP : GROUP + KEPT].astype(jnp.int32)
    acc_ref[...] = jnp.zeros_like(acc_ref)

    def step(frame, carry):
        def row_of(row, pol, part):
            if row < RIM:
                return own_row(buf_ref, frame - 1, row + KEPT - RIM, pol, part)
            return own_row(buf_ref, frame, row - RIM, pol, part)

        before, own = sorted_ref[frame - 1, :GROUP], sorted_ref[frame, :GROUP]

        def weights_of(block):
            if block < RIM // 2:
                return before[:, block + BLOCKS - RIM // 2 : block + BLOCKS - RIM // 2 + 1]
            return own[:, block - RIM // 2 : block - RIM // 2 + 1]

        lay_gains(gains, weights_of)
        bases = sorted_ref[frame, BASE_ROW : BASE_ROW + 1].astype(jnp.int32)
        frame_profile(
            row_of,
            lambda block: gains[block],
            lambda m: bases[0, m],
            lambda m: marks_from(marks, frame, m),
            chirp_ref,
            twist_ref,
            table_ref,
            *scratches,
            acc_ref,
        )
        return carry

    lax.fori_loop(1, RUNS, step, 0)


def first_kernel(
    buf_ref, tail_ref, sorted_ref, chirp_ref, twist_ref, table_ref, given_ref, out_ref, acc, gains, marks, *scratches
):
    acc[...] = given_ref[...]
    high, middle, low = (tail_ref[0, 0, part // 2, part % 2, :, :LANES].astype(jnp.float32) for part in range(3))
    before = (high + middle) + low
    own = sorted_ref[0, :GROUP]
    marks[0] = sorted_ref[0, GROUP : GROUP + KEPT].astype(jnp.int32)

    def weights_of(block):
        if block < RIM // 2:
            return before[:, block + BLOCKS - RIM // 2 : block + BLOCKS - RIM // 2 + 1]
        return own[:, block - RIM // 2 : block - RIM // 2 + 1]

    def row_of(row, pol, part):
        if row < RIM:
            return own_row(tail_ref, 0, row + 1, pol, part)
        return own_row(buf_ref, 0, row - RIM, pol, part)

    lay_gains(gains, weights_of)
    bases = sorted_ref[0, BASE_ROW : BASE_ROW + 1].astype(jnp.int32)
    frame_profile(
        row_of,
        lambda block: gains[block],
        lambda m: bases[0, m],
        lambda m: marks_from(marks, 0, m),
        chirp_ref,
        twist_ref,
        table_ref,
        *scratches,
        acc,
    )
    acc[:WINDOW] += acc[NBIN:]
    for share in range(NBIN // 16):
        place = share % RUNS * (NBIN // 16 // RUNS) + share // RUNS
        out_ref[place] = jnp.concatenate([acc[16 * share : 16 * share + 8], acc[16 * share + 8 : 16 * share + 16]], axis=1).astype(
            out_ref.dtype
        )


def tail_kernel(me_ref, *refs):
    letter_refs, piece_refs, out_ref, sorted_ref = refs[:RUNS], refs[RUNS:-2], refs[-2], refs[-1]
    me = me_ref[0]
    for turn in range(RUNS):
        sorted_ref[(me - turn + RUNS) % RUNS] = letter_refs[turn][:GROUP]
    rest = sorted_ref[RUNS - 1]
    for index, piece in enumerate(piece_refs):
        out_ref[index] = piece[0]
    for part in range(3):
        rounded = rest.astype(jnp.bfloat16)
        out_ref[0, 0, part // 2, part % 2, :, :LANES] = rounded
        rest = rest - rounded.astype(jnp.float32)


def spread_kernel(samples_ref, out_ref, held, in_sems, out_sems):
    places = [(pol, part) for pol in range(2) for part in range(2)]
    arriving = [pltpu.make_async_copy(samples_ref.at[at], held.at[at], in_sems.at[at]) for at in places]
    leaving = [pltpu.make_async_copy(held.at[at], out_ref.at[:, at[0], at[1]], out_sems.at[at]) for at in places]
    for copy in arriving:
        copy.start()
    for came, copy in zip(arriving, leaving):
        came.wait()
        copy.start()
    for copy in leaving:
        copy.wait()


def scratch():
    return [
        pltpu.VMEM((2, 2, 4, 8, GROUP, LANES), jnp.float32),
        pltpu.VMEM((2, 2, ROWS * GROUP, 2 * LANES), jnp.bfloat16),
        pltpu.VMEM((2, ROWS * GROUP, 2 * LANES), jnp.float32),
        pltpu.VMEM((BLOCKS, 4 * GROUP, BLK), jnp.bfloat16),
    ]


def whole():
    return pl.BlockSpec(memory_space=pltpu.VMEM)


def small_kernel():
    return pltpu.CompilerParams(vmem_limit_bytes=4 * 1024 * 1024)


def smem():
    return pl.BlockSpec(memory_space=pltpu.SMEM)


def tail_message(me, letters, buf):
    block = (1, 1) + buf.shape[2:]
    first = MEMBERS - 3
    return pl.pallas_call(
        tail_kernel,
        out_shape=jax.ShapeDtypeStruct((3, 1) + buf.shape[2:], buf.dtype),
        grid=(1,),
        in_specs=[smem()]
        + [whole()] * RUNS
        + [pl.BlockSpec(block, lambda i, at=first + at: (at, RUNS - 1, 0, 0, 0, 0)) for at in range(3)],
        out_specs=whole(),
        scratch_shapes=[pltpu.VMEM((RUNS, GROUP, LANES), jnp.float32)],
        compiler_params=small_kernel(),
        name="tail_message",
    )(me, *letters, buf, buf, buf)


def fold_frames(buf, tail_of, me, letters, chirp):
    twist = jnp.asarray(np.stack(twist_tables()))
    table = jnp.asarray(np.stack(lane_tables()))
    tail = tail_of(tail_message(me, letters, buf))
    params = pltpu.CompilerParams(vmem_limit_bytes=28 * 1024 * 1024)
    flops = 2 * 2 * 2 * 3 * ROWS * GROUP * 256 * 256
    later, ordered = pl.pallas_call(
        later_kernel,
        out_shape=[
            jax.ShapeDtypeStruct((ACC_ROWS, 4 * GROUP), jnp.float32),
            jax.ShapeDtypeStruct((RUNS, LETTER_ROWS, LANES), jnp.float32),
        ],
        in_specs=[smem()] + [whole()] * (RUNS + 4),
        out_specs=[whole()] * 2,
        scratch_shapes=[
            pltpu.VMEM((ROWS // 2, GROUP, LANES), jnp.float32),
            pltpu.VMEM((RUNS, KEPT, LANES), jnp.int32),
        ]
        + scratch(),
        compiler_params=params,
        cost_estimate=pl.CostEstimate(flops=3 * flops, bytes_accessed=30_000_000, transcendentals=0),
        name="later_frames",
    )(me, *letters, buf, chirp, twist, table)
    block = (MEMBERS, 1) + buf.shape[2:]
    return pl.pallas_call(
        first_kernel,
        out_shape=jax.ShapeDtypeStruct((NBIN // 16, 8, LANES), jnp.bfloat16),
        grid=(1,),
        in_specs=[pl.BlockSpec(block, lambda i: (0,) * 6)] + [whole()] * 6,
        out_specs=whole(),
        scratch_shapes=[
            pltpu.VMEM((ACC_ROWS, 4 * GROUP), jnp.float32),
            pltpu.VMEM((ROWS // 2, GROUP, LANES), jnp.float32),
            pltpu.VMEM((1, KEPT, LANES), jnp.int32),
        ]
        + scratch(),
        compiler_params=params,
        cost_estimate=pl.CostEstimate(flops=flops, bytes_accessed=10_000_000, transcendentals=0),
        name="first_frame",
    )(buf, tail, ordered, chirp, twist, table, later)


def last_kernel(scale, shares_ref, out_ref):
    total = [jnp.sum(shares_ref[slab].astype(jnp.float32), axis=0) * scale for slab in range(RUNS)]
    for half in range(2):
        for s in range(4):
            lanes = slice(64 * half + GROUP * s, 64 * half + GROUP * (s + 1))
            out_ref[pl.ds(32 * half + s, 8, stride=4)] = jnp.concatenate([part[:, lanes] for part in total], axis=1)


def turned_to(block_for, axis, turn):
    size = lax.axis_size(axis)
    there = (lax.axis_index(axis) + turn) % size
    if turn == 0:
        return block_for(there)
    return lax.ppermute(block_for(there), axis, [(i, (i + turn) % size) for i in range(size)])


def from_before(block):
    size = lax.axis_size("xy")
    return lax.ppermute(block, "xy", [(i, i + 1) for i in range(size - 1)])


def chirp_table(sweep):
    k = jnp.arange(ROWS, dtype=jnp.int32)[:, None] + ROWS * jnp.arange(LANES, dtype=jnp.int32)[None, :]
    u = jnp.where(k < NFFT // 2, k, k - NFFT).astype(jnp.float32) / NFFT
    phase = (jnp.pi * sweep)[None, :, None] * (u * u + u)[:, None, :]
    table = jnp.stack([jnp.cos(phase), jnp.sin(phase)]) * (1.0 / NFFT)
    return table.reshape(2, ROWS * GROUP, LANES)


def on_device(samples, scales, flags, sweep, phase_bin):
    parts = pl.pallas_call(
        spread_kernel,
        out_shape=jax.ShapeDtypeStruct((MEMBERS * RUNS, 2, 2, GROUP, PIECE), samples.dtype),
        in_specs=[pl.BlockSpec(memory_space=pltpu.HBM)],
        out_specs=pl.BlockSpec(memory_space=pltpu.HBM),
        scratch_shapes=[
            pltpu.VMEM((2, 2, MEMBERS * RUNS, GROUP, PIECE), samples.dtype),
            pltpu.SemaphoreType.DMA((2, 2)),
            pltpu.SemaphoreType.DMA((2, 2)),
        ],
        compiler_params=pltpu.CompilerParams(vmem_limit_bytes=60 * 1024 * 1024),
        name="spread",
    )(samples.reshape(2, 2, MEMBERS * RUNS, GROUP, PIECE))
    buf = lax.all_to_all(parts, ("chan", "zl"), split_axis=0, concat_axis=0, tiled=True)
    buf = buf.reshape(MEMBERS, RUNS, 2, 2, GROUP, PIECE)

    me = lax.axis_index("zl")
    weight = scales * (1 - flags).astype(jnp.float32)
    weight = jnp.pad(weight, ((0, 0), (0, LANES - BLOCKS)))
    bins = phase_bin.reshape(KEPT, LANES)
    base = bins[::2, 0] // 8 * 8
    marks = (bins - jnp.repeat(base, 2)[:, None]) % NBIN

    def weights_for(place):
        return lax.dynamic_slice_in_dim(weight, place * GROUP, GROUP, 0)

    base_rows = jnp.pad(base[None, :], ((0, LETTER_ROWS - BASE_ROW - 1), (0, LANES - BLOCKS)))
    below = jnp.concatenate([marks, base_rows]).astype(jnp.float32)
    letters = [
        turned_to(lambda place: jnp.concatenate([weights_for(place), below]), "zl", turn) for turn in range(RUNS)
    ]
    chirp = chirp_table(lax.dynamic_slice_in_dim(sweep, me * GROUP, GROUP, 0))

    partial = fold_frames(buf, from_before, me.reshape(1), letters, chirp)
    shares = lax.all_to_all(partial, ("zl", "xy"), split_axis=0, concat_axis=0, tiled=True)
    size = lax.axis_size("xy")
    return pl.pallas_call(
        functools.partial(last_kernel, NBIN / (SLAB * RUNS * size)),
        out_shape=jax.ShapeDtypeStruct((16 * 4, RUNS * GROUP), jnp.float32),
        compiler_params=small_kernel(),
        name="last_sum",
    )(shares.reshape(RUNS, size, 8, LANES)).reshape(16, 4, RUNS * GROUP)


def solution(mesh):
    inner = Mesh(mesh.devices.reshape(-1, RUNS, MEMBERS), ("xy", "zl", "chan"))
    time = ("xy", "zl")
    placed = (
        P(None, None, None, ("xy", "zl", "chan")),
        P("chan", time),
        P("chan", time),
        P("chan"),
        P(time),
    )
    return jax.shard_map(
        on_device, mesh=inner, in_specs=placed, out_specs=P(time, None, "chan"), check_vma=False
    )
```

```python
import functools
import math

import jax
import jax.numpy as jnp
import numpy as np
from jax import lax
from jax.experimental import pallas as pl
from jax.experimental.pallas import tpu as pltpu
from jax.sharding import Mesh, PartitionSpec as P

NFFT = 4096
OVER = 1024
BLK = 256
NBIN = 1024
LANES = 128
ROWS = NFFT // LANES
RIM = OVER // LANES
KEPT = ROWS - RIM
RUNS = 4
MEMBERS = 8
PIECE = 384
SLAB = MEMBERS * PIECE
GROUP = 16
BLOCKS = SLAB // BLK
WINDOW = 144
ACC_ROWS = NBIN + WINDOW
DOT_ROWS = 256
BASE_ROW = GROUP + KEPT
LETTER_ROWS = BASE_ROW + 8
HALF_ROOT = math.sqrt(0.5)


def lane_tables():
    angle = 2.0 * np.pi / LANES * (np.arange(LANES)[:, None] * np.arange(LANES)[None, :] % LANES)
    cos, sin = np.cos(angle), np.sin(angle)
    table = np.block([[cos, -sin], [sin, cos]]).astype(np.float32)
    high = table.astype(jnp.bfloat16)
    low = (table - high.astype(np.float32)).astype(jnp.bfloat16)
    return high, low


def twist_tables():
    angle = -2.0 * np.pi / NFFT * (np.arange(ROWS)[:, None] * np.arange(LANES)[None, :])
    return np.cos(angle).astype(np.float32), np.sin(angle).astype(np.float32)


def plus(a, b):
    return (a[0] + b[0], a[1] + b[1])


def minus(a, b):
    return (a[0] - b[0], a[1] - b[1])


def quarter(a, sign):
    return (a[1], -a[0]) if sign < 0 else (-a[1], a[0])


def dft4(x, sign):
    t0, t1 = plus(x[0], x[2]), minus(x[0], x[2])
    t2, t3 = plus(x[1], x[3]), quarter(minus(x[1], x[3]), sign)
    return [plus(t0, t2), plus(t1, t3), minus(t0, t2), minus(t1, t3)]


def dft8(x, sign):
    even = dft4(x[0::2], sign)
    odd = dft4(x[1::2], sign)
    re, im = odd[1]
    if sign < 0:
        odd[1] = ((re + im) * HALF_ROOT, (im - re) * HALF_ROOT)
    else:
        odd[1] = ((re - im) * HALF_ROOT, (im + re) * HALF_ROOT)
    odd[2] = quarter(odd[2], sign)
    re, im = odd[3]
    if sign < 0:
        odd[3] = ((im - re) * HALF_ROOT, (re + im) * -HALF_ROOT)
    else:
        odd[3] = ((re + im) * -HALF_ROOT, (re - im) * HALF_ROOT)
    return [plus(e, o) for e, o in zip(even, odd)] + [minus(e, o) for e, o in zip(even, odd)]


def turned(a, step, sign):
    step %= 32
    if step == 0:
        return a
    if step == 8:
        return quarter(a, sign)
    re, im = a
    if step == 4:
        if sign < 0:
            return ((re + im) * HALF_ROOT, (im - re) * HALF_ROOT)
        return ((re - im) * HALF_ROOT, (im + re) * HALF_ROOT)
    cos = math.cos(2.0 * math.pi * step / 32)
    sin = sign * math.sin(2.0 * math.pi * step / 32)
    return (re * cos - im * sin, re * sin + im * cos)


def split(values):
    high = values.astype(jnp.bfloat16)
    return high, (values - high.astype(jnp.float32)).astype(jnp.bfloat16)


def lane_dft(high, low, table_high, table_low):
    dot = functools.partial(jnp.dot, preferred_element_type=jnp.float32)
    return dot(high, table_high) + (dot(low, table_high) + dot(high, table_low))


def frame_profile(
    row_of, weight_of, base_of, marks_of, chirp_ref, twist_ref, table_ref, mid, y_refs, s_refs, stokes_ref, acc
):
    def rows_in(pol, b):
        rows = []
        for a in range(8):
            row = 4 * a + b
            gain = weight_of(row // 2)
            rows.append(tuple(row_of(row, pol, part).astype(jnp.float32) * gain for part in range(2)))
        for ka, value in enumerate(dft8(rows, -1)):
            value = turned(value, b * ka, -1)
            mid[pol, 0, b, ka] = value[0]
            mid[pol, 1, b, ka] = value[1]

    def rows_across(pol, ka):
        values = dft4([(mid[pol, 0, b, ka], mid[pol, 1, b, ka]) for b in range(4)], -1)
        for kb in range(4):
            k = ka + 8 * kb
            re, im = values[kb]
            if k:
                cos, sin = twist_ref[0, k : k + 1], twist_ref[1, k : k + 1]
                re, im = re * cos - im * sin, re * sin + im * cos
            for part, value in enumerate((re, im)):
                high, low = split(value)
                where = (pl.ds(GROUP * k, GROUP), pl.ds(LANES * part, LANES))
                y_refs[pol, 0, *where] = high
                y_refs[pol, 1, *where] = low

    def lanes(pol, m):
        rows = pl.ds(DOT_ROWS * m, DOT_ROWS)
        s_refs[pol, rows] = lane_dft(y_refs[pol, 0, rows], y_refs[pol, 1, rows], table_ref[0], table_ref[1])

    def filtered(pol, k):
        rows = pl.ds(GROUP * k, GROUP)
        re, im = s_refs[pol, rows, :LANES], s_refs[pol, rows, LANES:]
        cos, sin = chirp_ref[0, rows], chirp_ref[1, rows]
        for part, value in enumerate((re * sin + im * cos, re * cos - im * sin)):
            high, low = split(value)
            where = (rows, pl.ds(LANES * part, LANES))
            y_refs[pol, 0, *where] = high
            y_refs[pol, 1, *where] = low

    def untwisted(pol, k):
        rows = pl.ds(GROUP * k, GROUP)
        im, re = s_refs[pol, rows, :LANES], s_refs[pol, rows, LANES:]
        if k == 0:
            return re, im
        cos, sin = twist_ref[0, k : k + 1], twist_ref[1, k : k + 1]
        return re * cos + im * sin, im * cos - re * sin

    def rows_back(pol, b):
        values = dft8([untwisted(pol, 4 * a + b) for a in range(8)], 1)
        for na, value in enumerate(values):
            value = turned(value, b * na, 1)
            mid[pol, 0, b, na] = value[0]
            mid[pol, 1, b, na] = value[1]

    def rows_out(na):
        x, y = (
            dft4([(mid[pol, 0, b, na], mid[pol, 1, b, na]) for b in range(4)], 1) for pol in range(2)
        )
        for nb in range(1, 4):
            (xr, xi), (yr, yi) = x[nb], y[nb]
            power_x = xr * xr + xi * xi
            power_y = yr * yr + yi * yi
            cross_re = xr * yr + xi * yi
            cross_im = xi * yr - xr * yi
            row = na + 8 * (nb - 1)
            lanes = pl.ds(LANES * (row % 2), LANES)
            for s, value in enumerate((power_x + power_y, power_x - power_y, cross_re, cross_im)):
                stokes_ref[row // 2, pl.ds(GROUP * s, GROUP), lanes] = value.astype(jnp.bfloat16)

    bins = lax.broadcasted_iota(jnp.int32, (WINDOW, BLK), 0).astype(jnp.bfloat16)

    def fold(m):
        onehot = jnp.where(bins == marks_of(m).astype(jnp.bfloat16), jnp.bfloat16(1), jnp.bfloat16(0))
        part = lax.dot_general(
            onehot, stokes_ref[m], (((1,), (1,)), ((), ())), preferred_element_type=jnp.float32
        )
        place = pl.ds(pl.multiple_of(base_of(m), 8), WINDOW)
        acc[place] += part

    spans = ROWS * GROUP // DOT_ROWS
    for b in range(4):
        rows_in(0, b)
    for ka in range(8):
        rows_across(0, ka)
    for m in range(spans):
        lanes(0, m)
    for b in range(4):
        rows_in(1, b)
    for ka in range(8):
        rows_across(1, ka)
    for k in range(ROWS):
        filtered(0, k)
    for m in range(spans):
        lanes(1, m)
    for m in range(spans):
        lanes(0, m)
    for k in range(ROWS):
        filtered(1, k)
    for b in range(4):
        rows_back(0, b)
    for m in range(spans):
        lanes(1, m)
    for b in range(4):
        rows_back(1, b)
    for na in range(8):
        rows_out(na)
        if na % 2:
            for m in range(na // 2, BLOCKS, 4):
                fold(m)


def own_row(buf_ref, slab, row, pol, part):
    return buf_ref[row // 3, slab, pol, part, :, pl.ds(LANES * (row % 3), LANES)]


def lay_gains(gains, weights_of):
    for block in range(ROWS // 2):
        gains[block] = jnp.broadcast_to(weights_of(block), (GROUP, LANES))


def marks_from(marks_ref, index, m):
    return jnp.concatenate([marks_ref[index, 2 * m : 2 * m + 1], marks_ref[index, 2 * m + 1 : 2 * m + 2]], axis=1)


def later_kernel(me_ref, *refs):
    letter_refs, refs = refs[:RUNS], refs[RUNS:]
    buf_ref, chirp_ref, twist_ref, table_ref, acc_ref, sorted_ref, gains, marks, *scratches = refs
    me = me_ref[0]
    for turn in range(RUNS):
        sorted_ref[(me - turn + RUNS) % RUNS] = letter_refs[turn][...]
    marks[...] = sorted_ref[:, GROUP : GROUP + KEPT].astype(jnp.int32)
    acc_ref[...] = jnp.zeros_like(acc_ref)

    def step(frame, carry):
        def row_of(row, pol, part):
            if row < RIM:
                return own_row(buf_ref, frame - 1, row + KEPT - RIM, pol, part)
            return own_row(buf_ref, frame, row - RIM, pol, part)

        before, own = sorted_ref[frame - 1, :GROUP], sorted_ref[frame, :GROUP]

        def weights_of(block):
            if block < RIM // 2:
                return before[:, block + BLOCKS - RIM // 2 : block + BLOCKS - RIM // 2 + 1]
            return own[:, block - RIM // 2 : block - RIM // 2 + 1]

        lay_gains(gains, weights_of)
        bases = sorted_ref[frame, BASE_ROW : BASE_ROW + 1].astype(jnp.int32)
        frame_profile(
            row_of,
            lambda block: gains[block],
            lambda m: bases[0, m],
            lambda m: marks_from(marks, frame, m),
            chirp_ref,
            twist_ref,
            table_ref,
            *scratches,
            acc_ref,
        )
        return carry

    lax.fori_loop(1, RUNS, step, 0)


def first_kernel(
    buf_ref, tail_ref, sorted_ref, chirp_ref, twist_ref, table_ref, given_ref, out_ref, acc, gains, marks, *scratches
):
    acc[...] = given_ref[...]
    high, middle, low = (tail_ref[0, 0, part // 2, part % 2, :, :LANES].astype(jnp.float32) for part in range(3))
    before = (high + middle) + low
    own = sorted_ref[0, :GROUP]
    marks[0] = sorted_ref[0, GROUP : GROUP + KEPT].astype(jnp.int32)

    def weights_of(block):
        if block < RIM // 2:
            return before[:, block + BLOCKS - RIM // 2 : block + BLOCKS - RIM // 2 + 1]
        return own[:, block - RIM // 2 : block - RIM // 2 + 1]

    def row_of(row, pol, part):
        if row < RIM:
            return own_row(tail_ref, 0, row + 1, pol, part)
        return own_row(buf_ref, 0, row - RIM, pol, part)

    lay_gains(gains, weights_of)
    bases = sorted_ref[0, BASE_ROW : BASE_ROW + 1].astype(jnp.int32)
    frame_profile(
        row_of,
        lambda block: gains[block],
        lambda m: bases[0, m],
        lambda m: marks_from(marks, 0, m),
        chirp_ref,
        twist_ref,
        table_ref,
        *scratches,
        acc,
    )
    acc[:WINDOW] += acc[NBIN:]
    for share in range(NBIN // 16):
        place = share % RUNS * (NBIN // 16 // RUNS) + share // RUNS
        out_ref[place] = jnp.concatenate([acc[16 * share : 16 * share + 8], acc[16 * share + 8 : 16 * share + 16]], axis=1)


def tail_kernel(me_ref, *refs):
    letter_refs, piece_refs, out_ref, sorted_ref = refs[:RUNS], refs[RUNS:-2], refs[-2], refs[-1]
    me = me_ref[0]
    for turn in range(RUNS):
        sorted_ref[(me - turn + RUNS) % RUNS] = letter_refs[turn][:GROUP]
    rest = sorted_ref[RUNS - 1]
    for index, piece in enumerate(piece_refs):
        out_ref[index] = piece[0]
    for part in range(3):
        rounded = rest.astype(jnp.bfloat16)
        out_ref[0, 0, part // 2, part % 2, :, :LANES] = rounded
        rest = rest - rounded.astype(jnp.float32)


def spread_kernel(samples_ref, out_ref, held, in_sems, out_sems):
    places = [(pol, part) for pol in range(2) for part in range(2)]
    arriving = [pltpu.make_async_copy(samples_ref.at[at], held.at[at], in_sems.at[at]) for at in places]
    leaving = [pltpu.make_async_copy(held.at[at], out_ref.at[:, at[0], at[1]], out_sems.at[at]) for at in places]
    for copy in arriving:
        copy.start()
    for came, copy in zip(arriving, leaving):
        came.wait()
        copy.start()
    for copy in leaving:
        copy.wait()


def scratch():
    return [
        pltpu.VMEM((2, 2, 4, 8, GROUP, LANES), jnp.float32),
        pltpu.VMEM((2, 2, ROWS * GROUP, 2 * LANES), jnp.bfloat16),
        pltpu.VMEM((2, ROWS * GROUP, 2 * LANES), jnp.float32),
        pltpu.VMEM((BLOCKS, 4 * GROUP, BLK), jnp.bfloat16),
    ]


def whole():
    return pl.BlockSpec(memory_space=pltpu.VMEM)


def small_kernel():
    return pltpu.CompilerParams(vmem_limit_bytes=4 * 1024 * 1024)


def smem():
    return pl.BlockSpec(memory_space=pltpu.SMEM)


def tail_message(me, letters, buf):
    block = (1, 1) + buf.shape[2:]
    first = MEMBERS - 3
    return pl.pallas_call(
        tail_kernel,
        out_shape=jax.ShapeDtypeStruct((3, 1) + buf.shape[2:], buf.dtype),
        grid=(1,),
        in_specs=[smem()]
        + [whole()] * RUNS
        + [pl.BlockSpec(block, lambda i, at=first + at: (at, RUNS - 1, 0, 0, 0, 0)) for at in range(3)],
        out_specs=whole(),
        scratch_shapes=[pltpu.VMEM((RUNS, GROUP, LANES), jnp.float32)],
        compiler_params=small_kernel(),
        name="tail_message",
    )(me, *letters, buf, buf, buf)


def fold_frames(buf, tail_of, me, letters, chirp):
    twist = jnp.asarray(np.stack(twist_tables()))
    table = jnp.asarray(np.stack(lane_tables()))
    tail = tail_of(tail_message(me, letters, buf))
    params = pltpu.CompilerParams(vmem_limit_bytes=28 * 1024 * 1024)
    flops = 2 * 2 * 2 * 3 * ROWS * GROUP * 256 * 256
    later, ordered = pl.pallas_call(
        later_kernel,
        out_shape=[
            jax.ShapeDtypeStruct((ACC_ROWS, 4 * GROUP), jnp.float32),
            jax.ShapeDtypeStruct((RUNS, LETTER_ROWS, LANES), jnp.float32),
        ],
        in_specs=[smem()] + [whole()] * (RUNS + 4),
        out_specs=[whole()] * 2,
        scratch_shapes=[
            pltpu.VMEM((ROWS // 2, GROUP, LANES), jnp.float32),
            pltpu.VMEM((RUNS, KEPT, LANES), jnp.int32),
        ]
        + scratch(),
        compiler_params=params,
        cost_estimate=pl.CostEstimate(flops=3 * flops, bytes_accessed=30_000_000, transcendentals=0),
        name="later_frames",
    )(me, *letters, buf, chirp, twist, table)
    block = (MEMBERS, 1) + buf.shape[2:]
    return pl.pallas_call(
        first_kernel,
        out_shape=jax.ShapeDtypeStruct((NBIN // 16, 8, LANES), jnp.float32),
        grid=(1,),
        in_specs=[pl.BlockSpec(block, lambda i: (0,) * 6)] + [whole()] * 6,
        out_specs=whole(),
        scratch_shapes=[
            pltpu.VMEM((ACC_ROWS, 4 * GROUP), jnp.float32),
            pltpu.VMEM((ROWS // 2, GROUP, LANES), jnp.float32),
            pltpu.VMEM((1, KEPT, LANES), jnp.int32),
        ]
        + scratch(),
        compiler_params=params,
        cost_estimate=pl.CostEstimate(flops=flops, bytes_accessed=10_000_000, transcendentals=0),
        name="first_frame",
    )(buf, tail, ordered, chirp, twist, table, later)


def last_kernel(scale, shares_ref, out_ref):
    total = [jnp.sum(shares_ref[slab], axis=0) * scale for slab in range(RUNS)]
    for half in range(2):
        for s in range(4):
            lanes = slice(64 * half + GROUP * s, 64 * half + GROUP * (s + 1))
            row = jnp.concatenate([part[:, lanes] for part in total], axis=1)
            out_ref[pl.ds(32 * half + s, 8, stride=4)] = row if s < 2 else 2.0 * row


def turned_to(block_for, axis, turn):
    size = lax.axis_size(axis)
    there = (lax.axis_index(axis) + turn) % size
    if turn == 0:
        return block_for(there)
    return lax.ppermute(block_for(there), axis, [(i, (i + turn) % size) for i in range(size)])


def from_before(block):
    size = lax.axis_size("xy")
    return lax.ppermute(block, "xy", [(i, i + 1) for i in range(size - 1)])


def chirp_table(sweep):
    k = jnp.arange(ROWS, dtype=jnp.int32)[:, None] + ROWS * jnp.arange(LANES, dtype=jnp.int32)[None, :]
    u = jnp.where(k < NFFT // 2, k, k - NFFT).astype(jnp.float32) / NFFT
    phase = (jnp.pi * sweep)[None, :, None] * (u * u + u)[:, None, :]
    table = jnp.stack([jnp.cos(phase), jnp.sin(phase)]) * (1.0 / NFFT)
    return table.reshape(2, ROWS * GROUP, LANES)


def on_device(samples, scales, flags, sweep, phase_bin):
    parts = pl.pallas_call(
        spread_kernel,
        out_shape=jax.ShapeDtypeStruct((MEMBERS * RUNS, 2, 2, GROUP, PIECE), samples.dtype),
        in_specs=[pl.BlockSpec(memory_space=pltpu.HBM)],
        out_specs=pl.BlockSpec(memory_space=pltpu.HBM),
        scratch_shapes=[
            pltpu.VMEM((2, 2, MEMBERS * RUNS, GROUP, PIECE), samples.dtype),
            pltpu.SemaphoreType.DMA((2, 2)),
            pltpu.SemaphoreType.DMA((2, 2)),
        ],
        compiler_params=pltpu.CompilerParams(vmem_limit_bytes=60 * 1024 * 1024),
        name="spread",
    )(samples.reshape(2, 2, MEMBERS * RUNS, GROUP, PIECE))
    buf = lax.all_to_all(parts, ("chan", "zl"), split_axis=0, concat_axis=0, tiled=True)
    buf = buf.reshape(MEMBERS, RUNS, 2, 2, GROUP, PIECE)

    me = lax.axis_index("zl")
    weight = scales * (1 - flags).astype(jnp.float32)
    weight = jnp.pad(weight, ((0, 0), (0, LANES - BLOCKS)))
    bins = phase_bin.reshape(KEPT, LANES)
    base = bins[::2, 0] // 8 * 8
    marks = (bins - jnp.repeat(base, 2)[:, None]) % NBIN

    def weights_for(place):
        return lax.dynamic_slice_in_dim(weight, place * GROUP, GROUP, 0)

    base_rows = jnp.pad(base[None, :], ((0, LETTER_ROWS - BASE_ROW - 1), (0, LANES - BLOCKS)))
    below = jnp.concatenate([marks, base_rows]).astype(jnp.float32)
    letters = [
        turned_to(lambda place: jnp.concatenate([weights_for(place), below]), "zl", turn) for turn in range(RUNS)
    ]
    chirp = chirp_table(lax.dynamic_slice_in_dim(sweep, me * GROUP, GROUP, 0))

    partial = fold_frames(buf, from_before, me.reshape(1), letters, chirp)
    shares = lax.all_to_all(partial, ("zl", "xy"), split_axis=0, concat_axis=0, tiled=True)
    size = lax.axis_size("xy")
    return pl.pallas_call(
        functools.partial(last_kernel, NBIN / (SLAB * RUNS * size)),
        out_shape=jax.ShapeDtypeStruct((16 * 4, RUNS * GROUP), jnp.float32),
        compiler_params=small_kernel(),
        name="last_sum",
    )(shares.reshape(RUNS, size, 8, LANES)).reshape(16, 4, RUNS * GROUP)


def solution(mesh):
    inner = Mesh(mesh.devices.reshape(-1, RUNS, MEMBERS), ("xy", "zl", "chan"))
    time = ("xy", "zl")
    placed = (
        P(None, None, None, ("xy", "zl", "chan")),
        P("chan", time),
        P("chan", time),
        P("chan"),
        P(time),
    )
    return jax.shard_map(
        on_device, mesh=inner, in_specs=placed, out_specs=P(time, None, "chan"), check_vma=False
    )
```

```python
import functools
import math

import jax
import jax.numpy as jnp
import numpy as np
from jax import lax
from jax.experimental import pallas as pl
from jax.experimental.pallas import tpu as pltpu
from jax.sharding import Mesh, PartitionSpec as P

NFFT = 4096
OVER = 1024
BLK = 256
NBIN = 1024
LANES = 128
ROWS = NFFT // LANES
RIM = OVER // LANES
KEPT = ROWS - RIM
RUNS = 4
MEMBERS = 8
PIECE = 384
SLAB = MEMBERS * PIECE
GROUP = 16
BLOCKS = SLAB // BLK
WINDOW = 144
ACC_ROWS = NBIN + WINDOW
DOT_ROWS = 256
BASE_ROW = GROUP + KEPT
LETTER_ROWS = BASE_ROW + 8
PARTS_APART = 16
HALF_ROOT = math.sqrt(0.5)


def lane_tables():
    angle = 2.0 * np.pi / LANES * (np.arange(LANES)[:, None] * np.arange(LANES)[None, :] % LANES)
    cos, sin = np.cos(angle), np.sin(angle)
    table = np.block([[cos, -sin], [sin, cos]]).astype(np.float32)
    high = table.astype(jnp.bfloat16)
    low = (table - high.astype(np.float32)).astype(jnp.bfloat16)
    return high, low


def twist_tables():
    angle = -2.0 * np.pi / NFFT * (np.arange(ROWS)[:, None] * np.arange(LANES)[None, :])
    return np.cos(angle).astype(np.float32), np.sin(angle).astype(np.float32)


def plus(a, b):
    return (a[0] + b[0], a[1] + b[1])


def minus(a, b):
    return (a[0] - b[0], a[1] - b[1])


def quarter(a, sign):
    return (a[1], -a[0]) if sign < 0 else (-a[1], a[0])


def dft4(x, sign):
    t0, t1 = plus(x[0], x[2]), minus(x[0], x[2])
    t2, t3 = plus(x[1], x[3]), quarter(minus(x[1], x[3]), sign)
    return [plus(t0, t2), plus(t1, t3), minus(t0, t2), minus(t1, t3)]


def dft8(x, sign):
    even = dft4(x[0::2], sign)
    odd = dft4(x[1::2], sign)
    re, im = odd[1]
    if sign < 0:
        odd[1] = ((re + im) * HALF_ROOT, (im - re) * HALF_ROOT)
    else:
        odd[1] = ((re - im) * HALF_ROOT, (im + re) * HALF_ROOT)
    odd[2] = quarter(odd[2], sign)
    re, im = odd[3]
    if sign < 0:
        odd[3] = ((im - re) * HALF_ROOT, (re + im) * -HALF_ROOT)
    else:
        odd[3] = ((re + im) * -HALF_ROOT, (re - im) * HALF_ROOT)
    return [plus(e, o) for e, o in zip(even, odd)] + [minus(e, o) for e, o in zip(even, odd)]


def turned(a, step, sign):
    step %= 32
    if step == 0:
        return a
    if step == 8:
        return quarter(a, sign)
    re, im = a
    if step == 4:
        if sign < 0:
            return ((re + im) * HALF_ROOT, (im - re) * HALF_ROOT)
        return ((re - im) * HALF_ROOT, (im + re) * HALF_ROOT)
    cos = math.cos(2.0 * math.pi * step / 32)
    sin = sign * math.sin(2.0 * math.pi * step / 32)
    return (re * cos - im * sin, re * sin + im * cos)


def split(values):
    high = values.astype(jnp.bfloat16)
    return high, (values - high.astype(jnp.float32)).astype(jnp.bfloat16)


def lane_dft(high, low, table_high, table_low):
    dot = functools.partial(jnp.dot, preferred_element_type=jnp.float32)
    return dot(high, table_high) + (dot(low, table_high) + dot(high, table_low))


def frame_profile(
    row_of, weight_of, base_of, marks_of, chirp_ref, twist_ref, table_ref, mid, y_refs, s_refs, stokes_ref, acc
):
    def rows_in(pol, b):
        rows = []
        for a in range(8):
            row = 4 * a + b
            gain = weight_of(row // 2)
            rows.append(tuple(row_of(row, pol, part).astype(jnp.float32) * gain for part in range(2)))
        for ka, value in enumerate(dft8(rows, -1)):
            value = turned(value, b * ka, -1)
            mid[pol, 0, b, ka] = value[0]
            mid[pol, 1, b, ka] = value[1]

    def rows_across(pol, ka):
        values = dft4([(mid[pol, 0, b, ka], mid[pol, 1, b, ka]) for b in range(4)], -1)
        for kb in range(4):
            k = ka + 8 * kb
            re, im = values[kb]
            if k:
                cos, sin = twist_ref[0, k : k + 1], twist_ref[1, k : k + 1]
                re, im = re * cos - im * sin, re * sin + im * cos
            for part, value in enumerate((re, im)):
                high, low = split(value)
                where = (pl.ds(GROUP * k, GROUP), pl.ds(LANES * part, LANES))
                y_refs[pol, 0, *where] = high
                y_refs[pol, 1, *where] = low

    def lanes(pol, m):
        rows = pl.ds(DOT_ROWS * m, DOT_ROWS)
        s_refs[pol, rows] = lane_dft(y_refs[pol, 0, rows], y_refs[pol, 1, rows], table_ref[0], table_ref[1])

    def filtered(pol, k):
        rows = pl.ds(GROUP * k, GROUP)
        re, im = s_refs[pol, rows, :LANES], s_refs[pol, rows, LANES:]
        cos, sin = chirp_ref[0, rows], chirp_ref[1, rows]
        for part, value in enumerate((re * sin + im * cos, re * cos - im * sin)):
            high, low = split(value)
            where = (rows, pl.ds(LANES * part, LANES))
            y_refs[pol, 0, *where] = high
            y_refs[pol, 1, *where] = low

    def untwisted(pol, k):
        rows = pl.ds(GROUP * k, GROUP)
        im, re = s_refs[pol, rows, :LANES], s_refs[pol, rows, LANES:]
        if k == 0:
            return re, im
        cos, sin = twist_ref[0, k : k + 1], twist_ref[1, k : k + 1]
        return re * cos + im * sin, im * cos - re * sin

    def rows_back(pol, b):
        values = dft8([untwisted(pol, 4 * a + b) for a in range(8)], 1)
        for na, value in enumerate(values):
            value = turned(value, b * na, 1)
            mid[pol, 0, b, na] = value[0]
            mid[pol, 1, b, na] = value[1]

    def rows_out(na):
        x, y = (
            dft4([(mid[pol, 0, b, na], mid[pol, 1, b, na]) for b in range(4)], 1) for pol in range(2)
        )
        for nb in range(1, 4):
            (xr, xi), (yr, yi) = x[nb], y[nb]
            power_x = xr * xr + xi * xi
            power_y = yr * yr + yi * yi
            cross_re = xr * yr + xi * yi
            cross_im = xi * yr - xr * yi
            row = na + 8 * (nb - 1)
            lanes = pl.ds(LANES * (row % 2), LANES)
            for s, value in enumerate((power_x + power_y, power_x - power_y, cross_re, cross_im)):
                stokes_ref[row // 2, pl.ds(GROUP * s, GROUP), lanes] = value.astype(jnp.bfloat16)

    bins = lax.broadcasted_iota(jnp.int32, (WINDOW, BLK), 0).astype(jnp.bfloat16)

    def fold(m):
        onehot = jnp.where(bins == marks_of(m).astype(jnp.bfloat16), jnp.bfloat16(1), jnp.bfloat16(0))
        part = lax.dot_general(
            onehot, stokes_ref[m], (((1,), (1,)), ((), ())), preferred_element_type=jnp.float32
        )
        place = pl.ds(pl.multiple_of(base_of(m), 8), WINDOW)
        acc[place] += part

    spans = ROWS * GROUP // DOT_ROWS
    for b in range(4):
        rows_in(0, b)
    for ka in range(8):
        rows_across(0, ka)
    for m in range(spans):
        lanes(0, m)
    for b in range(4):
        rows_in(1, b)
    for ka in range(8):
        rows_across(1, ka)
    for k in range(ROWS):
        filtered(0, k)
    for m in range(spans):
        lanes(1, m)
    for m in range(spans):
        lanes(0, m)
    for k in range(ROWS):
        filtered(1, k)
    for b in range(4):
        rows_back(0, b)
    for m in range(spans):
        lanes(1, m)
    for b in range(4):
        rows_back(1, b)
    for na in range(8):
        rows_out(na)
        if na % 2:
            for m in range(na // 2, BLOCKS, 4):
                fold(m)


def own_row(buf_ref, slab, row, pol, part):
    return buf_ref[row // 3, slab, pol, part, :, pl.ds(LANES * (row % 3), LANES)]


def in_parts(weight):
    high = lax.reduce_precision(weight, 8, 7)
    middle = lax.reduce_precision(weight - high, 8, 7)
    parts = [high, middle, weight - high - middle]
    width = PARTS_APART - weight.shape[1]
    side_by_side = jnp.concatenate([jnp.pad(part, ((0, 0), (0, width))) for part in parts], axis=1)
    return jnp.pad(side_by_side, ((0, 0), (0, LANES - 3 * PARTS_APART))).astype(jnp.bfloat16)


def joined(rows):
    first, second, third = (rows[:, PARTS_APART * part : PARTS_APART * (part + 1)] for part in range(3))
    return (first + second) + third


def lay_gains(gains, weights_of):
    for block in range(ROWS // 2):
        gains[block] = jnp.broadcast_to(weights_of(block), (GROUP, LANES))


def marks_from(marks_ref, index, m):
    return jnp.concatenate([marks_ref[index, 2 * m : 2 * m + 1], marks_ref[index, 2 * m + 1 : 2 * m + 2]], axis=1)


def later_kernel(me_ref, *refs):
    letter_refs, refs = refs[:RUNS], refs[RUNS:]
    buf_ref, chirp_ref, twist_ref, table_ref, acc_ref, sorted_ref, gains, marks, *scratches = refs
    me = me_ref[0]
    for turn in range(RUNS):
        slab = (me - turn + RUNS) % RUNS
        sorted_ref[slab] = letter_refs[turn][...].astype(jnp.float32)
        sorted_ref[slab, :GROUP, :PARTS_APART] = joined(sorted_ref[slab, :GROUP])
    marks[...] = sorted_ref[:, GROUP : GROUP + KEPT].astype(jnp.int32)
    acc_ref[...] = jnp.zeros_like(acc_ref)

    def step(frame, carry):
        def row_of(row, pol, part):
            if row < RIM:
                return own_row(buf_ref, frame - 1, row + KEPT - RIM, pol, part)
            return own_row(buf_ref, frame, row - RIM, pol, part)

        before, own = sorted_ref[frame - 1, :GROUP], sorted_ref[frame, :GROUP]

        def weights_of(block):
            if block < RIM // 2:
                return before[:, block + BLOCKS - RIM // 2 : block + BLOCKS - RIM // 2 + 1]
            return own[:, block - RIM // 2 : block - RIM // 2 + 1]

        lay_gains(gains, weights_of)
        bases = 8 * sorted_ref[frame, BASE_ROW : BASE_ROW + 1].astype(jnp.int32)
        frame_profile(
            row_of,
            lambda block: gains[block],
            lambda m: bases[0, m],
            lambda m: marks_from(marks, frame, m),
            chirp_ref,
            twist_ref,
            table_ref,
            *scratches,
            acc_ref,
        )
        return carry

    lax.fori_loop(1, RUNS, step, 0)


def first_kernel(
    buf_ref, tail_ref, sorted_ref, chirp_ref, twist_ref, table_ref, given_ref, out_ref, acc, gains, marks, *scratches
):
    acc[...] = given_ref[...]
    before = joined(tail_ref[0, 0, 0, 0, :, :LANES].astype(jnp.float32))
    own = sorted_ref[0, :GROUP]
    marks[0] = sorted_ref[0, GROUP : GROUP + KEPT].astype(jnp.int32)

    def weights_of(block):
        if block < RIM // 2:
            return before[:, block + BLOCKS - RIM // 2 : block + BLOCKS - RIM // 2 + 1]
        return own[:, block - RIM // 2 : block - RIM // 2 + 1]

    def row_of(row, pol, part):
        if row < RIM:
            return own_row(tail_ref, 0, row + 1, pol, part)
        return own_row(buf_ref, 0, row - RIM, pol, part)

    lay_gains(gains, weights_of)
    bases = 8 * sorted_ref[0, BASE_ROW : BASE_ROW + 1].astype(jnp.int32)
    frame_profile(
        row_of,
        lambda block: gains[block],
        lambda m: bases[0, m],
        lambda m: marks_from(marks, 0, m),
        chirp_ref,
        twist_ref,
        table_ref,
        *scratches,
        acc,
    )
    acc[:WINDOW] += acc[NBIN:]
    for share in range(NBIN // 16):
        place = share % RUNS * (NBIN // 16 // RUNS) + share // RUNS
        out_ref[place] = jnp.concatenate([acc[16 * share : 16 * share + 8], acc[16 * share + 8 : 16 * share + 16]], axis=1)


def tail_kernel(me_ref, *refs):
    letter_refs, piece_refs, out_ref, sorted_ref = refs[:RUNS], refs[RUNS:-2], refs[-2], refs[-1]
    me = me_ref[0]
    for turn in range(RUNS):
        sorted_ref[(me - turn + RUNS) % RUNS] = letter_refs[turn][:GROUP]
    for index, piece in enumerate(piece_refs):
        out_ref[index] = piece[0]
    out_ref[0, 0, 0, 0, :, :LANES] = sorted_ref[RUNS - 1]


def spread_kernel(samples_ref, out_ref, held, in_sems, out_sems):
    places = [(pol, part) for pol in range(2) for part in range(2)]
    arriving = [pltpu.make_async_copy(samples_ref.at[at], held.at[at], in_sems.at[at]) for at in places]
    leaving = [pltpu.make_async_copy(held.at[at], out_ref.at[:, at[0], at[1]], out_sems.at[at]) for at in places]
    for copy in arriving:
        copy.start()
    for came, copy in zip(arriving, leaving):
        came.wait()
        copy.start()
    for copy in leaving:
        copy.wait()


def scratch():
    return [
        pltpu.VMEM((2, 2, 4, 8, GROUP, LANES), jnp.float32),
        pltpu.VMEM((2, 2, ROWS * GROUP, 2 * LANES), jnp.bfloat16),
        pltpu.VMEM((2, ROWS * GROUP, 2 * LANES), jnp.float32),
        pltpu.VMEM((BLOCKS, 4 * GROUP, BLK), jnp.bfloat16),
    ]


def whole():
    return pl.BlockSpec(memory_space=pltpu.VMEM)


def small_kernel():
    return pltpu.CompilerParams(vmem_limit_bytes=4 * 1024 * 1024)


def smem():
    return pl.BlockSpec(memory_space=pltpu.SMEM)


def tail_message(me, letters, buf):
    block = (1, 1) + buf.shape[2:]
    first = MEMBERS - 3
    return pl.pallas_call(
        tail_kernel,
        out_shape=jax.ShapeDtypeStruct((3, 1) + buf.shape[2:], buf.dtype),
        grid=(1,),
        in_specs=[smem()]
        + [whole()] * RUNS
        + [pl.BlockSpec(block, lambda i, at=first + at: (at, RUNS - 1, 0, 0, 0, 0)) for at in range(3)],
        out_specs=whole(),
        scratch_shapes=[pltpu.VMEM((RUNS, GROUP, LANES), jnp.bfloat16)],
        compiler_params=small_kernel(),
        name="tail_message",
    )(me, *letters, buf, buf, buf)


def fold_frames(buf, tail_of, me, letters, chirp):
    twist = jnp.asarray(np.stack(twist_tables()))
    table = jnp.asarray(np.stack(lane_tables()))
    tail = tail_of(tail_message(me, letters, buf))
    params = pltpu.CompilerParams(vmem_limit_bytes=28 * 1024 * 1024)
    flops = 2 * 2 * 2 * 3 * ROWS * GROUP * 256 * 256
    later, ordered = pl.pallas_call(
        later_kernel,
        out_shape=[
            jax.ShapeDtypeStruct((ACC_ROWS, 4 * GROUP), jnp.float32),
            jax.ShapeDtypeStruct((RUNS, LETTER_ROWS, LANES), jnp.float32),
        ],
        in_specs=[smem()] + [whole()] * (RUNS + 4),
        out_specs=[whole()] * 2,
        scratch_shapes=[
            pltpu.VMEM((ROWS // 2, GROUP, LANES), jnp.float32),
            pltpu.VMEM((RUNS, KEPT, LANES), jnp.int32),
        ]
        + scratch(),
        compiler_params=params,
        cost_estimate=pl.CostEstimate(flops=3 * flops, bytes_accessed=30_000_000, transcendentals=0),
        name="later_frames",
    )(me, *letters, buf, chirp, twist, table)
    block = (MEMBERS, 1) + buf.shape[2:]
    return pl.pallas_call(
        first_kernel,
        out_shape=jax.ShapeDtypeStruct((NBIN // 16, 8, LANES), jnp.float32),
        grid=(1,),
        in_specs=[pl.BlockSpec(block, lambda i: (0,) * 6)] + [whole()] * 6,
        out_specs=whole(),
        scratch_shapes=[
            pltpu.VMEM((ACC_ROWS, 4 * GROUP), jnp.float32),
            pltpu.VMEM((ROWS // 2, GROUP, LANES), jnp.float32),
            pltpu.VMEM((1, KEPT, LANES), jnp.int32),
        ]
        + scratch(),
        compiler_params=params,
        cost_estimate=pl.CostEstimate(flops=flops, bytes_accessed=10_000_000, transcendentals=0),
        name="first_frame",
    )(buf, tail, ordered, chirp, twist, table, later)


def last_kernel(scale, shares_ref, out_ref):
    total = [jnp.sum(shares_ref[slab], axis=0) * scale for slab in range(RUNS)]
    for half in range(2):
        for s in range(4):
            lanes = slice(64 * half + GROUP * s, 64 * half + GROUP * (s + 1))
            row = jnp.concatenate([part[:, lanes] for part in total], axis=1)
            out_ref[pl.ds(32 * half + s, 8, stride=4)] = row if s < 2 else 2.0 * row


def turned_to(block_for, axis, turn):
    size = lax.axis_size(axis)
    there = (lax.axis_index(axis) + turn) % size
    if turn == 0:
        return block_for(there)
    return lax.ppermute(block_for(there), axis, [(i, (i + turn) % size) for i in range(size)])


def from_before(block):
    size = lax.axis_size("xy")
    return lax.ppermute(block, "xy", [(i, i + 1) for i in range(size - 1)])


def chirp_table(sweep):
    k = jnp.arange(ROWS, dtype=jnp.int32)[:, None] + ROWS * jnp.arange(LANES, dtype=jnp.int32)[None, :]
    u = jnp.where(k < NFFT // 2, k, k - NFFT).astype(jnp.float32) / NFFT
    phase = (jnp.pi * sweep)[None, :, None] * (u * u + u)[:, None, :]
    table = jnp.stack([jnp.cos(phase), jnp.sin(phase)]) * (1.0 / NFFT)
    return table.reshape(2, ROWS * GROUP, LANES)


def on_device(samples, scales, flags, sweep, phase_bin):
    parts = pl.pallas_call(
        spread_kernel,
        out_shape=jax.ShapeDtypeStruct((MEMBERS * RUNS, 2, 2, GROUP, PIECE), samples.dtype),
        in_specs=[pl.BlockSpec(memory_space=pltpu.HBM)],
        out_specs=pl.BlockSpec(memory_space=pltpu.HBM),
        scratch_shapes=[
            pltpu.VMEM((2, 2, MEMBERS * RUNS, GROUP, PIECE), samples.dtype),
            pltpu.SemaphoreType.DMA((2, 2)),
            pltpu.SemaphoreType.DMA((2, 2)),
        ],
        compiler_params=pltpu.CompilerParams(vmem_limit_bytes=60 * 1024 * 1024),
        name="spread",
    )(samples.reshape(2, 2, MEMBERS * RUNS, GROUP, PIECE))
    buf = lax.all_to_all(parts, ("chan", "zl"), split_axis=0, concat_axis=0, tiled=True)
    buf = buf.reshape(MEMBERS, RUNS, 2, 2, GROUP, PIECE)

    me = lax.axis_index("zl")
    weight = scales * (1 - flags).astype(jnp.float32)
    weight = in_parts(weight)
    bins = phase_bin.reshape(KEPT, LANES)
    base = bins[::2, 0] // 8 * 8
    marks = (bins - jnp.repeat(base, 2)[:, None]) % NBIN

    def weights_for(place):
        return lax.dynamic_slice_in_dim(weight, place * GROUP, GROUP, 0)

    base_rows = jnp.pad(base[None, :] // 8, ((0, LETTER_ROWS - BASE_ROW - 1), (0, LANES - BLOCKS)))
    below = jnp.concatenate([marks, base_rows]).astype(jnp.bfloat16)
    letters = [
        turned_to(lambda place: jnp.concatenate([weights_for(place), below]), "zl", turn) for turn in range(RUNS)
    ]
    chirp = chirp_table(lax.dynamic_slice_in_dim(sweep, me * GROUP, GROUP, 0))

    partial = fold_frames(buf, from_before, me.reshape(1), letters, chirp)
    shares = lax.all_to_all(partial, ("zl", "xy"), split_axis=0, concat_axis=0, tiled=True)
    size = lax.axis_size("xy")
    return pl.pallas_call(
        functools.partial(last_kernel, NBIN / (SLAB * RUNS * size)),
        out_shape=jax.ShapeDtypeStruct((16 * 4, RUNS * GROUP), jnp.float32),
        compiler_params=small_kernel(),
        name="last_sum",
    )(shares.reshape(RUNS, size, 8, LANES)).reshape(16, 4, RUNS * GROUP)


def solution(mesh):
    inner = Mesh(mesh.devices.reshape(-1, RUNS, MEMBERS), ("xy", "zl", "chan"))
    time = ("xy", "zl")
    placed = (
        P(None, None, None, ("xy", "zl", "chan")),
        P("chan", time),
        P("chan", time),
        P("chan"),
        P(time),
    )
    return jax.shard_map(
        on_device, mesh=inner, in_specs=placed, out_specs=P(time, None, "chan"), check_vma=False
    )
```

```python
import functools
import math

import jax
import jax.numpy as jnp
import numpy as np
from jax import lax
from jax.experimental import pallas as pl
from jax.experimental.pallas import tpu as pltpu
from jax.sharding import Mesh, PartitionSpec as P

NFFT = 4096
OVER = 1024
BLK = 256
NBIN = 1024
LANES = 128
ROWS = NFFT // LANES
RIM = OVER // LANES
KEPT = ROWS - RIM
RUNS = 4
MEMBERS = 8
PIECE = 384
SLAB = MEMBERS * PIECE
GROUP = 16
BLOCKS = SLAB // BLK
NARROW = 80
WINDOW = 144
ACC_ROWS = NBIN + WINDOW
DOT_ROWS = 256
BASE_ROW = GROUP + KEPT
LETTER_ROWS = BASE_ROW + 8
HALF_ROOT = math.sqrt(0.5)


def lane_tables():
    angle = 2.0 * np.pi / LANES * (np.arange(LANES)[:, None] * np.arange(LANES)[None, :] % LANES)
    cos, sin = np.cos(angle), np.sin(angle)
    table = np.block([[cos, -sin], [sin, cos]]).astype(np.float32)
    high = table.astype(jnp.bfloat16)
    low = (table - high.astype(np.float32)).astype(jnp.bfloat16)
    return high, low


def twist_tables():
    angle = -2.0 * np.pi / NFFT * (np.arange(ROWS)[:, None] * np.arange(LANES)[None, :])
    return np.cos(angle).astype(np.float32), np.sin(angle).astype(np.float32)


def plus(a, b):
    return (a[0] + b[0], a[1] + b[1])


def minus(a, b):
    return (a[0] - b[0], a[1] - b[1])


def quarter(a, sign):
    return (a[1], -a[0]) if sign < 0 else (-a[1], a[0])


def dft4(x, sign):
    t0, t1 = plus(x[0], x[2]), minus(x[0], x[2])
    t2, t3 = plus(x[1], x[3]), quarter(minus(x[1], x[3]), sign)
    return [plus(t0, t2), plus(t1, t3), minus(t0, t2), minus(t1, t3)]


def dft8(x, sign):
    even = dft4(x[0::2], sign)
    odd = dft4(x[1::2], sign)
    re, im = odd[1]
    if sign < 0:
        odd[1] = ((re + im) * HALF_ROOT, (im - re) * HALF_ROOT)
    else:
        odd[1] = ((re - im) * HALF_ROOT, (im + re) * HALF_ROOT)
    odd[2] = quarter(odd[2], sign)
    re, im = odd[3]
    if sign < 0:
        odd[3] = ((im - re) * HALF_ROOT, (re + im) * -HALF_ROOT)
    else:
        odd[3] = ((re + im) * -HALF_ROOT, (re - im) * HALF_ROOT)
    return [plus(e, o) for e, o in zip(even, odd)] + [minus(e, o) for e, o in zip(even, odd)]


def turned(a, step, sign):
    step %= 32
    if step == 0:
        return a
    if step == 8:
        return quarter(a, sign)
    re, im = a
    if step == 4:
        if sign < 0:
            return ((re + im) * HALF_ROOT, (im - re) * HALF_ROOT)
        return ((re - im) * HALF_ROOT, (im + re) * HALF_ROOT)
    cos = math.cos(2.0 * math.pi * step / 32)
    sin = sign * math.sin(2.0 * math.pi * step / 32)
    return (re * cos - im * sin, re * sin + im * cos)


def split(values):
    high = values.astype(jnp.bfloat16)
    return high, (values - high.astype(jnp.float32)).astype(jnp.bfloat16)


def lane_dft(high, low, table_high, table_low):
    dot = functools.partial(jnp.dot, preferred_element_type=jnp.float32)
    return dot(high, table_high) + (dot(low, table_high) + dot(high, table_low))


def frame_profile(
    row_of, weight_of, base_of, marks_of, chirp_ref, twist_ref, table_ref, mid, y_refs, s_refs, stokes_ref, acc
):
    def rows_in(pol, b):
        rows = []
        for a in range(8):
            row = 4 * a + b
            gain = weight_of(row // 2)
            rows.append(tuple(row_of(row, pol, part).astype(jnp.float32) * gain for part in range(2)))
        for ka, value in enumerate(dft8(rows, -1)):
            value = turned(value, b * ka, -1)
            mid[pol, 0, b, ka] = value[0]
            mid[pol, 1, b, ka] = value[1]

    def rows_across(pol, ka):
        values = dft4([(mid[pol, 0, b, ka], mid[pol, 1, b, ka]) for b in range(4)], -1)
        for kb in range(4):
            k = ka + 8 * kb
            re, im = values[kb]
            if k:
                cos, sin = twist_ref[0, k : k + 1], twist_ref[1, k : k + 1]
                re, im = re * cos - im * sin, re * sin + im * cos
            for part, value in enumerate((re, im)):
                high, low = split(value)
                where = (pl.ds(GROUP * k, GROUP), pl.ds(LANES * part, LANES))
                y_refs[pol, 0, *where] = high
                y_refs[pol, 1, *where] = low

    def lanes(pol, m):
        rows = pl.ds(DOT_ROWS * m, DOT_ROWS)
        s_refs[pol, rows] = lane_dft(y_refs[pol, 0, rows], y_refs[pol, 1, rows], table_ref[0], table_ref[1])

    def filtered(pol, k):
        rows = pl.ds(GROUP * k, GROUP)
        re, im = s_refs[pol, rows, :LANES], s_refs[pol, rows, LANES:]
        cos, sin = chirp_ref[0, rows], chirp_ref[1, rows]
        for part, value in enumerate((re * sin + im * cos, re * cos - im * sin)):
            high, low = split(value)
            where = (rows, pl.ds(LANES * part, LANES))
            y_refs[pol, 0, *where] = high
            y_refs[pol, 1, *where] = low

    def untwisted(pol, k):
        rows = pl.ds(GROUP * k, GROUP)
        im, re = s_refs[pol, rows, :LANES], s_refs[pol, rows, LANES:]
        if k == 0:
            return re, im
        cos, sin = twist_ref[0, k : k + 1], twist_ref[1, k : k + 1]
        return re * cos + im * sin, im * cos - re * sin

    def rows_back(pol, b):
        values = dft8([untwisted(pol, 4 * a + b) for a in range(8)], 1)
        for na, value in enumerate(values):
            value = turned(value, b * na, 1)
            mid[pol, 0, b, na] = value[0]
            mid[pol, 1, b, na] = value[1]

    def rows_out(na):
        x, y = (
            dft4([(mid[pol, 0, b, na], mid[pol, 1, b, na]) for b in range(4)], 1) for pol in range(2)
        )
        for nb in range(1, 4):
            (xr, xi), (yr, yi) = x[nb], y[nb]
            power_x = xr * xr + xi * xi
            power_y = yr * yr + yi * yi
            cross_re = xr * yr + xi * yi
            cross_im = xi * yr - xr * yi
            row = na + 8 * (nb - 1)
            lanes = pl.ds(LANES * (row % 2), LANES)
            for s, value in enumerate((power_x + power_y, power_x - power_y, cross_re, cross_im)):
                stokes_ref[row // 2, pl.ds(GROUP * s, GROUP), lanes] = value.astype(jnp.bfloat16)

    def fold(window):
        bins = lax.broadcasted_iota(jnp.int32, (window, BLK), 0).astype(jnp.bfloat16)
        for m in range(BLOCKS):
            onehot = jnp.where(bins == marks_of(m).astype(jnp.bfloat16), jnp.bfloat16(1), jnp.bfloat16(0))
            part = lax.dot_general(
                onehot, stokes_ref[m], (((1,), (1,)), ((), ())), preferred_element_type=jnp.float32
            )
            place = pl.ds(pl.multiple_of(base_of(m), 8), window)
            acc[place] += part

    spans = ROWS * GROUP // DOT_ROWS
    for b in range(4):
        rows_in(0, b)
    for ka in range(8):
        rows_across(0, ka)
    for m in range(spans):
        lanes(0, m)
    for b in range(4):
        rows_in(1, b)
    for ka in range(8):
        rows_across(1, ka)
    for k in range(ROWS):
        filtered(0, k)
    for m in range(spans):
        lanes(1, m)
    for m in range(spans):
        lanes(0, m)
    for k in range(ROWS):
        filtered(1, k)
    for b in range(4):
        rows_back(0, b)
    for m in range(spans):
        lanes(1, m)
    for b in range(4):
        rows_back(1, b)
    for na in range(8):
        rows_out(na)
    narrow = base_of(BLOCKS) < NARROW
    pl.when(narrow)(functools.partial(fold, NARROW))
    pl.when(jnp.logical_not(narrow))(functools.partial(fold, WINDOW))


def own_row(buf_ref, slab, row, pol, part):
    return buf_ref[row // 3, slab, pol, part, :, pl.ds(LANES * (row % 3), LANES)]


def lay_gains(gains, weights_of):
    for block in range(ROWS // 2):
        gains[block] = jnp.broadcast_to(weights_of(block), (GROUP, LANES))


def marks_from(marks_ref, index, m):
    return jnp.concatenate([marks_ref[index, 2 * m : 2 * m + 1], marks_ref[index, 2 * m + 1 : 2 * m + 2]], axis=1)


def later_kernel(me_ref, *refs):
    letter_refs, refs = refs[:RUNS], refs[RUNS:]
    buf_ref, chirp_ref, twist_ref, table_ref, acc_ref, sorted_ref, gains, marks, *scratches = refs
    me = me_ref[0]
    for turn in range(RUNS):
        sorted_ref[(me - turn + RUNS) % RUNS] = letter_refs[turn][...]
    marks[...] = sorted_ref[:, GROUP : GROUP + KEPT].astype(jnp.int32)
    acc_ref[...] = jnp.zeros_like(acc_ref)

    def step(frame, carry):
        def row_of(row, pol, part):
            if row < RIM:
                return own_row(buf_ref, frame - 1, row + KEPT - RIM, pol, part)
            return own_row(buf_ref, frame, row - RIM, pol, part)

        before, own = sorted_ref[frame - 1, :GROUP], sorted_ref[frame, :GROUP]

        def weights_of(block):
            if block < RIM // 2:
                return before[:, block + BLOCKS - RIM // 2 : block + BLOCKS - RIM // 2 + 1]
            return own[:, block - RIM // 2 : block - RIM // 2 + 1]

        lay_gains(gains, weights_of)
        bases = sorted_ref[frame, BASE_ROW : BASE_ROW + 1].astype(jnp.int32)
        frame_profile(
            row_of,
            lambda block: gains[block],
            lambda m: bases[0, m],
            lambda m: marks_from(marks, frame, m),
            chirp_ref,
            twist_ref,
            table_ref,
            *scratches,
            acc_ref,
        )
        return carry

    lax.fori_loop(1, RUNS, step, 0)


def first_kernel(
    buf_ref, tail_ref, sorted_ref, chirp_ref, twist_ref, table_ref, given_ref, out_ref, acc, gains, marks, *scratches
):
    acc[...] = given_ref[...]
    high, middle, low = (tail_ref[0, 0, part // 2, part % 2, :, :LANES].astype(jnp.float32) for part in range(3))
    before = (high + middle) + low
    own = sorted_ref[0, :GROUP]
    marks[0] = sorted_ref[0, GROUP : GROUP + KEPT].astype(jnp.int32)

    def weights_of(block):
        if block < RIM // 2:
            return before[:, block + BLOCKS - RIM // 2 : block + BLOCKS - RIM // 2 + 1]
        return own[:, block - RIM // 2 : block - RIM // 2 + 1]

    def row_of(row, pol, part):
        if row < RIM:
            return own_row(tail_ref, 0, row + 1, pol, part)
        return own_row(buf_ref, 0, row - RIM, pol, part)

    lay_gains(gains, weights_of)
    bases = sorted_ref[0, BASE_ROW : BASE_ROW + 1].astype(jnp.int32)
    frame_profile(
        row_of,
        lambda block: gains[block],
        lambda m: bases[0, m],
        lambda m: marks_from(marks, 0, m),
        chirp_ref,
        twist_ref,
        table_ref,
        *scratches,
        acc,
    )
    acc[:WINDOW] += acc[NBIN:]
    for share in range(NBIN // 16):
        place = share % RUNS * (NBIN // 16 // RUNS) + share // RUNS
        out_ref[place] = jnp.concatenate([acc[16 * share : 16 * share + 8], acc[16 * share + 8 : 16 * share + 16]], axis=1)


def tail_kernel(me_ref, *refs):
    letter_refs, piece_refs, out_ref, sorted_ref = refs[:RUNS], refs[RUNS:-2], refs[-2], refs[-1]
    me = me_ref[0]
    for turn in range(RUNS):
        sorted_ref[(me - turn + RUNS) % RUNS] = letter_refs[turn][:GROUP]
    rest = sorted_ref[RUNS - 1]
    for index, piece in enumerate(piece_refs):
        out_ref[index] = piece[0]
    for part in range(3):
        rounded = rest.astype(jnp.bfloat16)
        out_ref[0, 0, part // 2, part % 2, :, :LANES] = rounded
        rest = rest - rounded.astype(jnp.float32)


def spread_kernel(samples_ref, out_ref, held, in_sems, out_sems):
    places = [(pol, part) for pol in range(2) for part in range(2)]
    arriving = [pltpu.make_async_copy(samples_ref.at[at], held.at[at], in_sems.at[at]) for at in places]
    leaving = [pltpu.make_async_copy(held.at[at], out_ref.at[:, at[0], at[1]], out_sems.at[at]) for at in places]
    for copy in arriving:
        copy.start()
    for came, copy in zip(arriving, leaving):
        came.wait()
        copy.start()
    for copy in leaving:
        copy.wait()


def scratch():
    return [
        pltpu.VMEM((2, 2, 4, 8, GROUP, LANES), jnp.float32),
        pltpu.VMEM((2, 2, ROWS * GROUP, 2 * LANES), jnp.bfloat16),
        pltpu.VMEM((2, ROWS * GROUP, 2 * LANES), jnp.float32),
        pltpu.VMEM((BLOCKS, 4 * GROUP, BLK), jnp.bfloat16),
    ]


def whole():
    return pl.BlockSpec(memory_space=pltpu.VMEM)


def small_kernel():
    return pltpu.CompilerParams(vmem_limit_bytes=4 * 1024 * 1024)


def smem():
    return pl.BlockSpec(memory_space=pltpu.SMEM)


def tail_message(me, letters, buf):
    block = (1, 1) + buf.shape[2:]
    first = MEMBERS - 3
    return pl.pallas_call(
        tail_kernel,
        out_shape=jax.ShapeDtypeStruct((3, 1) + buf.shape[2:], buf.dtype),
        grid=(1,),
        in_specs=[smem()]
        + [whole()] * RUNS
        + [pl.BlockSpec(block, lambda i, at=first + at: (at, RUNS - 1, 0, 0, 0, 0)) for at in range(3)],
        out_specs=whole(),
        scratch_shapes=[pltpu.VMEM((RUNS, GROUP, LANES), jnp.float32)],
        compiler_params=small_kernel(),
        name="tail_message",
    )(me, *letters, buf, buf, buf)


def fold_frames(buf, tail_of, me, letters, chirp):
    twist = jnp.asarray(np.stack(twist_tables()))
    table = jnp.asarray(np.stack(lane_tables()))
    tail = tail_of(tail_message(me, letters, buf))
    params = pltpu.CompilerParams(vmem_limit_bytes=28 * 1024 * 1024)
    flops = 2 * 2 * 2 * 3 * ROWS * GROUP * 256 * 256
    later, ordered = pl.pallas_call(
        later_kernel,
        out_shape=[
            jax.ShapeDtypeStruct((ACC_ROWS, 4 * GROUP), jnp.float32),
            jax.ShapeDtypeStruct((RUNS, LETTER_ROWS, LANES), jnp.float32),
        ],
        in_specs=[smem()] + [whole()] * (RUNS + 4),
        out_specs=[whole()] * 2,
        scratch_shapes=[
            pltpu.VMEM((ROWS // 2, GROUP, LANES), jnp.float32),
            pltpu.VMEM((RUNS, KEPT, LANES), jnp.int32),
        ]
        + scratch(),
        compiler_params=params,
        cost_estimate=pl.CostEstimate(flops=3 * flops, bytes_accessed=30_000_000, transcendentals=0),
        name="later_frames",
    )(me, *letters, buf, chirp, twist, table)
    block = (MEMBERS, 1) + buf.shape[2:]
    return pl.pallas_call(
        first_kernel,
        out_shape=jax.ShapeDtypeStruct((NBIN // 16, 8, LANES), jnp.float32),
        grid=(1,),
        in_specs=[pl.BlockSpec(block, lambda i: (0,) * 6)] + [whole()] * 6,
        out_specs=whole(),
        scratch_shapes=[
            pltpu.VMEM((ACC_ROWS, 4 * GROUP), jnp.float32),
            pltpu.VMEM((ROWS // 2, GROUP, LANES), jnp.float32),
            pltpu.VMEM((1, KEPT, LANES), jnp.int32),
        ]
        + scratch(),
        compiler_params=params,
        cost_estimate=pl.CostEstimate(flops=flops, bytes_accessed=10_000_000, transcendentals=0),
        name="first_frame",
    )(buf, tail, ordered, chirp, twist, table, later)


def last_kernel(scale, shares_ref, out_ref):
    total = [jnp.sum(shares_ref[slab], axis=0) * scale for slab in range(RUNS)]
    for half in range(2):
        for s in range(4):
            lanes = slice(64 * half + GROUP * s, 64 * half + GROUP * (s + 1))
            row = jnp.concatenate([part[:, lanes] for part in total], axis=1)
            out_ref[pl.ds(32 * half + s, 8, stride=4)] = row if s < 2 else 2.0 * row


def turned_to(block_for, axis, turn):
    size = lax.axis_size(axis)
    there = (lax.axis_index(axis) + turn) % size
    if turn == 0:
        return block_for(there)
    return lax.ppermute(block_for(there), axis, [(i, (i + turn) % size) for i in range(size)])


def from_before(block):
    size = lax.axis_size("xy")
    return lax.ppermute(block, "xy", [(i, i + 1) for i in range(size - 1)])


def chirp_table(sweep):
    k = jnp.arange(ROWS, dtype=jnp.int32)[:, None] + ROWS * jnp.arange(LANES, dtype=jnp.int32)[None, :]
    u = jnp.where(k < NFFT // 2, k, k - NFFT).astype(jnp.float32) / NFFT
    phase = (jnp.pi * sweep)[None, :, None] * (u * u + u)[:, None, :]
    table = jnp.stack([jnp.cos(phase), jnp.sin(phase)]) * (1.0 / NFFT)
    return table.reshape(2, ROWS * GROUP, LANES)


def on_device(samples, scales, flags, sweep, phase_bin):
    parts = pl.pallas_call(
        spread_kernel,
        out_shape=jax.ShapeDtypeStruct((MEMBERS * RUNS, 2, 2, GROUP, PIECE), samples.dtype),
        in_specs=[pl.BlockSpec(memory_space=pltpu.HBM)],
        out_specs=pl.BlockSpec(memory_space=pltpu.HBM),
        scratch_shapes=[
            pltpu.VMEM((2, 2, MEMBERS * RUNS, GROUP, PIECE), samples.dtype),
            pltpu.SemaphoreType.DMA((2, 2)),
            pltpu.SemaphoreType.DMA((2, 2)),
        ],
        compiler_params=pltpu.CompilerParams(vmem_limit_bytes=60 * 1024 * 1024),
        name="spread",
    )(samples.reshape(2, 2, MEMBERS * RUNS, GROUP, PIECE))
    buf = lax.all_to_all(parts, ("chan", "zl"), split_axis=0, concat_axis=0, tiled=True)
    buf = buf.reshape(MEMBERS, RUNS, 2, 2, GROUP, PIECE)

    me = lax.axis_index("zl")
    weight = scales * (1 - flags).astype(jnp.float32)
    weight = jnp.pad(weight, ((0, 0), (0, LANES - BLOCKS)))
    bins = phase_bin.reshape(KEPT, LANES)
    base = bins[::2, 0] // 8 * 8
    marks = (bins - jnp.repeat(base, 2)[:, None]) % NBIN

    def weights_for(place):
        return lax.dynamic_slice_in_dim(weight, place * GROUP, GROUP, 0)

    places = jnp.concatenate([base, jnp.max(marks)[None]])
    base_rows = jnp.pad(places[None, :], ((0, LETTER_ROWS - BASE_ROW - 1), (0, LANES - BLOCKS - 1)))
    below = jnp.concatenate([marks, base_rows]).astype(jnp.float32)
    letters = [
        turned_to(lambda place: jnp.concatenate([weights_for(place), below]), "zl", turn) for turn in range(RUNS)
    ]
    chirp = chirp_table(lax.dynamic_slice_in_dim(sweep, me * GROUP, GROUP, 0))

    partial = fold_frames(buf, from_before, me.reshape(1), letters, chirp)
    shares = lax.all_to_all(partial, ("zl", "xy"), split_axis=0, concat_axis=0, tiled=True)
    size = lax.axis_size("xy")
    return pl.pallas_call(
        functools.partial(last_kernel, NBIN / (SLAB * RUNS * size)),
        out_shape=jax.ShapeDtypeStruct((16 * 4, RUNS * GROUP), jnp.float32),
        compiler_params=small_kernel(),
        name="last_sum",
    )(shares.reshape(RUNS, size, 8, LANES)).reshape(16, 4, RUNS * GROUP)


def solution(mesh):
    inner = Mesh(mesh.devices.reshape(-1, RUNS, MEMBERS), ("xy", "zl", "chan"))
    time = ("xy", "zl")
    placed = (
        P(None, None, None, ("xy", "zl", "chan")),
        P("chan", time),
        P("chan", time),
        P("chan"),
        P(time),
    )
    return jax.shard_map(
        on_device, mesh=inner, in_specs=placed, out_specs=P(time, None, "chan"), check_vma=False
    )
```

```python
import functools
import math

import jax
import jax.numpy as jnp
import numpy as np
from jax import lax
from jax.experimental import pallas as pl
from jax.experimental.pallas import tpu as pltpu
from jax.sharding import Mesh, PartitionSpec as P

NFFT = 4096
OVER = 1024
BLK = 256
NBIN = 1024
LANES = 128
ROWS = NFFT // LANES
RIM = OVER // LANES
KEPT = ROWS - RIM
RUNS = 4
MEMBERS = 8
PIECE = 384
SLAB = MEMBERS * PIECE
GROUP = 16
BLOCKS = SLAB // BLK
NARROW = 80
WINDOW = 144
ACC_ROWS = NBIN + WINDOW
DOT_ROWS = 256
BASE_ROW = GROUP + KEPT
LETTER_ROWS = BASE_ROW + 8
PARTS_APART = 16
HALF_ROOT = math.sqrt(0.5)


def lane_tables():
    angle = 2.0 * np.pi / LANES * (np.arange(LANES)[:, None] * np.arange(LANES)[None, :] % LANES)
    cos, sin = np.cos(angle), np.sin(angle)
    table = np.block([[cos, -sin], [sin, cos]]).astype(np.float32)
    high = table.astype(jnp.bfloat16)
    low = (table - high.astype(np.float32)).astype(jnp.bfloat16)
    return high, low


def twist_tables():
    angle = -2.0 * np.pi / NFFT * (np.arange(ROWS)[:, None] * np.arange(LANES)[None, :])
    return np.cos(angle).astype(np.float32), np.sin(angle).astype(np.float32)


def plus(a, b):
    return (a[0] + b[0], a[1] + b[1])


def minus(a, b):
    return (a[0] - b[0], a[1] - b[1])


def quarter(a, sign):
    return (a[1], -a[0]) if sign < 0 else (-a[1], a[0])


def dft4(x, sign):
    t0, t1 = plus(x[0], x[2]), minus(x[0], x[2])
    t2, t3 = plus(x[1], x[3]), quarter(minus(x[1], x[3]), sign)
    return [plus(t0, t2), plus(t1, t3), minus(t0, t2), minus(t1, t3)]


def dft8(x, sign):
    even = dft4(x[0::2], sign)
    odd = dft4(x[1::2], sign)
    re, im = odd[1]
    if sign < 0:
        odd[1] = ((re + im) * HALF_ROOT, (im - re) * HALF_ROOT)
    else:
        odd[1] = ((re - im) * HALF_ROOT, (im + re) * HALF_ROOT)
    odd[2] = quarter(odd[2], sign)
    re, im = odd[3]
    if sign < 0:
        odd[3] = ((im - re) * HALF_ROOT, (re + im) * -HALF_ROOT)
    else:
        odd[3] = ((re + im) * -HALF_ROOT, (re - im) * HALF_ROOT)
    return [plus(e, o) for e, o in zip(even, odd)] + [minus(e, o) for e, o in zip(even, odd)]


def turned(a, step, sign):
    step %= 32
    if step == 0:
        return a
    if step == 8:
        return quarter(a, sign)
    re, im = a
    if step == 4:
        if sign < 0:
            return ((re + im) * HALF_ROOT, (im - re) * HALF_ROOT)
        return ((re - im) * HALF_ROOT, (im + re) * HALF_ROOT)
    cos = math.cos(2.0 * math.pi * step / 32)
    sin = sign * math.sin(2.0 * math.pi * step / 32)
    return (re * cos - im * sin, re * sin + im * cos)


def split(values):
    high = values.astype(jnp.bfloat16)
    return high, (values - high.astype(jnp.float32)).astype(jnp.bfloat16)


def lane_dft(high, low, table_high, table_low):
    dot = functools.partial(jnp.dot, preferred_element_type=jnp.float32)
    return dot(high, table_high) + (dot(low, table_high) + dot(high, table_low))


def frame_profile(
    row_of, weight_of, base_of, marks_of, chirp_ref, twist_ref, table_ref, mid, y_refs, s_refs, stokes_ref, acc
):
    def rows_in(pol, b):
        rows = []
        for a in range(8):
            row = 4 * a + b
            gain = weight_of(row // 2)
            rows.append(tuple(row_of(row, pol, part).astype(jnp.float32) * gain for part in range(2)))
        for ka, value in enumerate(dft8(rows, -1)):
            value = turned(value, b * ka, -1)
            mid[pol, 0, b, ka] = value[0]
            mid[pol, 1, b, ka] = value[1]

    def rows_across(pol, ka):
        values = dft4([(mid[pol, 0, b, ka], mid[pol, 1, b, ka]) for b in range(4)], -1)
        for kb in range(4):
            k = ka + 8 * kb
            re, im = values[kb]
            if k:
                cos, sin = twist_ref[0, k : k + 1], twist_ref[1, k : k + 1]
                re, im = re * cos - im * sin, re * sin + im * cos
            for part, value in enumerate((re, im)):
                high, low = split(value)
                where = (pl.ds(GROUP * k, GROUP), pl.ds(LANES * part, LANES))
                y_refs[pol, 0, *where] = high
                y_refs[pol, 1, *where] = low

    def lanes(pol, m):
        rows = pl.ds(DOT_ROWS * m, DOT_ROWS)
        s_refs[pol, rows] = lane_dft(y_refs[pol, 0, rows], y_refs[pol, 1, rows], table_ref[0], table_ref[1])

    def filtered(pol, k):
        rows = pl.ds(GROUP * k, GROUP)
        re, im = s_refs[pol, rows, :LANES], s_refs[pol, rows, LANES:]
        cos, sin = chirp_ref[0, rows], chirp_ref[1, rows]
        for part, value in enumerate((re * sin + im * cos, re * cos - im * sin)):
            high, low = split(value)
            where = (rows, pl.ds(LANES * part, LANES))
            y_refs[pol, 0, *where] = high
            y_refs[pol, 1, *where] = low

    def untwisted(pol, k):
        rows = pl.ds(GROUP * k, GROUP)
        im, re = s_refs[pol, rows, :LANES], s_refs[pol, rows, LANES:]
        if k == 0:
            return re, im
        cos, sin = twist_ref[0, k : k + 1], twist_ref[1, k : k + 1]
        return re * cos + im * sin, im * cos - re * sin

    def rows_back(pol, b):
        values = dft8([untwisted(pol, 4 * a + b) for a in range(8)], 1)
        for na, value in enumerate(values):
            value = turned(value, b * na, 1)
            mid[pol, 0, b, na] = value[0]
            mid[pol, 1, b, na] = value[1]

    def rows_out(na):
        x, y = (
            dft4([(mid[pol, 0, b, na], mid[pol, 1, b, na]) for b in range(4)], 1) for pol in range(2)
        )
        for nb in range(1, 4):
            (xr, xi), (yr, yi) = x[nb], y[nb]
            power_x = xr * xr + xi * xi
            power_y = yr * yr + yi * yi
            cross_re = xr * yr + xi * yi
            cross_im = xi * yr - xr * yi
            row = na + 8 * (nb - 1)
            lanes = pl.ds(LANES * (row % 2), LANES)
            for s, value in enumerate((power_x + power_y, power_x - power_y, cross_re, cross_im)):
                stokes_ref[row // 2, pl.ds(GROUP * s, GROUP), lanes] = value.astype(jnp.bfloat16)

    def fold(window):
        bins = lax.broadcasted_iota(jnp.int32, (window, BLK), 0).astype(jnp.bfloat16)
        for m in range(BLOCKS):
            onehot = jnp.where(bins == marks_of(m).astype(jnp.bfloat16), jnp.bfloat16(1), jnp.bfloat16(0))
            part = lax.dot_general(
                onehot, stokes_ref[m], (((1,), (1,)), ((), ())), preferred_element_type=jnp.float32
            )
            place = pl.ds(pl.multiple_of(base_of(m), 8), window)
            acc[place] += part

    spans = ROWS * GROUP // DOT_ROWS
    for b in range(4):
        rows_in(0, b)
    for ka in range(8):
        rows_across(0, ka)
    for m in range(spans):
        lanes(0, m)
    for b in range(4):
        rows_in(1, b)
    for ka in range(8):
        rows_across(1, ka)
    for k in range(ROWS):
        filtered(0, k)
    for m in range(spans):
        lanes(1, m)
    for m in range(spans):
        lanes(0, m)
    for k in range(ROWS):
        filtered(1, k)
    for b in range(4):
        rows_back(0, b)
    for m in range(spans):
        lanes(1, m)
    for b in range(4):
        rows_back(1, b)
    for na in range(8):
        rows_out(na)
    narrow = base_of(BLOCKS) < NARROW
    pl.when(narrow)(functools.partial(fold, NARROW))
    pl.when(jnp.logical_not(narrow))(functools.partial(fold, WINDOW))


def own_row(buf_ref, slab, row, pol, part):
    return buf_ref[row // 3, slab, pol, part, :, pl.ds(LANES * (row % 3), LANES)]


def in_parts(weight):
    high = lax.reduce_precision(weight, 8, 7)
    middle = lax.reduce_precision(weight - high, 8, 7)
    parts = [high, middle, weight - high - middle]
    width = PARTS_APART - weight.shape[1]
    side_by_side = jnp.concatenate([jnp.pad(part, ((0, 0), (0, width))) for part in parts], axis=1)
    return jnp.pad(side_by_side, ((0, 0), (0, LANES - 3 * PARTS_APART))).astype(jnp.bfloat16)


def joined(rows):
    first, second, third = (rows[:, PARTS_APART * part : PARTS_APART * (part + 1)] for part in range(3))
    return (first + second) + third


def lay_gains(gains, weights_of):
    for block in range(ROWS // 2):
        gains[block] = jnp.broadcast_to(weights_of(block), (GROUP, LANES))


def marks_from(marks_ref, index, m):
    return jnp.concatenate([marks_ref[index, 2 * m : 2 * m + 1], marks_ref[index, 2 * m + 1 : 2 * m + 2]], axis=1)


def later_kernel(me_ref, *refs):
    letter_refs, refs = refs[:RUNS], refs[RUNS:]
    buf_ref, chirp_ref, twist_ref, table_ref, acc_ref, sorted_ref, gains, marks, *scratches = refs
    me = me_ref[0]
    for turn in range(RUNS):
        slab = (me - turn + RUNS) % RUNS
        sorted_ref[slab] = letter_refs[turn][...].astype(jnp.float32)
        sorted_ref[slab, :GROUP, :PARTS_APART] = joined(sorted_ref[slab, :GROUP])
    marks[...] = sorted_ref[:, GROUP : GROUP + KEPT].astype(jnp.int32)
    acc_ref[...] = jnp.zeros_like(acc_ref)

    def step(frame, carry):
        def row_of(row, pol, part):
            if row < RIM:
                return own_row(buf_ref, frame - 1, row + KEPT - RIM, pol, part)
            return own_row(buf_ref, frame, row - RIM, pol, part)

        before, own = sorted_ref[frame - 1, :GROUP], sorted_ref[frame, :GROUP]

        def weights_of(block):
            if block < RIM // 2:
                return before[:, block + BLOCKS - RIM // 2 : block + BLOCKS - RIM // 2 + 1]
            return own[:, block - RIM // 2 : block - RIM // 2 + 1]

        lay_gains(gains, weights_of)
        bases = 8 * sorted_ref[frame, BASE_ROW : BASE_ROW + 1].astype(jnp.int32)
        frame_profile(
            row_of,
            lambda block: gains[block],
            lambda m: bases[0, m],
            lambda m: marks_from(marks, frame, m),
            chirp_ref,
            twist_ref,
            table_ref,
            *scratches,
            acc_ref,
        )
        return carry

    lax.fori_loop(1, RUNS, step, 0)


def first_kernel(
    buf_ref, tail_ref, sorted_ref, chirp_ref, twist_ref, table_ref, given_ref, out_ref, acc, gains, marks, *scratches
):
    acc[...] = given_ref[...]
    before = joined(tail_ref[0, 0, 0, 0, :, :LANES].astype(jnp.float32))
    own = sorted_ref[0, :GROUP]
    marks[0] = sorted_ref[0, GROUP : GROUP + KEPT].astype(jnp.int32)

    def weights_of(block):
        if block < RIM // 2:
            return before[:, block + BLOCKS - RIM // 2 : block + BLOCKS - RIM // 2 + 1]
        return own[:, block - RIM // 2 : block - RIM // 2 + 1]

    def row_of(row, pol, part):
        if row < RIM:
            return own_row(tail_ref, 0, row + 1, pol, part)
        return own_row(buf_ref, 0, row - RIM, pol, part)

    lay_gains(gains, weights_of)
    bases = 8 * sorted_ref[0, BASE_ROW : BASE_ROW + 1].astype(jnp.int32)
    frame_profile(
        row_of,
        lambda block: gains[block],
        lambda m: bases[0, m],
        lambda m: marks_from(marks, 0, m),
        chirp_ref,
        twist_ref,
        table_ref,
        *scratches,
        acc,
    )
    acc[:WINDOW] += acc[NBIN:]
    for share in range(NBIN // 16):
        place = share % RUNS * (NBIN // 16 // RUNS) + share // RUNS
        out_ref[place] = jnp.concatenate([acc[16 * share : 16 * share + 8], acc[16 * share + 8 : 16 * share + 16]], axis=1)


def tail_kernel(me_ref, *refs):
    letter_refs, piece_refs, out_ref, sorted_ref = refs[:RUNS], refs[RUNS:-2], refs[-2], refs[-1]
    me = me_ref[0]
    for turn in range(RUNS):
        sorted_ref[(me - turn + RUNS) % RUNS] = letter_refs[turn][:GROUP]
    for index, piece in enumerate(piece_refs):
        out_ref[index] = piece[0]
    out_ref[0, 0, 0, 0, :, :LANES] = sorted_ref[RUNS - 1]


def spread_kernel(samples_ref, out_ref, held, in_sems, out_sems):
    places = [(pol, part) for pol in range(2) for part in range(2)]
    arriving = [pltpu.make_async_copy(samples_ref.at[at], held.at[at], in_sems.at[at]) for at in places]
    leaving = [pltpu.make_async_copy(held.at[at], out_ref.at[:, at[0], at[1]], out_sems.at[at]) for at in places]
    for copy in arriving:
        copy.start()
    for came, copy in zip(arriving, leaving):
        came.wait()
        copy.start()
    for copy in leaving:
        copy.wait()


def scratch():
    return [
        pltpu.VMEM((2, 2, 4, 8, GROUP, LANES), jnp.float32),
        pltpu.VMEM((2, 2, ROWS * GROUP, 2 * LANES), jnp.bfloat16),
        pltpu.VMEM((2, ROWS * GROUP, 2 * LANES), jnp.float32),
        pltpu.VMEM((BLOCKS, 4 * GROUP, BLK), jnp.bfloat16),
    ]


def whole():
    return pl.BlockSpec(memory_space=pltpu.VMEM)


def small_kernel():
    return pltpu.CompilerParams(vmem_limit_bytes=4 * 1024 * 1024)


def smem():
    return pl.BlockSpec(memory_space=pltpu.SMEM)


def tail_message(me, letters, buf):
    block = (1, 1) + buf.shape[2:]
    first = MEMBERS - 3
    return pl.pallas_call(
        tail_kernel,
        out_shape=jax.ShapeDtypeStruct((3, 1) + buf.shape[2:], buf.dtype),
        grid=(1,),
        in_specs=[smem()]
        + [whole()] * RUNS
        + [pl.BlockSpec(block, lambda i, at=first + at: (at, RUNS - 1, 0, 0, 0, 0)) for at in range(3)],
        out_specs=whole(),
        scratch_shapes=[pltpu.VMEM((RUNS, GROUP, LANES), jnp.bfloat16)],
        compiler_params=small_kernel(),
        name="tail_message",
    )(me, *letters, buf, buf, buf)


def fold_frames(buf, tail_of, me, letters, chirp):
    twist = jnp.asarray(np.stack(twist_tables()))
    table = jnp.asarray(np.stack(lane_tables()))
    tail = tail_of(tail_message(me, letters, buf))
    params = pltpu.CompilerParams(vmem_limit_bytes=28 * 1024 * 1024)
    flops = 2 * 2 * 2 * 3 * ROWS * GROUP * 256 * 256
    later, ordered = pl.pallas_call(
        later_kernel,
        out_shape=[
            jax.ShapeDtypeStruct((ACC_ROWS, 4 * GROUP), jnp.float32),
            jax.ShapeDtypeStruct((RUNS, LETTER_ROWS, LANES), jnp.float32),
        ],
        in_specs=[smem()] + [whole()] * (RUNS + 4),
        out_specs=[whole()] * 2,
        scratch_shapes=[
            pltpu.VMEM((ROWS // 2, GROUP, LANES), jnp.float32),
            pltpu.VMEM((RUNS, KEPT, LANES), jnp.int32),
        ]
        + scratch(),
        compiler_params=params,
        cost_estimate=pl.CostEstimate(flops=3 * flops, bytes_accessed=30_000_000, transcendentals=0),
        name="later_frames",
    )(me, *letters, buf, chirp, twist, table)
    block = (MEMBERS, 1) + buf.shape[2:]
    return pl.pallas_call(
        first_kernel,
        out_shape=jax.ShapeDtypeStruct((NBIN // 16, 8, LANES), jnp.float32),
        grid=(1,),
        in_specs=[pl.BlockSpec(block, lambda i: (0,) * 6)] + [whole()] * 6,
        out_specs=whole(),
        scratch_shapes=[
            pltpu.VMEM((ACC_ROWS, 4 * GROUP), jnp.float32),
            pltpu.VMEM((ROWS // 2, GROUP, LANES), jnp.float32),
            pltpu.VMEM((1, KEPT, LANES), jnp.int32),
        ]
        + scratch(),
        compiler_params=params,
        cost_estimate=pl.CostEstimate(flops=flops, bytes_accessed=10_000_000, transcendentals=0),
        name="first_frame",
    )(buf, tail, ordered, chirp, twist, table, later)


def last_kernel(scale, shares_ref, out_ref):
    total = [jnp.sum(shares_ref[slab], axis=0) * scale for slab in range(RUNS)]
    for half in range(2):
        for s in range(4):
            lanes = slice(64 * half + GROUP * s, 64 * half + GROUP * (s + 1))
            row = jnp.concatenate([part[:, lanes] for part in total], axis=1)
            out_ref[pl.ds(32 * half + s, 8, stride=4)] = row if s < 2 else 2.0 * row


def turned_to(block_for, axis, turn):
    size = lax.axis_size(axis)
    there = (lax.axis_index(axis) + turn) % size
    if turn == 0:
        return block_for(there)
    return lax.ppermute(block_for(there), axis, [(i, (i + turn) % size) for i in range(size)])


def from_before(block):
    size = lax.axis_size("xy")
    return lax.ppermute(block, "xy", [(i, i + 1) for i in range(size - 1)])


def chirp_table(sweep):
    k = jnp.arange(ROWS, dtype=jnp.int32)[:, None] + ROWS * jnp.arange(LANES, dtype=jnp.int32)[None, :]
    u = jnp.where(k < NFFT // 2, k, k - NFFT).astype(jnp.float32) / NFFT
    phase = (jnp.pi * sweep)[None, :, None] * (u * u + u)[:, None, :]
    table = jnp.stack([jnp.cos(phase), jnp.sin(phase)]) * (1.0 / NFFT)
    return table.reshape(2, ROWS * GROUP, LANES)


def on_device(samples, scales, flags, sweep, phase_bin):
    parts = pl.pallas_call(
        spread_kernel,
        out_shape=jax.ShapeDtypeStruct((MEMBERS * RUNS, 2, 2, GROUP, PIECE), samples.dtype),
        in_specs=[pl.BlockSpec(memory_space=pltpu.HBM)],
        out_specs=pl.BlockSpec(memory_space=pltpu.HBM),
        scratch_shapes=[
            pltpu.VMEM((2, 2, MEMBERS * RUNS, GROUP, PIECE), samples.dtype),
            pltpu.SemaphoreType.DMA((2, 2)),
            pltpu.SemaphoreType.DMA((2, 2)),
        ],
        compiler_params=pltpu.CompilerParams(vmem_limit_bytes=60 * 1024 * 1024),
        name="spread",
    )(samples.reshape(2, 2, MEMBERS * RUNS, GROUP, PIECE))
    buf = lax.all_to_all(parts, ("chan", "zl"), split_axis=0, concat_axis=0, tiled=True)
    buf = buf.reshape(MEMBERS, RUNS, 2, 2, GROUP, PIECE)

    me = lax.axis_index("zl")
    weight = scales * (1 - flags).astype(jnp.float32)
    weight = in_parts(weight)
    bins = phase_bin.reshape(KEPT, LANES)
    base = bins[::2, 0] // 8 * 8
    marks = (bins - jnp.repeat(base, 2)[:, None]) % NBIN

    def weights_for(place):
        return lax.dynamic_slice_in_dim(weight, place * GROUP, GROUP, 0)

    places = jnp.concatenate([base, jnp.max(marks)[None]])
    base_rows = jnp.pad(places[None, :] // 8, ((0, LETTER_ROWS - BASE_ROW - 1), (0, LANES - BLOCKS - 1)))
    below = jnp.concatenate([marks, base_rows]).astype(jnp.bfloat16)
    letters = [
        turned_to(lambda place: jnp.concatenate([weights_for(place), below]), "zl", turn) for turn in range(RUNS)
    ]
    chirp = chirp_table(lax.dynamic_slice_in_dim(sweep, me * GROUP, GROUP, 0))

    partial = fold_frames(buf, from_before, me.reshape(1), letters, chirp)
    shares = lax.all_to_all(partial, ("zl", "xy"), split_axis=0, concat_axis=0, tiled=True)
    size = lax.axis_size("xy")
    return pl.pallas_call(
        functools.partial(last_kernel, NBIN / (SLAB * RUNS * size)),
        out_shape=jax.ShapeDtypeStruct((16 * 4, RUNS * GROUP), jnp.float32),
        compiler_params=small_kernel(),
        name="last_sum",
    )(shares.reshape(RUNS, size, 8, LANES)).reshape(16, 4, RUNS * GROUP)


def solution(mesh):
    inner = Mesh(mesh.devices.reshape(-1, RUNS, MEMBERS), ("xy", "zl", "chan"))
    time = ("xy", "zl")
    placed = (
        P(None, None, None, ("xy", "zl", "chan")),
        P("chan", time),
        P("chan", time),
        P("chan"),
        P(time),
    )
    return jax.shard_map(
        on_device, mesh=inner, in_specs=placed, out_specs=P(time, None, "chan"), check_vma=False
    )
```
